32 devices in a mesh: section: 2 (over x), seq: 4 (over y, core), wt: 4 (over z).
Axes of the slice: x: 2, y: 2, z: 4, core: 2. Of those that a mesh axis runs over, the one named last changes fastest.
Arguments:
- inputs: bfloat16 [8, 1280, 1024], P('wt', 'seq'), may hold values from -6 to 6
- lengths: int32 [8, 8], P('wt'), may hold values from 1 to 1273, as said below
- cotangent: bfloat16 [8, 1280, 1024], P('wt', 'seq'), may hold values from -6 to 6
- gain_attn: bfloat16 [2, 1024], P('section', ('seq', 'wt')), may hold values from 0.5 to 1.5
- w_query: bfloat16 [2, 1024, 1024], P('section', ('seq', 'wt')), may hold values from -0.1875 to 0.1875
- w_key: bfloat16 [2, 1024, 1024], P('section', ('seq', 'wt')), may hold values from -0.1875 to 0.1875
- w_value: bfloat16 [2, 1024, 1024], P('section', ('seq', 'wt')), may hold values from -0.1875 to 0.1875
- w_out: bfloat16 [2, 1024, 1024], P('section', ('seq', 'wt')), may hold values from -0.75 to 0.75
- gain_mlp: bfloat16 [2, 1024], P('section', ('seq', 'wt')), may hold values from 0.5 to 1.5
- w_gate: bfloat16 [2, 1024, 2816], P('section', ('seq', 'wt')), may hold values from -0.1875 to 0.1875
- w_up: bfloat16 [2, 1024, 2816], P('section', ('seq', 'wt')), may hold values from -0.1875 to 0.1875
- w_down: bfloat16 [2, 2816, 1024], P('section', ('seq', 'wt')), may hold values from -0.15625 to 0.15625
Outputs:
- activations: bfloat16 [2, 8, 1280, 1024], P('section', 'wt', 'seq')
- input_grads: bfloat16 [2, 8, 1280, 1024], P('section', 'wt', 'seq')
- grad_gain_attn: float32 [2, 1024], P('section', ('seq', 'wt'))
- grad_query: float32 [2, 1024, 1024], P('section', ('seq', 'wt'))
- grad_key: float32 [2, 1024, 1024], P('section', ('seq', 'wt'))
- grad_value: float32 [2, 1024, 1024], P('section', ('seq', 'wt'))
- grad_out: float32 [2, 1024, 1024], P('section', ('seq', 'wt'))
- grad_gain_mlp: float32 [2, 1024], P('section', ('seq', 'wt'))
- grad_gate: float32 [2, 1024, 2816], P('section', ('seq', 'wt'))
- grad_up: float32 [2, 1024, 2816], P('section', ('seq', 'wt'))
- grad_down: float32 [2, 2816, 1024], P('section', ('seq', 'wt'))
The draws below stay inside these ranges and needn't reach their ends.
Inputs may be any that keep to these rules, and one draw needn't show every extreme that they name: `lengths`: each row lists the token counts of 8 documents that fill one sequence of 1280 tokens exactly, each 1 or more. In each aligned group of 2 rows, one row drawn from the seed is a document of 1273 tokens followed by 8 - 1 documents of one token.
All inputs are finite; a program needn't handle non-finite values.
Results may differ from the reference program's by a relative error of at most 0.025.
Values may be sent and summed in bfloat16 or wider, within the bound.
No kernel may reach another device: no remote copies, remote signals or barrier semaphores. Data moves between devices by JAX's collectives and lax.ppermute only.
A program may use at most 320 MiB of HBM per device.

```python
import jax
import jax.numpy as jnp
from jax import lax

D = 1024
HEADS = 16
HEAD_DIM = 64
FF = 2816
RADIUS = 127
TOK_DEV = 320
MICRO = 2
DOCS = 8
LEN = 1280
SEQS = 8


def draw_lengths(key, part):
    key = jax.random.fold_in(key, 11)
    row_keys = jax.random.split(key, SEQS)

    def one_row(row_key):
        cuts = jnp.sort(jax.random.permutation(row_key, LEN - 1)[:DOCS - 1] + 1).astype(jnp.int32)
        bounds = jnp.concatenate([jnp.zeros((1,), jnp.int32), cuts, jnp.full((1,), LEN, jnp.int32)])
        return bounds[1:] - bounds[:-1]
    spans = jax.vmap(one_row)(row_keys)
    group_count = SEQS // MICRO
    chosen = jax.random.randint(jax.random.fold_in(key, 5), (group_count,), 0, MICRO)
    long_rows = jnp.arange(group_count, dtype=jnp.int32) * MICRO + chosen
    is_long = jnp.any(jnp.arange(SEQS, dtype=jnp.int32)[:, None] == long_rows[None, :], axis=-1)
    single = jnp.concatenate([jnp.full((1,), LEN - DOCS + 1, jnp.int32), jnp.ones((DOCS - 1,), jnp.int32)])
    return jnp.where(is_long[:, None], single[None, :], spans).astype(jnp.int32)


def block_levels(stream_key, extent, shards, smallest, largest):
    factor_of, own = 1.0, jax.random.fold_in(stream_key, 6)
    for position, parts in shards:
        steps = jnp.exp(jax.random.uniform(jax.random.fold_in(own, position), (parts,), jnp.float32, smallest / len(shards), largest / len(shards)))
        factor_of = factor_of * jnp.repeat(steps, extent[position] // parts).reshape([-1 if axis == position else 1 for axis in range(len(extent))])
    return factor_of


def gaussian(key, dims, width, most, shards=(), kind=jnp.bfloat16):
    loudness = block_levels(key, dims, shards, -0.22, 0.18) if shards else 1.0
    result = jax.random.normal(key, dims, jnp.float32) * width * loudness
    return jnp.minimum(jnp.maximum(result, -most), most).astype(kind)


def setup_inputs(seed: int = 0) -> dict:
    splits = jax.random.split(jax.random.key(seed), 13)
    inputs = gaussian(splits[0], (SEQS, LEN, D), 1.0, 6.0, ((0, 4), (1, 4)))
    lengths = draw_lengths(jax.random.fold_in(splits[12], 71), 0)
    cotangent = gaussian(splits[2], (SEQS, LEN, D), 1.0, 6.0, ((0, 4), (1, 4)))
    gain_attn = jnp.clip(1.0 + 0.1 * jax.random.normal(splits[3], (2, D), jnp.float32), 0.5, 1.5).astype(jnp.bfloat16)
    w_query = gaussian(splits[4], (2, D, D), D ** -0.5, 0.1875, ((0, 2), (1, 16)))
    w_key = gaussian(splits[5], (2, D, D), D ** -0.5, 0.1875, ((0, 2), (1, 16)))
    w_value = gaussian(splits[6], (2, D, D), D ** -0.5, 0.1875, ((0, 2), (1, 16)))
    w_out = gaussian(splits[7], (2, D, D), (D // 16) ** -0.5, 0.75, ((0, 2), (1, 16)))
    gain_mlp = jnp.clip(1.0 + 0.1 * jax.random.normal(splits[8], (2, D), jnp.float32), 0.5, 1.5).astype(jnp.bfloat16)
    w_gate = gaussian(splits[9], (2, D, FF), D ** -0.5, 0.1875, ((0, 2), (1, 16)))
    w_up = gaussian(splits[10], (2, D, FF), D ** -0.5, 0.1875, ((0, 2), (1, 16)))
    w_down = gaussian(splits[11], (2, FF, D), (FF // 2) ** -0.5, 0.15625, ((0, 2), (1, 16)))
    return {"inputs": inputs, "lengths": lengths, "cotangent": cotangent, "gain_attn": gain_attn, "w_query": w_query, "w_key": w_key, "w_value": w_value, "w_out": w_out, "gain_mlp": gain_mlp, "w_gate": w_gate, "w_up": w_up, "w_down": w_down}


EPSILON = 1e-06
TOP_PRECISION = lax.Precision.HIGHEST

@jax.custom_vjp
def low(v):
    return lax.optimization_barrier(v.astype(jnp.bfloat16)).astype(jnp.float32)

@jax.custom_vjp
def low_back(v):
    return v

def low_keep(v):
    return (low(v), None)

def low_pass(kept, grad):
    return (grad,)

def back_keep(v):
    return (v, None)

def back_low(kept, grad):
    return (low(grad),)
low.defvjp(low_keep, low_pass)
low_back.defvjp(back_keep, back_low)

def rms_scale(values, gain_vec):
    return values * lax.rsqrt(lax.optimization_barrier(jnp.mean(values * values, axis=-1, keepdims=True)) + EPSILON) * gain_vec

def matmul(left_side, right_side):
    return jnp.dot(left_side, right_side, preferred_element_type=jnp.float32, precision=TOP_PRECISION)

def segment_ids(lengths_row, positions):
    doc_ends = jnp.cumsum(lengths_row)
    return lax.optimization_barrier(jnp.sum((positions[:, None] >= doc_ends[None, :]).astype(jnp.int32), axis=-1)).astype(jnp.int32)

def attention(queries, keys, values, segments):
    seq_len = queries.shape[0]
    block_rows = 2 * TOK_DEV
    key_span = block_rows + 2 * RADIUS
    key_pad = jnp.pad(keys, ((RADIUS, RADIUS), (0, 0)))
    value_pad = jnp.pad(values, ((RADIUS, RADIUS), (0, 0)))
    seg_pad = jnp.pad(segments, (RADIUS, RADIUS), constant_values=-1)

    def one_block(block_index):
        block_start = (block_index * block_rows).astype(jnp.int32)
        query_rows = lax.dynamic_slice_in_dim(queries, block_start, block_rows, 0).reshape(block_rows, HEADS, HEAD_DIM)
        key_rows = lax.dynamic_slice_in_dim(key_pad, block_start, key_span, 0).reshape(key_span, HEADS, HEAD_DIM)
        value_rows = lax.dynamic_slice_in_dim(value_pad, block_start, key_span, 0).reshape(key_span, HEADS, HEAD_DIM)
        seg_query = lax.dynamic_slice_in_dim(segments, block_start, block_rows, 0)
        seg_key = lax.dynamic_slice_in_dim(seg_pad, block_start, key_span, 0)
        offset = jnp.arange(block_rows)[:, None] + RADIUS - jnp.arange(key_span)[None, :]
        allowed = (jnp.abs(offset) <= RADIUS) & (seg_query[:, None] == seg_key[None, :])
        scores = low_back(jnp.einsum('qhd,khd->hqk', query_rows, key_rows, precision=TOP_PRECISION) * HEAD_DIM ** (-0.5))
        masked = jnp.where(allowed[None], scores, -1e+30)
        exp_scores = jnp.exp(masked - lax.optimization_barrier(jnp.max(masked, axis=-1, keepdims=True)))
        probs_low = low(exp_scores / lax.optimization_barrier(jnp.sum(exp_scores, axis=-1, keepdims=True)))
        mixed_rows = jnp.einsum('hqk,khd->qhd', probs_low, value_rows, precision=TOP_PRECISION)
        return mixed_rows.reshape(block_rows, HEADS * HEAD_DIM)
    blocks = lax.map(jax.checkpoint(one_block), jnp.arange(seq_len // block_rows, dtype=jnp.int32))
    return blocks.reshape(seq_len, HEADS * HEAD_DIM)

def encoder_layer(source, segments, params):
    gain_one, query_w, key_w, value_w, out_w, gain_two, gate_w, up_w, down_w = params
    normed = low(rms_scale(source, gain_one))
    queries = low_back(low(matmul(normed, query_w)))
    keys = low_back(low(matmul(normed, key_w)))
    values = low_back(low(matmul(normed, value_w)))
    mixed = low_back(low(attention(queries, keys, values, segments)))
    residual = source + low_back(matmul(mixed, out_w))
    normed_two = low(rms_scale(residual, gain_two))
    gate_pre = low_back(matmul(normed_two, gate_w))
    up_pre = low_back(matmul(normed_two, up_w))
    gated_low = low(jax.nn.gelu(gate_pre, approximate=True) * up_pre)
    return residual + low_back(matmul(gated_low, down_w))

def reference(inputs, lengths, cotangent, gain_attn, w_query, w_key, w_value, w_out, gain_mlp, w_gate, w_up, w_down):
    stacked = tuple((member.astype(jnp.float32) for member in (gain_attn, w_query, w_key, w_value, w_out, gain_mlp, w_gate, w_up, w_down)))
    first_params = tuple((member[0] for member in stacked))
    second_params = tuple((member[1] for member in stacked))
    positions = jnp.arange(inputs.shape[1], dtype=jnp.int32)

    def per_sequence(totals, seq_index):
        source = inputs[seq_index].astype(jnp.float32)
        segments = segment_ids(lengths[seq_index], positions)

        def run_layer(values, *params):
            return encoder_layer(values, segments, params)
        out_one, back_one = jax.vjp(run_layer, source, *first_params)
        out_one_low = out_one.astype(jnp.bfloat16)
        out_two, back_two = jax.vjp(run_layer, out_one_low.astype(jnp.float32), *second_params)
        grads_two = back_two(cotangent[seq_index].astype(jnp.float32))
        middle_grad = grads_two[0].astype(jnp.bfloat16)
        grads_one = back_one(middle_grad.astype(jnp.float32))
        totals = tuple((running + jnp.stack([grad_first, grad_second]) for running, grad_first, grad_second in zip(totals, grads_one[1:], grads_two[1:])))
        return (totals, (out_one_low, out_two.astype(jnp.bfloat16), grads_one[0].astype(jnp.bfloat16), middle_grad))
    zero_grads = tuple((jnp.zeros(member.shape, jnp.float32) for member in stacked))
    totals, outputs = lax.scan(per_sequence, zero_grads, jnp.arange(inputs.shape[0], dtype=jnp.int32))
    activations = jnp.stack([outputs[0], outputs[1]])
    input_grads = jnp.stack([outputs[2], outputs[3]])
    return (activations, input_grads, totals[0], totals[1], totals[2], totals[3], totals[4], totals[5], totals[6], totals[7], totals[8])
```

```python
import functools

import jax
import jax.numpy as jnp
from jax import lax
from jax.experimental import pallas as pl
from jax.experimental.pallas import tpu as pltpu
from jax.sharding import PartitionSpec as P

HEAD_DIM = 64
RADIUS = 127


EPSILON = 1e-06


def with_halo(cells, sides, width):
    for axis, dim in sides:
        count = lax.axis_size(axis)
        ends = count - 1
        head = lax.slice_in_dim(cells, 0, width, axis=dim)
        tail = lax.slice_in_dim(cells, cells.shape[dim] - width, cells.shape[dim], axis=dim)
        cells = jnp.concatenate(
            [
                lax.ppermute(tail, axis, [(i, (i + 1) % count) for i in range(ends)]),
                cells,
                lax.ppermute(head, axis, [((i + 1) % count, i) for i in range(ends)]),
            ],
            axis=dim,
        )
    return cells


def shifted(shard, axis, by):
    length = lax.axis_size(axis)
    pairs = [(i, i + by) for i in range(length) if 0 <= i + by < length]
    return lax.ppermute(shard, axis, pairs)


def rms_scale(values, gain_vec):
    return (
        values * lax.rsqrt(jnp.mean(values * values, axis=-1, keepdims=True) + EPSILON) * gain_vec
    )


def gated_unit(gate_pre, up_pre):
    return jax.nn.gelu(gate_pre, approximate=True) * up_pre


def window_allowed(lengths_row, shard_no, rows_local, seq_len):
    key_span = rows_local + 2 * RADIUS
    doc_ends = jnp.cumsum(lengths_row)
    key_pos = shard_no * rows_local - RADIUS + jnp.arange(key_span, dtype=jnp.int32)
    key_seg = jnp.sum((key_pos[:, None] >= doc_ends[None, :]).astype(jnp.int32), axis=-1)
    inside = (key_pos >= 0) & (key_pos < seq_len)
    key_seg = jnp.where(inside, key_seg, -1)
    query_seg = key_seg[RADIUS : RADIUS + rows_local]
    offset = jnp.arange(rows_local)[:, None] + RADIUS - jnp.arange(key_span)[None, :]
    return (jnp.abs(offset) <= RADIUS) & (query_seg[:, None] == key_seg[None, :])


def layer_forward(layer_in, allowed, params):
    gain_one, query_w, key_w, value_w, out_w, gain_two, gate_w, up_w, down_w = params
    rows_local, model_width = layer_in.shape
    head_count = model_width // HEAD_DIM
    score_scale = HEAD_DIM ** (-0.5)
    source = layer_in.astype(jnp.float32)
    normed = rms_scale(source, gain_one.astype(jnp.float32)).astype(jnp.bfloat16)
    queries = jnp.dot(normed, query_w, preferred_element_type=jnp.float32).astype(jnp.bfloat16)
    keys_local = jnp.dot(normed, key_w, preferred_element_type=jnp.float32).astype(jnp.bfloat16)
    values_local = jnp.dot(normed, value_w, preferred_element_type=jnp.float32).astype(jnp.bfloat16)
    extended = with_halo(jnp.stack([keys_local, values_local]), (("seq", 1),), RADIUS)
    query_heads = queries.reshape(rows_local, head_count, HEAD_DIM)
    key_heads = extended[0].reshape(-1, head_count, HEAD_DIM)
    value_heads = extended[1].reshape(-1, head_count, HEAD_DIM)
    scores = (
        jnp.einsum("qhd,khd->hqk", query_heads, key_heads, preferred_element_type=jnp.float32)
        * score_scale
    )
    masked = jnp.where(allowed[None], scores, -1e30)
    exp_scores = jnp.exp(masked - jnp.max(masked, axis=-1, keepdims=True))
    attn_probs = exp_scores / jnp.sum(exp_scores, axis=-1, keepdims=True)
    probs_low = attn_probs.astype(jnp.bfloat16)
    mixed_heads = jnp.einsum(
        "hqk,khd->qhd", probs_low, value_heads, preferred_element_type=jnp.float32
    )
    mixed_low = mixed_heads.reshape(rows_local, model_width).astype(jnp.bfloat16)
    residual = source + jnp.dot(mixed_low, out_w, preferred_element_type=jnp.float32)
    normed_two = rms_scale(residual, gain_two.astype(jnp.float32)).astype(jnp.bfloat16)
    gate_pre = jnp.dot(normed_two, gate_w, preferred_element_type=jnp.float32)
    up_pre = jnp.dot(normed_two, up_w, preferred_element_type=jnp.float32)
    gated_low = gated_unit(gate_pre, up_pre).astype(jnp.bfloat16)
    result = residual + jnp.dot(gated_low, down_w, preferred_element_type=jnp.float32)
    kept_values = (
        source,
        normed,
        query_heads,
        key_heads,
        value_heads,
        attn_probs,
        probs_low,
        mixed_low,
        residual,
        normed_two,
        gate_pre,
        up_pre,
        gated_low,
    )
    return (result, kept_values)


def settle(extended, head_part, tail_part, row_count):
    center = extended[RADIUS : RADIUS + row_count]
    return (
        center
        + jnp.pad(head_part, ((0, row_count - RADIUS), (0, 0)))
        + jnp.pad(tail_part, ((row_count - RADIUS, 0), (0, 0)))
    )


def hops():
    rings, span = lax.axis_size("wt"), lax.axis_size("seq")
    high = span // 2
    along = [(i, (i + 1) % rings) for i in range(rings)]
    across = [(h * 2 + c, ((h + 1) % high) * 2 + c) for h in range(high) for c in range(2)]
    pairs = [(i, i ^ 1) for i in range(span)]
    return (
        lambda cells: lax.ppermute(cells, "wt", along),
        lambda cells: lax.ppermute(cells, "seq", across),
        lambda cells: lax.ppermute(cells, "seq", pairs),
    )


def places():
    rings, high = lax.axis_size("wt"), lax.axis_size("seq") // 2
    shard_no = lax.axis_index("seq")
    return rings, high, lax.axis_index("wt"), shard_no // 2, shard_no % 2


def gather_pieces(shard):
    along, across, swap = hops()
    rings, high = lax.axis_size("wt"), lax.axis_size("seq") // 2
    pieces = {}
    current = shard
    for k in range(rings):
        current = along(current) if k else current
        cells = current
        for j in range(high):
            cells = across(cells) if j else cells
            pieces[(k, j, 0)] = cells
    for k, j, _ in list(pieces):
        pieces[(k, j, 1)] = swap(pieces[(k, j, 0)])
    return pieces


def owner_of(k, j, p):
    rings, high, z, h, c = places()
    return (lax.rem(h - j + high, high) * 2 + (c + p) % 2) * rings + lax.rem(z - k + rings, rings)


def assemble_kernel(count, rows_list, owners_ref, *refs):
    parts, wholes, sems = refs[:count], refs[count:-1], refs[-1]
    copies = []
    for i in range(count):
        start = 0
        for w, rows in enumerate(rows_list):
            place = pl.multiple_of(owners_ref[i] * rows, rows)
            copies.append(
                pltpu.make_async_copy(
                    parts[i].at[pl.ds(start, rows)],
                    wholes[w].at[pl.ds(place, rows)],
                    sems.at[i * len(rows_list) + w],
                )
            )
            start += rows
    for copy in copies:
        copy.start()
    for copy in copies:
        copy.wait()


def assemble(pieces, rows_list):
    keys = sorted(pieces)
    count = len(keys)
    owners = [owner_of(*key) for key in keys]
    width, kind = pieces[keys[0]].shape[-1], pieces[keys[0]].dtype
    if any(rows % 16 for rows in rows_list):
        wholes, start = [], 0
        for rows in rows_list:
            whole = jnp.zeros((count * rows, width), kind)
            for key, place in zip(keys, owners):
                part = lax.slice_in_dim(pieces[key], start, start + rows, axis=0)
                whole = lax.dynamic_update_slice_in_dim(whole, part, place * rows, 0)
            wholes.append(whole)
            start += rows
        return wholes
    return pl.pallas_call(
        functools.partial(assemble_kernel, count, rows_list),
        out_shape=[jax.ShapeDtypeStruct((count * rows, width), kind) for rows in rows_list],
        grid_spec=pltpu.PrefetchScalarGridSpec(
            num_scalar_prefetch=1,
            grid=(),
            in_specs=[pl.BlockSpec(memory_space=pl.ANY)] * count,
            out_specs=[pl.BlockSpec(memory_space=pltpu.VMEM)] * len(rows_list),
            scratch_shapes=[pltpu.SemaphoreType.DMA((count * len(rows_list),))],
        ),
        compiler_params=pltpu.CompilerParams(vmem_limit_bytes=40 * 2**20),
    )(jnp.stack(owners).astype(jnp.int32), *[pieces[key] for key in keys])


def plus(left, right, kind):
    return (left.astype(jnp.float32) + right.astype(jnp.float32)).astype(kind)


def scatter_sum(partial, kind=jnp.bfloat16):
    along, across, swap = hops()
    rings, high, z, h, c = places()
    rows = partial.shape[0] // (rings * high * 2)
    cells = partial.reshape(high, 2, rings, rows, -1)
    mine = lax.dynamic_index_in_dim(cells, c, 1, False)
    received = swap(lax.dynamic_index_in_dim(cells, 1 - c, 1, False))

    def block(j, k):
        place = (lax.rem(h - j + high, high), lax.rem(z - k + rings, rings), 0, 0)
        size = (1, 1, rows, cells.shape[-1])
        return plus(
            lax.dynamic_slice(mine, place, size)[0, 0],
            lax.dynamic_slice(received, place, size)[0, 0],
            kind,
        )

    total = None
    for k in range(1, rings + 1):
        level = block(1, k)
        for j in range(2, high + 1):
            level = plus(across(level), block(j, k), kind)
        if total is not None:
            last = k == rings
            total = plus(along(total), level, jnp.float32 if last else kind)
        else:
            total = level
    return total.astype(jnp.float32)


def layer_backward(kept_values, params, grad_out):
    gain_one, query_w, key_w, value_w, out_w, gain_two, gate_w, up_w, down_w = params
    rows_local, model_width = grad_out.shape
    head_count = model_width // HEAD_DIM
    score_scale = HEAD_DIM ** (-0.5)
    (
        source,
        normed,
        query_heads,
        key_heads,
        value_heads,
        attn_probs,
        probs_low,
        mixed_low,
        residual,
        normed_two,
        gate_pre,
        up_pre,
        gated_low,
    ) = kept_values
    grad_gated = jnp.dot(grad_out, down_w.T, preferred_element_type=jnp.float32)
    unused_unit, unit_back = jax.vjp(gated_unit, gate_pre, up_pre)
    grad_gate_pre, grad_up_pre = unit_back(grad_gated)
    grad_gate_pre = grad_gate_pre.astype(jnp.bfloat16)
    grad_up_pre = grad_up_pre.astype(jnp.bfloat16)
    grad_normed_two = jnp.dot(
        grad_gate_pre, gate_w.T, preferred_element_type=jnp.float32
    ) + jnp.dot(grad_up_pre, up_w.T, preferred_element_type=jnp.float32)
    unused_two, norm_back_two = jax.vjp(rms_scale, residual, gain_two.astype(jnp.float32))
    grad_res_norm, grad_gain_two = norm_back_two(grad_normed_two)
    grad_residual = grad_out.astype(jnp.float32) + grad_res_norm
    grad_branch = grad_residual.astype(jnp.bfloat16)
    grad_mixed = jnp.dot(grad_branch, out_w.T, preferred_element_type=jnp.float32).astype(
        jnp.bfloat16
    )
    grad_mixed = grad_mixed.reshape(rows_local, head_count, HEAD_DIM)
    grad_probs = jnp.einsum(
        "qhd,khd->hqk", grad_mixed, value_heads, preferred_element_type=jnp.float32
    )
    grad_value_ext = jnp.einsum(
        "hqk,qhd->khd", probs_low, grad_mixed, preferred_element_type=jnp.float32
    ).reshape(-1, model_width)
    grad_scores = (
        attn_probs * (grad_probs - jnp.sum(attn_probs * grad_probs, axis=-1, keepdims=True))
    ).astype(jnp.bfloat16)
    grad_queries = (
        jnp.einsum("hqk,khd->qhd", grad_scores, key_heads, preferred_element_type=jnp.float32)
        * score_scale
    )
    grad_queries = grad_queries.reshape(rows_local, model_width).astype(jnp.bfloat16)
    grad_key_ext = (
        jnp.einsum("hqk,qhd->khd", grad_scores, query_heads, preferred_element_type=jnp.float32)
        * score_scale
    ).reshape(-1, model_width)
    from_above = shifted(jnp.stack([grad_key_ext[:RADIUS], grad_value_ext[:RADIUS]]), "seq", -1)
    from_below = shifted(
        jnp.stack([grad_key_ext[RADIUS + rows_local :], grad_value_ext[RADIUS + rows_local :]]),
        "seq",
        1,
    )
    grad_keys = settle(grad_key_ext, from_below[0], from_above[0], rows_local).astype(jnp.bfloat16)
    grad_values = settle(grad_value_ext, from_below[1], from_above[1], rows_local).astype(
        jnp.bfloat16
    )
    grad_normed = jnp.dot(grad_queries, query_w.T, preferred_element_type=jnp.float32)
    grad_normed = grad_normed + jnp.dot(grad_keys, key_w.T, preferred_element_type=jnp.float32)
    grad_normed = grad_normed + jnp.dot(grad_values, value_w.T, preferred_element_type=jnp.float32)
    unused_one, norm_back_one = jax.vjp(rms_scale, source, gain_one.astype(jnp.float32))
    grad_src_norm, grad_gain_one = norm_back_one(grad_normed)
    grad_in = grad_residual + grad_src_norm
    saved = (
        normed,
        grad_queries,
        grad_keys,
        grad_values,
        mixed_low,
        grad_branch,
        normed_two,
        grad_gate_pre,
        grad_up_pre,
        gated_low,
        grad_out,
    )
    return (grad_in, (grad_gain_one, grad_gain_two), saved)


def per_device(
    inputs,
    lengths,
    cotangent,
    gain_attn,
    w_query,
    w_key,
    w_value,
    w_out,
    gain_mlp,
    w_gate,
    w_up,
    w_down,
):
    section_no = lax.axis_index("section")
    shard_no = lax.axis_index("seq")
    micro_count, rows_local, model_width = inputs.shape
    seq_len = rows_local * lax.axis_size("seq")
    first_section = section_no == 0
    allowed_all = [
        window_allowed(lengths[number], shard_no, rows_local, seq_len)
        for number in range(micro_count)
    ]
    rows = w_query.shape[1]
    gains = jnp.pad(
        jnp.concatenate([gain_attn, gain_mlp], 1), ((0, 15), (0, model_width - 2 * rows))
    )
    narrow = gather_pieces(jnp.concatenate([w_query[0], w_key[0], w_value[0], w_out[0], gains], 0))
    wide = gather_pieces(jnp.concatenate([w_gate[0], w_up[0]], 0))
    deep = gather_pieces(w_down[0])
    query_w, key_w, value_w, out_w, gain_rows = assemble(narrow, [rows, rows, rows, rows, 16])
    gate_w, up_w = assemble(wide, [rows, rows])
    (down_w,) = assemble(deep, [w_down.shape[1]])
    gain_rows = gain_rows.reshape(-1, 16, model_width)[:, 0]
    gain_one = gain_rows[:, :rows].reshape(-1)
    gain_two = gain_rows[:, rows : 2 * rows].reshape(-1)
    params = (gain_one, query_w, key_w, value_w, out_w, gain_two, gate_w, up_w, down_w)

    arrived = jnp.zeros((rows_local, model_width), jnp.bfloat16)
    kept_all = []
    layer_outputs = []
    for moment in range(micro_count + 1):
        own_rows = inputs[min(moment, micro_count - 1)]
        layer_in = jnp.where(first_section, own_rows, arrived)
        allowed = jnp.where(
            first_section,
            allowed_all[min(moment, micro_count - 1)],
            allowed_all[max(moment - 1, 0)],
        )
        result, kept = layer_forward(layer_in, allowed, params)
        result_low = result.astype(jnp.bfloat16)
        kept_all.append(kept)
        layer_outputs.append(result_low)
        if moment < micro_count:
            arrived = shifted(result_low, "section", 1)
    activations = jnp.stack(
        [
            jnp.where(first_section, layer_outputs[number], layer_outputs[number + 1])
            for number in range(micro_count)
        ]
    )[None]
    arrived_grad = jnp.zeros((rows_local, model_width), jnp.bfloat16)
    grad_inputs = []
    saved_all = []
    gains_all = []
    for moment in range(micro_count + 1):
        late_index = max(moment - 1, 0)
        early_index = min(moment, micro_count - 1)
        grad_out = jnp.where(first_section, arrived_grad, cotangent[early_index])
        kept = tuple(
            jnp.where(first_section, late, early)
            for late, early in zip(kept_all[late_index], kept_all[min(moment + 1, micro_count)])
        )
        grad_in, gain_grads, saved = layer_backward(kept, params, grad_out)
        grad_low = grad_in.astype(jnp.bfloat16)
        grad_inputs.append(grad_low)
        if moment < micro_count:
            arrived_grad = shifted(grad_low, "section", -1)
        saved_all.append(saved)
        gains_all.append(gain_grads)

    def both(index):
        return jnp.concatenate(
            [
                jnp.where(first_section, saved_all[number + 1][index], saved_all[number][index])
                for number in range(micro_count)
            ],
            0,
        )

    (
        normed,
        grad_queries,
        grad_keys,
        grad_values,
        mixed_low,
        grad_branch,
        normed_two,
        grad_gate_pre,
        grad_up_pre,
        gated_low,
        grad_out,
    ) = [both(index) for index in range(11)]

    def product(left, right):
        return jnp.dot(left.T, right, preferred_element_type=jnp.float32).astype(jnp.bfloat16)

    grad_down_w = scatter_sum(product(gated_low, grad_out))
    grad_gate_w = scatter_sum(product(normed_two, grad_gate_pre))
    grad_up_w = scatter_sum(product(normed_two, grad_up_pre))
    grad_out_w = scatter_sum(product(mixed_low, grad_branch))
    grad_qkv_w = scatter_sum(
        product(normed, jnp.concatenate([grad_queries, grad_keys, grad_values], 1))
    )
    grad_query_w, grad_key_w, grad_value_w = jnp.split(grad_qkv_w, 3, axis=1)
    gain_parts = [
        sum(
            jnp.where(first_section, gains_all[number + 1][index], gains_all[number][index])
            for number in range(micro_count)
        )
        for index in range(2)
    ]
    gain_sum = scatter_sum(
        jnp.concatenate([part.reshape(-1, rows) for part in gain_parts], 1), jnp.float32
    )
    input_grads = jnp.stack(
        [
            jnp.where(first_section, grad_inputs[number + 1], grad_inputs[number])
            for number in range(micro_count)
        ]
    )[None]
    return (
        activations,
        input_grads,
        gain_sum[:, :rows],
        grad_query_w[None],
        grad_key_w[None],
        grad_value_w[None],
        grad_out_w[None],
        gain_sum[:, rows:],
        grad_gate_w[None],
        grad_up_w[None],
        grad_down_w[None],
    )


def solution(mesh):
    placed = (
        P("wt", "seq", None),
        P("wt", None),
        P("wt", "seq", None),
        P("section", ("seq", "wt")),
        P("section", ("seq", "wt"), None),
        P("section", ("seq", "wt"), None),
        P("section", ("seq", "wt"), None),
        P("section", ("seq", "wt"), None),
        P("section", ("seq", "wt")),
        P("section", ("seq", "wt"), None),
        P("section", ("seq", "wt"), None),
        P("section", ("seq", "wt"), None),
    )
    return jax.shard_map(
        per_device,
        mesh=mesh,
        in_specs=placed,
        out_specs=(
            P("section", "wt", "seq", None),
            P("section", "wt", "seq", None),
            P("section", ("seq", "wt")),
            P("section", ("seq", "wt"), None),
            P("section", ("seq", "wt"), None),
            P("section", ("seq", "wt"), None),
            P("section", ("seq", "wt"), None),
            P("section", ("seq", "wt")),
            P("section", ("seq", "wt"), None),
            P("section", ("seq", "wt"), None),
            P("section", ("seq", "wt"), None),
        ),
        check_vma=False,
    )
```

```python
import functools

import jax
import jax.numpy as jnp
from jax import lax
from jax.experimental import pallas as pl
from jax.experimental.pallas import tpu as pltpu
from jax.sharding import PartitionSpec as P

HEAD_DIM = 64
RADIUS = 127


EPSILON = 1e-06


def shifted(shard, axis, by):
    length = lax.axis_size(axis)
    pairs = [(i, i + by) for i in range(length) if 0 <= i + by < length]
    return lax.ppermute(shard, axis, pairs)


HALO = 128
BLOCK = 128
WIDE = 256
NEVER = -1e30


def call(kernel, grid, scalars, ins, in_specs, outs, out_specs, scratch=(), aliases=None, cost=None):
    return pl.pallas_call(
        kernel,
        out_shape=outs,
        grid_spec=pltpu.PrefetchScalarGridSpec(
            num_scalar_prefetch=1,
            grid=grid,
            in_specs=in_specs,
            out_specs=out_specs,
            scratch_shapes=list(scratch),
        ),
        input_output_aliases=aliases or {},
        compiler_params=pltpu.CompilerParams(
            vmem_limit_bytes=56 * 2**20, dimension_semantics=("arbitrary",) * len(grid)
        ),
        cost_estimate=cost,
    )(scalars, *ins)


def cost_of(flops, moved, transcendentals=0):
    return pl.CostEstimate(
        flops=int(flops), bytes_accessed=int(moved), transcendentals=int(transcendentals)
    )


def nt_dot(left, right):
    return lax.dot_general(
        left, right, (((1,), (1,)), ((), ())), preferred_element_type=jnp.float32
    )


def tn_dot(left, right):
    return lax.dot_general(
        left, right, (((0,), (0,)), ((), ())), preferred_element_type=jnp.float32
    )


def dot(left, right):
    return jnp.dot(left, right, preferred_element_type=jnp.float32)


def inverse_rms(values):
    return lax.rsqrt(jnp.mean(values * values, axis=-1, keepdims=True) + EPSILON)


def project_kernel(idx, own, arrived, gain, wq, wk, wv, *rest):
    x_out, n_out, q_out, kv_out, tail_out, head_out = rest[-6:]

    @pl.when(pl.program_id(0) == 0)
    def _():
        picked = jnp.where(
            idx[0] == 1, own[...].astype(jnp.float32), arrived[...].astype(jnp.float32)
        )
        x_out[...] = picked.astype(jnp.bfloat16)
        n_out[...] = (picked * inverse_rms(picked) * gain[...].astype(jnp.float32)).astype(
            jnp.bfloat16
        )

    normed = n_out[...]
    kv_out[0] = dot(normed, wk[...]).astype(jnp.bfloat16)
    kv_out[1] = dot(normed, wv[...]).astype(jnp.bfloat16)
    q_out[...] = dot(normed, wq[...]).astype(jnp.bfloat16)
    tail_out[...] = kv_out[:, pl.ds(kv_out.shape[1] - HALO, HALO)]
    head_out[...] = kv_out[:, pl.ds(0, HALO)]


def slot_call(kernel, grid, scalars, ins, in_specs, kept, fresh, store, slots, moment, scratch=(), cost=None):
    aliases, extra = {}, []
    outs, out_specs = [], []
    for name, shape, block, index, kind in kept:
        outs.append(jax.ShapeDtypeStruct((slots,) + shape, kind))
        if block is None:
            out_specs.append(pl.BlockSpec(memory_space=pl.ANY))
        else:
            out_specs.append(
                pl.BlockSpec((None,) + block, lambda j, s, index=index: (moment,) + index(j))
            )
        if name in store:
            aliases[1 + len(ins) + len(extra)] = len(outs) - 1
            extra.append(store[name])
    for shape, kind, spec in fresh:
        outs.append(jax.ShapeDtypeStruct(shape, kind))
        out_specs.append(spec)
    results = call(
        kernel,
        grid,
        scalars,
        list(ins) + extra,
        list(in_specs) + [pl.BlockSpec(memory_space=pl.ANY)] * len(extra),
        outs,
        out_specs,
        scratch,
        aliases,
        cost,
    )
    for (name, *_), value in zip(kept, results):
        store[name] = value
    return results[len(kept) :]


def whole_spec(shape):
    return pl.BlockSpec(shape, lambda j, s: (0,) * len(shape))


def project(store, slots, moment, scalars, own, arrived, params):
    rows, width = arrived.shape
    gain_one, query_w, key_w, value_w = params[:4]
    tile = WIDE
    columns = pl.BlockSpec((width, tile), lambda j, s: (0, j))
    at_start = lambda j: (0, 0)
    halo_spec = pl.BlockSpec((2, HALO, tile), lambda j, s: (0, 0, j))
    return slot_call(
        project_kernel,
        (width // tile,),
        scalars,
        [own, arrived, gain_one, query_w, key_w, value_w],
        [whole_spec((rows, width)), whole_spec((rows, width)), whole_spec((1, width))]
        + [columns] * 3,
        [
            ("source", (rows, width), (rows, width), at_start, jnp.bfloat16),
            ("normed", (rows, width), (rows, width), at_start, jnp.bfloat16),
            ("queries", (rows, width), (rows, tile), lambda j: (0, j), jnp.bfloat16),
        ],
        [
            (
                (2, rows, width),
                jnp.bfloat16,
                pl.BlockSpec((2, rows, tile), lambda j, s: (0, 0, j)),
            ),
            ((2, HALO, width), jnp.bfloat16, halo_spec),
            ((2, HALO, width), jnp.bfloat16, halo_spec),
        ],
        store,
        slots,
        moment,
        cost=cost_of(6 * rows * width * width, 6 * width * width + 14 * rows * width),
    )


def row_blocks(rows):
    return [(start, min(BLOCK, rows - start)) for start in range(0, rows, BLOCK)]


def head_masks(kind):
    lane = lax.broadcasted_iota(jnp.int32, (1, 2 * HEAD_DIM), 1)
    low = (lane < HEAD_DIM).astype(kind)
    return (low, (1 - low).astype(kind))


def wide_tile(size):
    return max(tile for tile in range(128, 1409, 128) if size % tile == 0)


def chunks(size, tile):
    return [(start, min(tile, size - start)) for start in range(0, size, tile)]


def stacked_heads(pair):
    return jnp.concatenate([pair * mask for mask in head_masks(pair.dtype)], 0)


def unstacked_heads(stacked):
    rows = stacked.shape[0] // 2
    low = lax.broadcasted_iota(jnp.int32, (1, 2 * HEAD_DIM), 1) < HEAD_DIM
    return jnp.where(low, stacked[:rows], stacked[rows:])


def attend_feed_kernel(
    moment, idx, q, kv, low, high, bias, wo, source, gain, wg, wu, wd, *rest
):
    (k_out, v_out, mixed_out, lse_out, res_out, two_out, gate_out, up_out, gated_out, result) = rest[-18:-8]
    total, gate_w, up_w, down_w, gate_all, up_all, gated_all, sems = rest[-8:]
    step = pl.program_id(0)
    rows, width = source.shape
    tiles = chunks(wg.shape[1], wide_tile(wg.shape[1]))
    ends = pl.num_programs(0) - 1

    def fetches():
        found = []
        for start, size in tiles:
            lanes = pl.ds(start, size)
            found.append(
                [
                    (wg.at[:, lanes], gate_w.at[:, lanes]),
                    (wu.at[:, lanes], up_w.at[:, lanes]),
                    (wd.at[lanes], down_w.at[lanes]),
                ]
            )
        return found

    def fetch(number, part):
        return pltpu.make_async_copy(
            *fetches()[number][part], sems.at[number * 3 + part]
        )

    @pl.when(step == 0)
    def _():
        for number in range(len(tiles)):
            for part in range(3):
                fetch(number, part).start()

    @pl.when(step < ends)
    def _():
        for place, out in ((0, k_out), (1, v_out)):
            out[pl.ds(0, HALO)] = low[place]
            out[pl.ds(HALO, rows)] = kv[place]
            out[pl.ds(HALO + rows, HALO)] = high[place]
        scale = jnp.bfloat16(HEAD_DIM**-0.5)
        for start, count in row_blocks(rows):
            span = count + 2 * HALO
            block_bias = bias[pl.ds(start, count), :span]
            both_bias = jnp.concatenate([block_bias, block_bias], 0)
            sums = []
            for pair in range(WIDE // (2 * HEAD_DIM)):
                lanes = slice(pair * 2 * HEAD_DIM, (pair + 1) * 2 * HEAD_DIM)
                q_both = stacked_heads(q[pl.ds(start, count), lanes] * scale)
                scores = nt_dot(q_both, k_out[pl.ds(start, span), lanes]) + both_bias
                most = jnp.max(scores, axis=-1, keepdims=True)
                powers = jnp.exp(scores - most)
                total_power = jnp.sum(powers, axis=-1, keepdims=True)
                probs = (powers * (1.0 / total_power)).astype(jnp.bfloat16)
                mixed = dot(probs, v_out[pl.ds(start, span), lanes])
                mixed_out[pl.ds(start, count), lanes] = unstacked_heads(mixed).astype(
                    jnp.bfloat16
                )
                log_sum = most + jnp.log(total_power)
                sums += [log_sum[:count], log_sum[count:]]
            lane = lax.broadcasted_iota(jnp.int32, (count, 2 * HEAD_DIM), 1)
            wide = jnp.zeros((count, 2 * HEAD_DIM), jnp.float32)
            for number, value in enumerate(sums):
                wide = jnp.where(lane == number, value, wide)
            lse_out[pl.ds(start, count)] = wide
        part = dot(mixed_out[...], wo[...])

        @pl.when(step == 0)
        def _():
            total[...] = source[...].astype(jnp.float32) + part

        @pl.when(step > 0)
        def _():
            total[...] += part

    @pl.when(step == ends)
    def _():
        residual = total[...]
        res_out[...] = residual
        normed = (residual * inverse_rms(residual) * gain[...].astype(jnp.float32)).astype(
            jnp.bfloat16
        )
        two_out[...] = normed
        base, stores = 3 * len(tiles), []
        for number, (start, size) in enumerate(tiles):
            lanes = slice(start, start + size)
            fetch(number, 0).wait()
            gate = dot(normed, gate_w[:, lanes])
            fetch(number, 1).wait()
            up = dot(normed, up_w[:, lanes])
            half, _, _ = gelu_parts(gate)
            gated = (gate * half * up).astype(jnp.bfloat16)
            gate_all[:, lanes] = gate.astype(jnp.bfloat16)
            up_all[:, lanes] = up.astype(jnp.bfloat16)
            gated_all[:, lanes] = gated
            for part, (here, there) in enumerate(
                ((gate_all, gate_out), (up_all, up_out), (gated_all, gated_out))
            ):
                copy = pltpu.make_async_copy(
                    here.at[:, pl.ds(start, size)],
                    there.at[moment, :, pl.ds(start, size)],
                    sems.at[base + 3 * number + part],
                )
                copy.start()
                stores.append(copy)
            fetch(number, 2).wait()
            total[...] += dot(gated, down_w[lanes])
        result[...] = total[...].astype(jnp.bfloat16)
        for copy in stores:
            copy.wait()


def attend_feed(store, slots, moment, scalars, kv, low, high, bias, params):
    rows, width = kv.shape[1:]
    out_w, gain_two, gate_w, up_w, down_w = params[4:]
    hidden = gate_w.shape[1]
    ext = rows + 2 * HALO
    quads = width // WIDE
    last = lambda j: jnp.minimum(j, quads - 1)
    at_start = lambda j: (0, 0)
    at_tile = lambda j: (0, last(j))
    halo_spec = pl.BlockSpec((2, HALO, WIDE), lambda j, s: (0, 0, last(j)))
    work = width * rows * ((BLOCK + 2 * HALO) * 8 + width * 2 + hidden * 6)
    tiles = len(chunks(hidden, wide_tile(hidden)))
    anywhere = pl.BlockSpec(memory_space=pl.ANY)
    (result,) = slot_call(
        functools.partial(attend_feed_kernel, moment),
        (quads + 1,),
        scalars,
        [store["queries"], kv, low, high, bias, out_w, store["source"], gain_two]
        + [gate_w, up_w, down_w],
        [
            pl.BlockSpec((None, rows, WIDE), lambda j, s: (moment, 0, last(j))),
            pl.BlockSpec((2, rows, WIDE), lambda j, s: (0, 0, last(j))),
            halo_spec,
            halo_spec,
            pl.BlockSpec((None,) + bias.shape[1:], lambda j, s: (s[2], 0, 0)),
            pl.BlockSpec((WIDE, width), lambda j, s: (last(j), 0)),
            pl.BlockSpec((None, rows, width), lambda j, s: (moment, 0, 0)),
            whole_spec((1, width)),
        ]
        + [anywhere] * 3,
        [
            ("keys", (ext, width), (ext, WIDE), at_tile, jnp.bfloat16),
            ("values", (ext, width), (ext, WIDE), at_tile, jnp.bfloat16),
            ("mixed", (rows, width), (rows, WIDE), at_tile, jnp.bfloat16),
            ("lse", (rows, quads * BLOCK), (rows, BLOCK), at_tile, jnp.float32),
            ("residual", (rows, width), (rows, width), at_start, jnp.float32),
            ("normed_two", (rows, width), (rows, width), at_start, jnp.bfloat16),
            ("gate", (rows, hidden), None, None, jnp.bfloat16),
            ("up", (rows, hidden), None, None, jnp.bfloat16),
            ("gated", (rows, hidden), None, None, jnp.bfloat16),
        ],
        [((rows, width), jnp.bfloat16, whole_spec((rows, width)))],
        store,
        slots,
        moment,
        [
            pltpu.VMEM((rows, width), jnp.float32),
            pltpu.VMEM((width, hidden), jnp.bfloat16),
            pltpu.VMEM((width, hidden), jnp.bfloat16),
            pltpu.VMEM((hidden, width), jnp.bfloat16),
            pltpu.VMEM((rows, hidden), jnp.bfloat16),
            pltpu.VMEM((rows, hidden), jnp.bfloat16),
            pltpu.VMEM((rows, hidden), jnp.bfloat16),
            pltpu.SemaphoreType.DMA((6 * tiles,)),
        ],
        cost_of(work, 6 * width * hidden + 2 * width * width + 20 * rows * width),
    )
    return result


def gelu_parts(gate):
    root = 0.7978845608028654
    bend = jnp.tanh(root * (gate + 0.044715 * gate * gate * gate))
    return 0.5 * (1.0 + bend), bend, root


def feed_back_kernel(idx, arrived, own, gate, up, residual, gain, wd, wg, wu, wo, *rest):
    g_out, dg_out, du_out, branch_out, gain_out, res_out, mixed_out, total = rest[-8:]
    step = pl.program_id(0)

    @pl.when(step == 0)
    def _():
        g_out[...] = jnp.where(
            idx[0] == 1, arrived[...].astype(jnp.float32), own[...].astype(jnp.float32)
        ).astype(jnp.bfloat16)

    gate_pre = gate[...].astype(jnp.float32)
    up_pre = up[...].astype(jnp.float32)
    grad_gated = nt_dot(g_out[...], wd[...])
    half, bend, root = gelu_parts(gate_pre)
    slope = half + 0.5 * gate_pre * (1.0 - bend * bend) * root * (
        1.0 + 3.0 * 0.044715 * gate_pre * gate_pre
    )
    grad_gate = (grad_gated * up_pre * slope).astype(jnp.bfloat16)
    grad_up = (grad_gated * gate_pre * half).astype(jnp.bfloat16)
    dg_out[...] = grad_gate
    du_out[...] = grad_up
    part = nt_dot(grad_gate, wg[...]) + nt_dot(grad_up, wu[...])

    @pl.when(step == 0)
    def _():
        total[...] = part

    @pl.when(step > 0)
    def _():
        total[...] += part

    @pl.when(step == pl.num_programs(0) - 1)
    def _():
        grads, grad_gain = norm_back(total[...], residual[...], gain[...].astype(jnp.float32))
        gain_out[...] = jnp.broadcast_to(grad_gain, gain_out.shape)
        grad_residual = g_out[...].astype(jnp.float32) + grads
        res_out[...] = grad_residual
        branch = grad_residual.astype(jnp.bfloat16)
        branch_out[...] = branch
        mixed_out[...] = nt_dot(branch, wo[...]).astype(jnp.bfloat16)


def norm_back(grads, values, gain):
    scale = inverse_rms(values)
    pulled = grads * gain
    mean = jnp.mean(pulled * values, axis=-1, keepdims=True)
    return (
        scale * pulled - values * (scale * scale * scale * mean),
        jnp.sum(grads * values * scale, axis=0, keepdims=True),
    )


def feed_back(store, slots, moment, scalars, arrived, own, params):
    out_w, gain_two, gate_w, up_w, down_w = params[4:]
    rows, width = arrived.shape
    hidden = gate_w.shape[1]
    tile = wide_tile(hidden)
    at_tile = lambda j: (0, j)
    at_start = lambda j: (0, 0)
    taken_tile = pl.BlockSpec((None, rows, tile), lambda j, s: (s[1], 0, j))
    return slot_call(
        feed_back_kernel,
        (hidden // tile,),
        scalars,
        [arrived, own, store["gate"], store["up"], store["residual"], gain_two]
        + [down_w, gate_w, up_w, out_w],
        [whole_spec((rows, width)), whole_spec((rows, width)), taken_tile, taken_tile]
        + [pl.BlockSpec((None, rows, width), lambda j, s: (s[1], 0, 0)), whole_spec((1, width))]
        + [pl.BlockSpec((tile, width), lambda j, s: (j, 0))]
        + [pl.BlockSpec((width, tile), lambda j, s: (0, j))] * 2
        + [whole_spec((width, width))],
        [
            ("grad_result", (rows, width), (rows, width), at_start, jnp.bfloat16),
            ("grad_gate", (rows, hidden), (rows, tile), at_tile, jnp.bfloat16),
            ("grad_up", (rows, hidden), (rows, tile), at_tile, jnp.bfloat16),
            ("grad_branch", (rows, width), (rows, width), at_start, jnp.bfloat16),
            ("gain_two", (8, width), (8, width), at_start, jnp.float32),
        ],
        [
            ((rows, width), jnp.float32, whole_spec((rows, width))),
            ((rows, width), jnp.bfloat16, whole_spec((rows, width))),
        ],
        store,
        slots,
        moment,
        [pltpu.VMEM((rows, width), jnp.float32)],
        cost_of(6 * rows * width * hidden + 2 * rows * width * width, 6 * width * hidden),
    )


def attend_back_kernel(idx, q, keys, values, mixed, lse, grad_mixed, bias, *rest):
    q_out, center, top, bottom, k_total, v_total = rest[-6:]
    rows = q.shape[0]
    scale = jnp.bfloat16(HEAD_DIM**-0.5)
    k_total[...] = jnp.zeros_like(k_total)
    v_total[...] = jnp.zeros_like(v_total)
    for start, count in row_blocks(rows):
        span = count + 2 * HALO
        block_bias = bias[pl.ds(start, count), :span]
        both_bias = jnp.concatenate([block_bias, block_bias], 0)
        for pair in range(WIDE // (2 * HEAD_DIM)):
            lanes = slice(pair * 2 * HEAD_DIM, (pair + 1) * 2 * HEAD_DIM)
            q_both = stacked_heads(q[pl.ds(start, count), lanes] * scale)
            g_both = stacked_heads(grad_mixed[pl.ds(start, count), lanes])
            m_pair = mixed[pl.ds(start, count), lanes].astype(jnp.float32)
            k_pair = keys[pl.ds(start, span), lanes]
            log_sum = jnp.concatenate(
                [lse[pl.ds(start, count), 2 * pair + n : 2 * pair + n + 1] for n in range(2)], 0
            )
            probs = jnp.exp(nt_dot(q_both, k_pair) + (both_bias - log_sum))
            grad_probs = nt_dot(g_both, values[pl.ds(start, span), lanes])
            mean = jnp.sum(
                g_both.astype(jnp.float32) * jnp.concatenate([m_pair, m_pair], 0),
                axis=-1,
                keepdims=True,
            )
            grad_scores = (probs * (grad_probs - mean)).astype(jnp.bfloat16)
            q_out[pl.ds(start, count), lanes] = (
                unstacked_heads(dot(grad_scores, k_pair)) * (HEAD_DIM**-0.5)
            ).astype(jnp.bfloat16)
            k_total[pl.ds(start, span), lanes] += tn_dot(grad_scores, q_both)
            v_total[pl.ds(start, span), lanes] += tn_dot(probs.astype(jnp.bfloat16), g_both)
    for place, total in ((0, k_total), (1, v_total)):
        top[place] = total[pl.ds(0, HALO)].astype(jnp.bfloat16)
        center[place] = total[pl.ds(HALO, rows)]
        bottom[place] = total[pl.ds(HALO + rows, HALO)].astype(jnp.bfloat16)


def attend_back(store, slots, moment, scalars, grad_mixed, bias):
    rows, width = grad_mixed.shape
    ext = rows + 2 * HALO
    taken = pl.BlockSpec((None, rows, WIDE), lambda j, s: (s[1], 0, j))
    taken_ext = pl.BlockSpec((None, ext, WIDE), lambda j, s: (s[1], 0, j))
    halo_spec = pl.BlockSpec((2, HALO, WIDE), lambda j, s: (0, 0, j))
    work = width * rows * (BLOCK + 2 * HALO) * 2
    return slot_call(
        attend_back_kernel,
        (width // WIDE,),
        scalars,
        [store["queries"], store["keys"], store["values"], store["mixed"], store["lse"]]
        + [grad_mixed, bias],
        [
            taken,
            taken_ext,
            taken_ext,
            taken,
            pl.BlockSpec((None, rows, BLOCK), lambda j, s: (s[1], 0, j)),
            pl.BlockSpec((rows, WIDE), lambda j, s: (0, j)),
            pl.BlockSpec((None,) + bias.shape[1:], lambda j, s: (s[2], 0, 0)),
        ],
        [("grad_queries", (rows, width), (rows, WIDE), lambda j: (0, j), jnp.bfloat16)],
        [
            (
                (2, rows, width),
                jnp.float32,
                pl.BlockSpec((2, rows, WIDE), lambda j, s: (0, 0, j)),
            ),
            ((2, HALO, width), jnp.bfloat16, halo_spec),
            ((2, HALO, width), jnp.bfloat16, halo_spec),
        ],
        store,
        slots,
        moment,
        [pltpu.VMEM((ext, WIDE), jnp.float32)] * 2,
        cost_of(work * 20, 24 * rows * width),
    )


def project_back_kernel(
    idx, grad_q, center, below, above, source, gain, grad_res, wq, wk, wv, *rest
):
    k_out, v_out, gain_out, in_out, total = rest[-5:]
    step = pl.program_id(0)
    rows = source.shape[0]
    for place, out in ((0, k_out), (1, v_out)):
        head = center[place, pl.ds(0, HALO)] + below[place].astype(jnp.float32)
        tail = center[place, pl.ds(rows - HALO, HALO)] + above[place].astype(jnp.float32)
        out[pl.ds(0, HALO)] = head.astype(jnp.bfloat16)
        out[pl.ds(HALO, rows - 2 * HALO)] = center[place, pl.ds(HALO, rows - 2 * HALO)].astype(
            jnp.bfloat16
        )
        out[pl.ds(rows - HALO, HALO)] = tail.astype(jnp.bfloat16)
    part = nt_dot(grad_q[...], wq[...]) + nt_dot(k_out[...], wk[...]) + nt_dot(v_out[...], wv[...])

    @pl.when(step == 0)
    def _():
        total[...] = part

    @pl.when(step > 0)
    def _():
        total[...] += part

    @pl.when(step == pl.num_programs(0) - 1)
    def _():
        grads, grad_gain = norm_back(
            total[...], source[...].astype(jnp.float32), gain[...].astype(jnp.float32)
        )
        gain_out[...] = jnp.broadcast_to(grad_gain, gain_out.shape)
        in_out[...] = (grad_res[...] + grads).astype(jnp.bfloat16)


def project_back(store, slots, moment, scalars, center, below, above, grad_res, params):
    rows, width = grad_res.shape
    gain_one, query_w, key_w, value_w = params[:4]
    at_tile = lambda j: (0, j)
    at_start = lambda j: (0, 0)
    halo_spec = pl.BlockSpec((2, HALO, WIDE), lambda j, s: (0, 0, j))
    columns = pl.BlockSpec((width, WIDE), lambda j, s: (0, j))
    return slot_call(
        project_back_kernel,
        (width // WIDE,),
        scalars,
        [store["grad_queries"], center, below, above, store["source"], gain_one, grad_res]
        + [query_w, key_w, value_w],
        [
            pl.BlockSpec((None, rows, WIDE), lambda j, s: (moment, 0, j)),
            pl.BlockSpec((2, rows, WIDE), lambda j, s: (0, 0, j)),
            halo_spec,
            halo_spec,
            pl.BlockSpec((None, rows, width), lambda j, s: (s[1], 0, 0)),
            whole_spec((1, width)),
            whole_spec((rows, width)),
        ]
        + [columns] * 3,
        [
            ("grad_keys", (rows, width), (rows, WIDE), at_tile, jnp.bfloat16),
            ("grad_values", (rows, width), (rows, WIDE), at_tile, jnp.bfloat16),
            ("gain_one", (8, width), (8, width), at_start, jnp.float32),
        ],
        [((rows, width), jnp.bfloat16, whole_spec((rows, width)))],
        store,
        slots,
        moment,
        [pltpu.VMEM((rows, width), jnp.float32)],
        cost_of(6 * rows * width * width, 6 * width * width + 20 * rows * width),
    )


def window_bias(lengths_row, shard_no, rows, seq_len):
    ends = jnp.cumsum(lengths_row)
    first = shard_no * rows
    row = jnp.arange(rows, dtype=jnp.int32)
    place = (row // BLOCK * BLOCK)[:, None] - HALO + jnp.arange(BLOCK + 2 * HALO, dtype=jnp.int32)

    def document(position):
        return jnp.sum((position[..., None] >= ends).astype(jnp.int32), axis=-1)

    key = first + place
    allowed = (
        (jnp.abs(row[:, None] - place) <= RADIUS)
        & (key >= 0)
        & (key < seq_len)
        & (document(first + row)[:, None] == document(key))
    )
    return jnp.where(allowed, 0.0, NEVER).astype(jnp.float32)


def after(cells, *others):
    return lax.optimization_barrier((cells,) + others)[0] if others else cells


class Link:
    def __init__(self, axis, pairs, depth):
        self.axis, self.pairs, self.depth, self.sent = axis, pairs, depth, []

    def __call__(self, cells):
        if self.depth and len(self.sent) >= self.depth:
            cells = after(cells, self.sent[-self.depth])
        self.sent.append(lax.ppermute(cells, self.axis, self.pairs))
        return self.sent[-1]


def links(depth=2):
    span = lax.axis_size("seq")
    high = span // 2
    across = [(h * 2 + c, ((h + 1) % high) * 2 + c) for h in range(high) for c in range(2)]
    pairs = [(i, i ^ 1) for i in range(span)]
    rings = lax.axis_size("wt")
    along = [(i, (i + 1) % rings) for i in range(rings)]
    return Link("seq", across, depth), Link("seq", pairs, 0), Link("wt", along, 0)


def places():
    high = lax.axis_size("seq") // 2
    shard_no = lax.axis_index("seq")
    return high, shard_no // 2, shard_no % 2


class Gather:
    def __init__(self, shard, lines):
        self.across, self.swap = lines[:2]
        self.level = lax.all_gather(shard, "wt", axis=0)

    def cross(self, *others):
        self.row = [after(self.level, *others)]
        for _ in range(1, lax.axis_size("seq") // 2):
            self.row.append(self.across(self.row[-1]))
        return self

    def pieces(self, *others):
        found = {}
        for j, part in enumerate(self.row):
            part = after(part, *others) if j else part
            found[(None, j, 0)] = part
            found[(None, j, 1)] = self.swap(part)
        return found


def ring_gather(shard, lines):
    across, swap, along = lines
    found, current = {}, shard
    for k in range(lax.axis_size("wt")):
        current = along(current) if k else current
        cells = current
        for j in range(lax.axis_size("seq") // 2):
            cells = across(cells) if j else cells
            found[(k, j, 0)] = cells
            found[(k, j, 1)] = swap(cells)
    return found


def assemble_kernel(count, plan, seat_ref, *refs):
    parts, wholes, sems = refs[:count], refs[count:-1], refs[-1]
    copies = []
    for number, (source, start, rows, seat, ring, whole, to) in enumerate(plan):
        there = wholes[whole].at[seat_ref[seat]]
        if ring is None:
            here, there = parts[source].at[:, pl.ds(start, rows)], there.at[:, pl.ds(to, rows)]
        else:
            here = parts[source].at[pl.ds(start, rows)]
            there = there.at[seat_ref[ring], pl.ds(to, rows)]
        copies.append(pltpu.make_async_copy(here, there, sems.at[number]))
    for copy in copies:
        copy.start()
    for copy in copies:
        copy.wait()


def assemble(pieces, pack):
    high, h, c = places()
    rings, z = lax.axis_size("wt"), lax.axis_index("wt")
    seats = [
        lax.rem(h - j + high, high) * 2 + (c + p) % 2 for j in range(high) for p in range(2)
    ] + [lax.rem(z - k + rings, rings) for k in range(rings)]
    sources, plan = [], []
    for (k, j, p), part in pieces.items():
        start = 0
        for whole, rows in enumerate(pack):
            ring = None if k is None else 2 * high + k
            plan.append((len(sources), start, rows, j * 2 + p, ring, whole, 0))
            start += rows
        sources.append(part)
    width, kind = sources[0].shape[-1], sources[0].dtype
    shapes = [(2 * high, rings, rows, width) for rows in pack]
    if any(rows % 16 for rows in pack):
        wholes = [jnp.zeros(shape, kind) for shape in shapes]
        for source, start, rows, seat, ring, whole, to in plan:
            part = sources[source]
            part = part[None] if ring is None else part[None, None]
            part = part[:, :, start : start + rows]
            place = (seats[seat], 0 if ring is None else seats[ring], to, 0)
            wholes[whole] = lax.dynamic_update_slice(wholes[whole], part, place)
    else:
        wholes = pl.pallas_call(
            functools.partial(assemble_kernel, len(sources), plan),
            out_shape=[jax.ShapeDtypeStruct(shape, kind) for shape in shapes],
            grid_spec=pltpu.PrefetchScalarGridSpec(
                num_scalar_prefetch=1,
                grid=(),
                in_specs=[pl.BlockSpec(memory_space=pl.ANY)] * len(sources),
                out_specs=[pl.BlockSpec(memory_space=pltpu.VMEM)] * len(shapes),
                scratch_shapes=[pltpu.SemaphoreType.DMA((len(plan),))],
            ),
            compiler_params=pltpu.CompilerParams(vmem_limit_bytes=40 * 2**20),
            cost_estimate=cost_of(0, 2 * sum(source.size * 2 for source in sources)),
        )(jnp.stack(seats).astype(jnp.int32), *sources)
    return [whole.reshape(-1, width) for whole in wholes]


def plus(left, right, kind):
    return (left.astype(jnp.float32) + right.astype(jnp.float32)).astype(kind)


class Scatter:
    def __init__(self, partial, lines, kind=jnp.bfloat16, along_first=False):
        self.across, self.swap = lines[:2]
        self.kind, self.along_first = kind, along_first
        high, h, c = places()
        self.high, self.h = high, h
        cells = partial.reshape(high, 2, -1, partial.shape[-1])
        self.mine = lax.dynamic_index_in_dim(cells, c, 1, False)
        self.received = self.swap(lax.dynamic_index_in_dim(cells, 1 - c, 1, False))
        if along_first:
            rows = self.mine.shape[1]
            rings = lax.axis_size("wt")
            whole = plus(self.mine, self.received, kind)
            whole = whole.reshape(high, rings, rows // rings, -1).swapaxes(0, 1)
            self.summed = whole.reshape(high * rows, -1)
            summed = lax.psum_scatter(self.summed, "wt", scatter_dimension=0, tiled=True)
            self.mine = summed.reshape(high, rows // rings, -1)
            self.level = None
        else:
            self.level = self.block(1)

    def block(self, j):
        place = lax.rem(self.h - j + self.high, self.high)
        mine = lax.dynamic_index_in_dim(self.mine, place, 0, False)
        if self.along_first:
            return mine
        return plus(mine, lax.dynamic_index_in_dim(self.received, place, 0, False), self.kind)

    def cross(self, *others):
        self.level = self.block(1) if self.level is None else self.level
        self.arrived = self.across(after(self.level, *others))
        return self

    def add(self, *others):
        level = self.arrived
        for j in range(2, self.high + 1):
            level = plus(after(level, *others), self.block(j), self.kind)
            if j < self.high:
                level = self.across(level)
        self.level = level
        return self

    def finish(self):
        level = self.level
        if not self.along_first:
            level = lax.psum_scatter(level, "wt", scatter_dimension=0, tiled=True)
        return level.astype(jnp.float32)


def ring_scatter(partial, lines):
    across, swap, along = lines
    high, h, c = places()
    rings, z = lax.axis_size("wt"), lax.axis_index("wt")
    cells = partial.reshape(high, 2, rings, -1, partial.shape[-1])
    mine = lax.dynamic_index_in_dim(cells, c, 1, False)
    received = swap(lax.dynamic_index_in_dim(cells, 1 - c, 1, False))
    size = (1, 1) + cells.shape[3:]

    def block(j, k):
        place = (lax.rem(h - j + high, high), lax.rem(z - k + rings, rings), 0, 0)
        return plus(
            lax.dynamic_slice(mine, place, size)[0, 0],
            lax.dynamic_slice(received, place, size)[0, 0],
            jnp.bfloat16,
        )

    total = None
    for k in range(1, rings + 1):
        level = block(1, k)
        for j in range(2, high + 1):
            level = plus(across(level), block(j, k), jnp.bfloat16)
        if total is None:
            total = level
        else:
            total = plus(along(total), level, jnp.float32 if k == rings else jnp.bfloat16)
    return total.astype(jnp.float32)


def per_device(
    inputs,
    lengths,
    cotangent,
    gain_attn,
    w_query,
    w_key,
    w_value,
    w_out,
    gain_mlp,
    w_gate,
    w_up,
    w_down,
):
    section_no = lax.axis_index("section")
    shard_no = lax.axis_index("seq")
    micro_count, rows_local, model_width = inputs.shape
    seq_len = rows_local * lax.axis_size("seq")
    is_first = (section_no == 0).astype(jnp.int32)
    slots = micro_count + 1
    bias = jnp.stack(
        [
            window_bias(lengths[number], shard_no, rows_local, seq_len)
            for number in range(micro_count)
        ]
    )

    def choose(of_first, of_second):
        return is_first * of_first + (1 - is_first) * of_second

    rows = w_query.shape[1]
    gains = jnp.pad(
        jnp.concatenate([gain_attn, gain_mlp], 1), ((0, 15), (0, model_width - 2 * rows))
    )
    lines = links()
    narrow = jnp.concatenate([w_query[0], w_key[0], w_value[0], w_out[0], gains], 0)
    gate_gather = Gather(w_gate[0], lines)
    up_gather = Gather(w_up[0], lines)
    down_gather = Gather(w_down[0], lines)
    query_w, key_w, value_w, out_w, gain_rows = assemble(
        ring_gather(narrow, lines), [rows, rows, rows, rows, 16]
    )
    gate_gather.cross()
    gain_rows = gain_rows.reshape(-1, 16, model_width)[:, 0]
    gain_one = gain_rows[:, :rows].reshape(1, -1)
    gain_two = gain_rows[:, rows : 2 * rows].reshape(1, -1)
    params = (gain_one, query_w, key_w, value_w, out_w, gain_two)

    store, results, grad_sources = {}, [], []
    arrived = jnp.zeros((rows_local, model_width), jnp.bfloat16)
    for moment in range(slots):
        early, late = min(moment, micro_count - 1), max(moment - 1, 0)
        scalars = jnp.stack([is_first, is_first * 0 + moment, choose(early, late)])
        kv, tail, head = project(store, slots, moment, scalars, inputs[early], arrived, params)
        low = shifted(tail, "seq", 1)
        high = shifted(head, "seq", -1)
        if moment == 0:
            up_gather.cross(kv)
            down_gather.cross(kv)
            (gate_w,) = assemble(gate_gather.pieces(kv), [rows])
            (up_w,) = assemble(up_gather.pieces(kv), [rows])
            (down_w,) = assemble(down_gather.pieces(kv), [w_down.shape[1]])
            params = params + (gate_w, up_w, down_w)
        result = attend_feed(store, slots, moment, scalars, kv, low, high, bias, params)
        results.append(result)
        if moment < micro_count:
            arrived = shifted(result, "section", 1)
    activations = jnp.stack(
        [
            jnp.where(is_first == 1, results[number], results[number + 1])
            for number in range(micro_count)
        ]
    )[None]

    def both(name, start):
        chosen = lax.dynamic_slice_in_dim(store[name], start, micro_count, 0)
        return chosen.reshape(-1, chosen.shape[-1])

    def product(left, *right):
        left = both(left, 1 - is_first)
        right = jnp.concatenate([both(name, is_first) for name in right], 1)
        return jnp.dot(left.T, right, preferred_element_type=jnp.float32).astype(jnp.bfloat16)

    arrived_grad = jnp.zeros((rows_local, model_width), jnp.bfloat16)
    for moment in range(slots):
        early, late = min(moment, micro_count - 1), max(moment - 1, 0)
        scalars = jnp.stack(
            [is_first, choose(late, min(moment + 1, micro_count)), choose(late, early)]
        )
        grad_res, grad_mixed = feed_back(
            store, slots, moment, scalars, arrived_grad, cotangent[early], params
        )
        if moment == micro_count:
            lines = links()
            out_part = product("mixed", "grad_branch")
            out_sum = Scatter(out_part, lines, along_first=True)
            gate_sum = Scatter(after(product("normed_two", "grad_gate"), out_part), lines)
            down_sum = Scatter(after(product("gated", "grad_result"), out_sum.summed), lines)
            gate_sum.cross(out_sum.summed)
            up_part = product("normed_two", "grad_up")
            grad_mixed = after(grad_mixed, up_part, down_sum.level)
            up_sum = Scatter(up_part, lines)
            down_sum.cross()
        center, top, bottom = attend_back(store, slots, moment, scalars, grad_mixed, bias)
        above = shifted(top, "seq", -1)
        below = shifted(bottom, "seq", 1)
        if moment == micro_count:
            gate_sum.add(center)
            center = after(center, gate_sum.level, up_sum.level)
        (grad_source,) = project_back(
            store, slots, moment, scalars, center, below, above, grad_res, params
        )
        grad_sources.append(grad_source)
        if moment < micro_count:
            arrived_grad = shifted(grad_source, "section", -1)
    input_grads = jnp.stack(
        [
            jnp.where(is_first == 1, grad_sources[number + 1], grad_sources[number])
            for number in range(micro_count)
        ]
    )[None]
    up_sum.cross()
    down_sum.add(grad_source)
    gain_rows = jnp.concatenate(
        [
            jnp.sum(lax.dynamic_slice_in_dim(store[name], is_first, micro_count, 0), 0)
            for name in ("gain_one", "gain_two")
        ]
    ).astype(jnp.bfloat16)
    picked = jnp.arange(2 * 8)[:, None] == jnp.arange(BLOCK)[None] * 8
    right = jnp.concatenate(
        [both(name, is_first) for name in ("grad_queries", "grad_keys", "grad_values")], 1
    )
    right = jnp.concatenate(
        [
            jnp.pad(right, ((0, 0), (0, BLOCK))),
            jnp.pad(picked.astype(jnp.bfloat16), ((0, 0), (right.shape[1], 0))),
        ]
    )
    left = jnp.concatenate([both("normed", 1 - is_first), gain_rows])
    qkv_part = jnp.dot(left.T, right, preferred_element_type=jnp.float32).astype(jnp.bfloat16)
    up_sum.add(qkv_part)
    qkv_all = ring_scatter(after(qkv_part, down_sum.level), lines)
    grad_out_w = out_sum.cross().add().finish()
    grad_gate_w, grad_down_w, grad_up_w = gate_sum.finish(), down_sum.finish(), up_sum.finish()
    grad_query_w, grad_key_w, grad_value_w, gain_sum = (
        qkv_all[:, number * model_width : (number + 1) * model_width] for number in range(4)
    )
    return (
        activations,
        input_grads,
        gain_sum[:, 0][None],
        grad_query_w[None],
        grad_key_w[None],
        grad_value_w[None],
        grad_out_w[None],
        gain_sum[:, 1][None],
        grad_gate_w[None],
        grad_up_w[None],
        grad_down_w[None],
    )


def solution(mesh):
    placed = (
        P("wt", "seq", None),
        P("wt", None),
        P("wt", "seq", None),
        P("section", ("seq", "wt")),
        P("section", ("seq", "wt"), None),
        P("section", ("seq", "wt"), None),
        P("section", ("seq", "wt"), None),
        P("section", ("seq", "wt"), None),
        P("section", ("seq", "wt")),
        P("section", ("seq", "wt"), None),
        P("section", ("seq", "wt"), None),
        P("section", ("seq", "wt"), None),
    )
    return jax.shard_map(
        per_device,
        mesh=mesh,
        in_specs=placed,
        out_specs=(
            P("section", "wt", "seq", None),
            P("section", "wt", "seq", None),
            P("section", ("seq", "wt")),
            P("section", ("seq", "wt"), None),
            P("section", ("seq", "wt"), None),
            P("section", ("seq", "wt"), None),
            P("section", ("seq", "wt"), None),
            P("section", ("seq", "wt")),
            P("section", ("seq", "wt"), None),
            P("section", ("seq", "wt"), None),
            P("section", ("seq", "wt"), None),
        ),
        check_vma=False,
    )
```

```python
import functools

import jax
import jax.numpy as jnp
from jax import lax
from jax.experimental import pallas as pl
from jax.experimental.pallas import tpu as pltpu
from jax.sharding import PartitionSpec as P

HEAD_DIM = 64
RADIUS = 127


EPSILON = 1e-06


def shifted(shard, axis, by):
    length = lax.axis_size(axis)
    pairs = [(i, i + by) for i in range(length) if 0 <= i + by < length]
    return lax.ppermute(shard, axis, pairs)


HALO = 128
BLOCK = 128
WIDE = 256
NEVER = -1e30


def call(kernel, grid, scalars, ins, in_specs, outs, out_specs, scratch=(), aliases=None, cost=None):
    return pl.pallas_call(
        kernel,
        out_shape=outs,
        grid_spec=pltpu.PrefetchScalarGridSpec(
            num_scalar_prefetch=1,
            grid=grid,
            in_specs=in_specs,
            out_specs=out_specs,
            scratch_shapes=list(scratch),
        ),
        input_output_aliases=aliases or {},
        compiler_params=pltpu.CompilerParams(
            vmem_limit_bytes=56 * 2**20, dimension_semantics=("arbitrary",) * len(grid)
        ),
        cost_estimate=cost,
    )(scalars, *ins)


def cost_of(flops, moved, transcendentals=0):
    return pl.CostEstimate(
        flops=int(flops), bytes_accessed=int(moved), transcendentals=int(transcendentals)
    )


def nt_dot(left, right):
    return lax.dot_general(
        left, right, (((1,), (1,)), ((), ())), preferred_element_type=jnp.float32
    )


def tn_dot(left, right):
    return lax.dot_general(
        left, right, (((0,), (0,)), ((), ())), preferred_element_type=jnp.float32
    )


def dot(left, right):
    return jnp.dot(left, right, preferred_element_type=jnp.float32)


def inverse_rms(values):
    return lax.rsqrt(jnp.mean(values * values, axis=-1, keepdims=True) + EPSILON)


def flat(ref):
    cells = ref[...]
    return cells.reshape(-1, cells.shape[-1])


def packed_spec(packed, number, tile):
    rows = (packed.shape[1] - 16) // 4
    return pl.BlockSpec((packed.shape[0], rows, tile), lambda j, s: (0, number, j))


def project_kernel(idx, own, arrived, gain, wq, wk, wv, *rest):
    x_out, n_out, q_out, kv_out, tail_out, head_out = rest[-6:]

    @pl.when(pl.program_id(0) == 0)
    def _():
        picked = jnp.where(
            idx[0] == 1, own[...].astype(jnp.float32), arrived[...].astype(jnp.float32)
        )
        x_out[...] = picked.astype(jnp.bfloat16)
        n_out[...] = (picked * inverse_rms(picked) * gain[...].astype(jnp.float32)).astype(
            jnp.bfloat16
        )

    normed = n_out[...]
    kv_out[0] = dot(normed, flat(wk)).astype(jnp.bfloat16)
    kv_out[1] = dot(normed, flat(wv)).astype(jnp.bfloat16)
    q_out[...] = dot(normed, flat(wq)).astype(jnp.bfloat16)
    tail_out[...] = kv_out[:, pl.ds(kv_out.shape[1] - HALO, HALO)]
    head_out[...] = kv_out[:, pl.ds(0, HALO)]


def slot_call(kernel, grid, scalars, ins, in_specs, kept, fresh, store, slots, moment, scratch=(), cost=None):
    aliases, extra = {}, []
    outs, out_specs = [], []
    for name, shape, block, index, kind in kept:
        outs.append(jax.ShapeDtypeStruct((slots,) + shape, kind))
        if block is None:
            out_specs.append(pl.BlockSpec(memory_space=pl.ANY))
        else:
            out_specs.append(
                pl.BlockSpec((None,) + block, lambda j, s, index=index: (moment,) + index(j))
            )
        if name in store:
            aliases[1 + len(ins) + len(extra)] = len(outs) - 1
            extra.append(store[name])
    for shape, kind, spec in fresh:
        outs.append(jax.ShapeDtypeStruct(shape, kind))
        out_specs.append(spec)
    results = call(
        kernel,
        grid,
        scalars,
        list(ins) + extra,
        list(in_specs) + [pl.BlockSpec(memory_space=pl.ANY)] * len(extra),
        outs,
        out_specs,
        scratch,
        aliases,
        cost,
    )
    for (name, *_), value in zip(kept, results):
        store[name] = value
    return results[len(kept) :]


def whole_spec(shape):
    return pl.BlockSpec(shape, lambda j, s: (0,) * len(shape))


def project(store, slots, moment, scalars, own, arrived, params):
    rows, width = arrived.shape
    gain_one, packed = params[:2]
    tile = WIDE
    at_start = lambda j: (0, 0)
    halo_spec = pl.BlockSpec((2, HALO, tile), lambda j, s: (0, 0, j))
    return slot_call(
        project_kernel,
        (width // tile,),
        scalars,
        [own, arrived, gain_one, packed, packed, packed],
        [whole_spec((rows, width)), whole_spec((rows, width)), whole_spec((1, width))]
        + [packed_spec(packed, number, tile) for number in range(3)],
        [
            ("source", (rows, width), (rows, width), at_start, jnp.bfloat16),
            ("normed", (rows, width), (rows, width), at_start, jnp.bfloat16),
            ("queries", (rows, width), (rows, tile), lambda j: (0, j), jnp.bfloat16),
        ],
        [
            (
                (2, rows, width),
                jnp.bfloat16,
                pl.BlockSpec((2, rows, tile), lambda j, s: (0, 0, j)),
            ),
            ((2, HALO, width), jnp.bfloat16, halo_spec),
            ((2, HALO, width), jnp.bfloat16, halo_spec),
        ],
        store,
        slots,
        moment,
        cost=cost_of(6 * rows * width * width, 6 * width * width + 14 * rows * width),
    )


def row_blocks(rows):
    return [(start, min(BLOCK, rows - start)) for start in range(0, rows, BLOCK)]


def head_masks(kind):
    lane = lax.broadcasted_iota(jnp.int32, (1, 2 * HEAD_DIM), 1)
    low = (lane < HEAD_DIM).astype(kind)
    return (low, (1 - low).astype(kind))


def wide_tile(size):
    return max(tile for tile in range(128, 1409, 128) if size % tile == 0)


def chunks(size, tile):
    return [(start, min(tile, size - start)) for start in range(0, size, tile)]


def stacked_heads(pair):
    return jnp.concatenate([pair * mask for mask in head_masks(pair.dtype)], 0)


def unstacked_heads(stacked):
    rows = stacked.shape[0] // 2
    low = lax.broadcasted_iota(jnp.int32, (1, 2 * HEAD_DIM), 1) < HEAD_DIM
    return jnp.where(low, stacked[:rows], stacked[rows:])


def attend_step(q, kv, low, high, bias, wo, k_out, v_out, mixed_out, lse_out):
    rows = q.shape[0]
    for place, out in ((0, k_out), (1, v_out)):
        out[pl.ds(0, HALO)] = low[place]
        out[pl.ds(HALO, rows)] = kv[place]
        out[pl.ds(HALO + rows, HALO)] = high[place]
    scale = jnp.bfloat16(HEAD_DIM**-0.5)
    for start, count in row_blocks(rows):
        span = count + 2 * HALO
        block_bias = bias[pl.ds(start, count), :span]
        both_bias = jnp.concatenate([block_bias, block_bias], 0)
        sums = []
        for pair in range(WIDE // (2 * HEAD_DIM)):
            lanes = slice(pair * 2 * HEAD_DIM, (pair + 1) * 2 * HEAD_DIM)
            q_both = stacked_heads(q[pl.ds(start, count), lanes] * scale)
            scores = nt_dot(q_both, k_out[pl.ds(start, span), lanes]) + both_bias
            most = jnp.max(scores, axis=-1, keepdims=True)
            powers = jnp.exp(scores - most)
            total_power = jnp.sum(powers, axis=-1, keepdims=True)
            probs = (powers * (1.0 / total_power)).astype(jnp.bfloat16)
            mixed = dot(probs, v_out[pl.ds(start, span), lanes])
            mixed_out[pl.ds(start, count), lanes] = unstacked_heads(mixed).astype(jnp.bfloat16)
            log_sum = most + jnp.log(total_power)
            sums += [log_sum[:count], log_sum[count:]]
        lane = lax.broadcasted_iota(jnp.int32, (count, 2 * HEAD_DIM), 1)
        wide = jnp.zeros((count, 2 * HEAD_DIM), jnp.float32)
        for number, value in enumerate(sums):
            wide = jnp.where(lane == number, value, wide)
        lse_out[pl.ds(start, count)] = wide
    return dot(mixed_out[...], flat(wo))


def attend_steps(parts, source, gain, res_out, two_out, total, steps):
    step = pl.program_id(0)

    @pl.when(step < steps)
    def _():
        part = attend_step(*parts)

        @pl.when(step == 0)
        def _():
            total[...] = source[...].astype(jnp.float32) + part

        @pl.when(step > 0)
        def _():
            total[...] += part

        @pl.when(step == steps - 1)
        def _():
            residual = total[...]
            res_out[...] = residual
            two_out[...] = (
                residual * inverse_rms(residual) * gain[...].astype(jnp.float32)
            ).astype(jnp.bfloat16)


def attend_kernel(steps, idx, q, kv, low, high, bias, wo, source, gain, *rest):
    k_out, v_out, mixed_out, lse_out, res_out, two_out, total = rest[-7:]
    parts = (q, kv, low, high, bias, wo, k_out, v_out, mixed_out, lse_out)
    attend_steps(parts, source, gain, res_out, two_out, total, steps)


class Feed:
    def __init__(self, moment, weights, outs, held, sems):
        self.moment, self.weights, self.outs, self.held, self.sems = (
            moment,
            weights,
            outs,
            held,
            sems,
        )
        size = weights[0].shape[1]
        self.tiles = chunks(size, wide_tile(size))

    def fetch(self, number, part):
        start, size = self.tiles[number]
        place = (slice(None), pl.ds(start, size)) if part < 2 else (pl.ds(start, size),)
        return pltpu.make_async_copy(
            self.weights[part].at[place], self.held[part].at[place], self.sems.at[3 * number + part]
        )

    def start(self):
        for number in range(len(self.tiles)):
            for part in range(3):
                self.fetch(number, part).start()

    def run(self, normed, total, result):
        gate_w, up_w, down_w = self.held[:3]
        stores = []
        for number, (start, size) in enumerate(self.tiles):
            lanes = slice(start, start + size)
            self.fetch(number, 0).wait()
            gate = dot(normed, gate_w[:, lanes])
            self.fetch(number, 1).wait()
            up = dot(normed, up_w[:, lanes])
            half, _, _ = gelu_parts(gate)
            gated = (gate * half * up).astype(jnp.bfloat16)
            values = (gate.astype(jnp.bfloat16), up.astype(jnp.bfloat16), gated)
            for part, value in enumerate(values):
                held = self.held[3 + part]
                held[:, lanes] = value
                copy = pltpu.make_async_copy(
                    held.at[:, pl.ds(start, size)],
                    self.outs[part].at[self.moment, :, pl.ds(start, size)],
                    self.sems.at[3 * len(self.tiles) + 3 * number + part],
                )
                copy.start()
                stores.append(copy)
            self.fetch(number, 2).wait()
            total[...] += dot(gated, down_w[lanes])
        result[...] = total[...].astype(jnp.bfloat16)
        for copy in stores:
            copy.wait()


def feed_kernel(moment, idx, two, residual, wg, wu, wd, *rest):
    outs, result, total, held, sems = rest[-12:-9], rest[-9], rest[-8], rest[-7:-1], rest[-1]
    feed = Feed(moment, (wg, wu, wd), outs, held, sems)
    feed.start()
    total[...] = residual[...]
    feed.run(two[...], total, result)


def attend_feed_kernel(
    moment, steps, idx, q, kv, low, high, bias, wo, source, gain, wg, wu, wd, *rest
):
    k_out, v_out, mixed_out, lse_out, res_out, two_out = rest[-18:-12]
    outs, result, total, held, sems = rest[-12:-9], rest[-9], rest[-8], rest[-7:-1], rest[-1]
    feed = Feed(moment, (wg, wu, wd), outs, held, sems)
    pl.when(pl.program_id(0) == 0)(feed.start)
    parts = (q, kv, low, high, bias, wo, k_out, v_out, mixed_out, lse_out)
    attend_steps(parts, source, gain, res_out, two_out, total, steps)

    @pl.when(pl.program_id(0) == steps)
    def _():
        feed.run(two_out[...], total, result)


def attend(store, slots, moment, scalars, kv, low, high, bias, params):
    rows, width = kv.shape[1:]
    packed, gain_two = params[1:3]
    weights = params[3:]
    shard = (packed.shape[1] - 16) // 4
    ext = rows + 2 * HALO
    quads = width // WIDE
    last = lambda j: jnp.minimum(j, quads - 1)
    at_start = lambda j: (0, 0)
    at_tile = lambda j: (0, last(j))
    halo_spec = pl.BlockSpec((2, HALO, WIDE), lambda j, s: (0, 0, last(j)))
    fed = feed_parts(rows, width, weights) if weights else ([], [], [], 0)
    kernel = functools.partial(attend_feed_kernel, moment) if weights else attend_kernel
    return slot_call(
        functools.partial(kernel, quads),
        (quads + (1 if weights else 0),),
        scalars,
        [store["queries"], kv, low, high, bias, packed, store["source"], gain_two, *weights],
        [
            pl.BlockSpec((None, rows, WIDE), lambda j, s: (moment, 0, last(j))),
            pl.BlockSpec((2, rows, WIDE), lambda j, s: (0, 0, last(j))),
            halo_spec,
            halo_spec,
            pl.BlockSpec((None,) + bias.shape[1:], lambda j, s: (s[2], 0, 0)),
            pl.BlockSpec((WIDE // shard, shard, width), lambda j, s: (last(j), 3, 0)),
            pl.BlockSpec((None, rows, width), lambda j, s: (moment, 0, 0)),
            whole_spec((1, width)),
        ]
        + [pl.BlockSpec(memory_space=pl.ANY)] * len(weights),
        [
            ("keys", (ext, width), (ext, WIDE), at_tile, jnp.bfloat16),
            ("values", (ext, width), (ext, WIDE), at_tile, jnp.bfloat16),
            ("mixed", (rows, width), (rows, WIDE), at_tile, jnp.bfloat16),
            ("lse", (rows, quads * BLOCK), (rows, BLOCK), at_tile, jnp.float32),
            ("residual", (rows, width), (rows, width), at_start, jnp.float32),
            ("normed_two", (rows, width), (rows, width), at_start, jnp.bfloat16),
        ]
        + fed[0],
        fed[1],
        store,
        slots,
        moment,
        [pltpu.VMEM((rows, width), jnp.float32)] + fed[2],
        cost_of(
            width * rows * ((BLOCK + 2 * HALO) * 8 + width * 2) + fed[3],
            2 * width * width + 20 * rows * width + fed[3] // rows,
        ),
    )


def feed_parts(rows, width, weights):
    hidden = weights[0].shape[1]
    tiles = len(chunks(hidden, wide_tile(hidden)))
    return (
        [(name, (rows, hidden), None, None, jnp.bfloat16) for name in ("gate", "up", "gated")],
        [((rows, width), jnp.bfloat16, whole_spec((rows, width)))],
        [pltpu.VMEM(weight.shape, jnp.bfloat16) for weight in weights]
        + [pltpu.VMEM((rows, hidden), jnp.bfloat16)] * 3
        + [pltpu.SemaphoreType.DMA((6 * tiles,))],
        6 * rows * width * hidden,
    )


def feed(store, slots, moment, scalars, params):
    weights = params[3:]
    rows, width = store["residual"].shape[1:]
    fed = feed_parts(rows, width, weights)
    return slot_call(
        functools.partial(feed_kernel, moment),
        (1,),
        scalars,
        [store["normed_two"], store["residual"], *weights],
        [pl.BlockSpec((None, rows, width), lambda j, s: (moment, 0, 0))] * 2
        + [pl.BlockSpec(memory_space=pl.ANY)] * 3,
        fed[0],
        fed[1],
        store,
        slots,
        moment,
        [pltpu.VMEM((rows, width), jnp.float32)] + fed[2],
        cost_of(fed[3], fed[3] // rows + 10 * rows * width),
    )


def gelu_parts(gate):
    root = 0.7978845608028654
    bend = jnp.tanh(root * (gate + 0.044715 * gate * gate * gate))
    return 0.5 * (1.0 + bend), bend, root


def feed_back_kernel(idx, arrived, own, gate, up, residual, gain, wd, wg, wu, wo, *rest):
    g_out, dg_out, du_out, branch_out, gain_out, res_out, mixed_out, total = rest[-8:]
    step = pl.program_id(0)

    @pl.when(step == 0)
    def _():
        g_out[...] = jnp.where(
            idx[0] == 1, arrived[...].astype(jnp.float32), own[...].astype(jnp.float32)
        ).astype(jnp.bfloat16)

    gate_pre = gate[...].astype(jnp.float32)
    up_pre = up[...].astype(jnp.float32)
    grad_gated = nt_dot(g_out[...], wd[...])
    half, bend, root = gelu_parts(gate_pre)
    slope = half + 0.5 * gate_pre * (1.0 - bend * bend) * root * (
        1.0 + 3.0 * 0.044715 * gate_pre * gate_pre
    )
    grad_gate = (grad_gated * up_pre * slope).astype(jnp.bfloat16)
    grad_up = (grad_gated * gate_pre * half).astype(jnp.bfloat16)
    dg_out[...] = grad_gate
    du_out[...] = grad_up
    part = nt_dot(grad_gate, wg[...]) + nt_dot(grad_up, wu[...])

    @pl.when(step == 0)
    def _():
        total[...] = part

    @pl.when(step > 0)
    def _():
        total[...] += part

    @pl.when(step == pl.num_programs(0) - 1)
    def _():
        grads, grad_gain = norm_back(total[...], residual[...], gain[...].astype(jnp.float32))
        gain_out[...] = jnp.broadcast_to(grad_gain, gain_out.shape)
        grad_residual = g_out[...].astype(jnp.float32) + grads
        res_out[...] = grad_residual
        branch = grad_residual.astype(jnp.bfloat16)
        branch_out[...] = branch
        mixed_out[...] = nt_dot(branch, flat(wo)).astype(jnp.bfloat16)


def norm_back(grads, values, gain):
    scale = inverse_rms(values)
    pulled = grads * gain
    mean = jnp.mean(pulled * values, axis=-1, keepdims=True)
    return (
        scale * pulled - values * (scale * scale * scale * mean),
        jnp.sum(grads * values * scale, axis=0, keepdims=True),
    )


def feed_back(store, slots, moment, scalars, arrived, own, params):
    packed, gain_two, gate_w, up_w, down_w = params[1:]
    rows, width = arrived.shape
    hidden = gate_w.shape[1]
    tile = wide_tile(hidden)
    at_tile = lambda j: (0, j)
    at_start = lambda j: (0, 0)
    taken_tile = pl.BlockSpec((None, rows, tile), lambda j, s: (s[1], 0, j))
    return slot_call(
        feed_back_kernel,
        (hidden // tile,),
        scalars,
        [arrived, own, store["gate"], store["up"], store["residual"], gain_two]
        + [down_w, gate_w, up_w, packed],
        [whole_spec((rows, width)), whole_spec((rows, width)), taken_tile, taken_tile]
        + [pl.BlockSpec((None, rows, width), lambda j, s: (s[1], 0, 0)), whole_spec((1, width))]
        + [pl.BlockSpec((tile, width), lambda j, s: (j, 0))]
        + [pl.BlockSpec((width, tile), lambda j, s: (0, j))] * 2
        + [
            pl.BlockSpec(
                (packed.shape[0], (packed.shape[1] - 16) // 4, width), lambda j, s: (0, 3, 0)
            )
        ],
        [
            ("grad_result", (rows, width), (rows, width), at_start, jnp.bfloat16),
            ("grad_gate", (rows, hidden), (rows, tile), at_tile, jnp.bfloat16),
            ("grad_up", (rows, hidden), (rows, tile), at_tile, jnp.bfloat16),
            ("grad_branch", (rows, width), (rows, width), at_start, jnp.bfloat16),
            ("gain_two", (8, width), (8, width), at_start, jnp.float32),
        ],
        [
            ((rows, width), jnp.float32, whole_spec((rows, width))),
            ((rows, width), jnp.bfloat16, whole_spec((rows, width))),
        ],
        store,
        slots,
        moment,
        [pltpu.VMEM((rows, width), jnp.float32)],
        cost_of(6 * rows * width * hidden + 2 * rows * width * width, 6 * width * hidden),
    )


def attend_back_kernel(idx, q, keys, values, mixed, lse, grad_mixed, bias, *rest):
    q_out, center, top, bottom, k_total, v_total = rest[-6:]
    rows = q.shape[0]
    scale = jnp.bfloat16(HEAD_DIM**-0.5)
    k_total[...] = jnp.zeros_like(k_total)
    v_total[...] = jnp.zeros_like(v_total)
    for start, count in row_blocks(rows):
        span = count + 2 * HALO
        block_bias = bias[pl.ds(start, count), :span]
        both_bias = jnp.concatenate([block_bias, block_bias], 0)
        for pair in range(WIDE // (2 * HEAD_DIM)):
            lanes = slice(pair * 2 * HEAD_DIM, (pair + 1) * 2 * HEAD_DIM)
            q_both = stacked_heads(q[pl.ds(start, count), lanes] * scale)
            g_both = stacked_heads(grad_mixed[pl.ds(start, count), lanes])
            m_pair = mixed[pl.ds(start, count), lanes].astype(jnp.float32)
            k_pair = keys[pl.ds(start, span), lanes]
            log_sum = jnp.concatenate(
                [lse[pl.ds(start, count), 2 * pair + n : 2 * pair + n + 1] for n in range(2)], 0
            )
            probs = jnp.exp(nt_dot(q_both, k_pair) + (both_bias - log_sum))
            grad_probs = nt_dot(g_both, values[pl.ds(start, span), lanes])
            mean = jnp.sum(
                g_both.astype(jnp.float32) * jnp.concatenate([m_pair, m_pair], 0),
                axis=-1,
                keepdims=True,
            )
            grad_scores = (probs * (grad_probs - mean)).astype(jnp.bfloat16)
            q_out[pl.ds(start, count), lanes] = (
                unstacked_heads(dot(grad_scores, k_pair)) * (HEAD_DIM**-0.5)
            ).astype(jnp.bfloat16)
            k_total[pl.ds(start, span), lanes] += tn_dot(grad_scores, q_both)
            v_total[pl.ds(start, span), lanes] += tn_dot(probs.astype(jnp.bfloat16), g_both)
    for place, total in ((0, k_total), (1, v_total)):
        top[place] = total[pl.ds(0, HALO)].astype(jnp.bfloat16)
        center[place] = total[pl.ds(HALO, rows)]
        bottom[place] = total[pl.ds(HALO + rows, HALO)].astype(jnp.bfloat16)


def attend_back(store, slots, moment, scalars, grad_mixed, bias):
    rows, width = grad_mixed.shape
    ext = rows + 2 * HALO
    taken = pl.BlockSpec((None, rows, WIDE), lambda j, s: (s[1], 0, j))
    taken_ext = pl.BlockSpec((None, ext, WIDE), lambda j, s: (s[1], 0, j))
    halo_spec = pl.BlockSpec((2, HALO, WIDE), lambda j, s: (0, 0, j))
    work = width * rows * (BLOCK + 2 * HALO) * 2
    return slot_call(
        attend_back_kernel,
        (width // WIDE,),
        scalars,
        [store["queries"], store["keys"], store["values"], store["mixed"], store["lse"]]
        + [grad_mixed, bias],
        [
            taken,
            taken_ext,
            taken_ext,
            taken,
            pl.BlockSpec((None, rows, BLOCK), lambda j, s: (s[1], 0, j)),
            pl.BlockSpec((rows, WIDE), lambda j, s: (0, j)),
            pl.BlockSpec((None,) + bias.shape[1:], lambda j, s: (s[2], 0, 0)),
        ],
        [("grad_queries", (rows, width), (rows, WIDE), lambda j: (0, j), jnp.bfloat16)],
        [
            (
                (2, rows, width),
                jnp.float32,
                pl.BlockSpec((2, rows, WIDE), lambda j, s: (0, 0, j)),
            ),
            ((2, HALO, width), jnp.bfloat16, halo_spec),
            ((2, HALO, width), jnp.bfloat16, halo_spec),
        ],
        store,
        slots,
        moment,
        [pltpu.VMEM((ext, WIDE), jnp.float32)] * 2,
        cost_of(work * 20, 24 * rows * width),
    )


def project_back_kernel(
    idx, grad_q, center, below, above, source, gain, grad_res, wq, wk, wv, *rest
):
    k_out, v_out, gain_out, in_out, total = rest[-5:]
    step = pl.program_id(0)
    rows = source.shape[0]
    for place, out in ((0, k_out), (1, v_out)):
        head = center[place, pl.ds(0, HALO)] + below[place].astype(jnp.float32)
        tail = center[place, pl.ds(rows - HALO, HALO)] + above[place].astype(jnp.float32)
        out[pl.ds(0, HALO)] = head.astype(jnp.bfloat16)
        out[pl.ds(HALO, rows - 2 * HALO)] = center[place, pl.ds(HALO, rows - 2 * HALO)].astype(
            jnp.bfloat16
        )
        out[pl.ds(rows - HALO, HALO)] = tail.astype(jnp.bfloat16)
    part = nt_dot(grad_q[...], flat(wq))
    part += nt_dot(k_out[...], flat(wk)) + nt_dot(v_out[...], flat(wv))

    @pl.when(step == 0)
    def _():
        total[...] = part

    @pl.when(step > 0)
    def _():
        total[...] += part

    @pl.when(step == pl.num_programs(0) - 1)
    def _():
        grads, grad_gain = norm_back(
            total[...], source[...].astype(jnp.float32), gain[...].astype(jnp.float32)
        )
        gain_out[...] = jnp.broadcast_to(grad_gain, gain_out.shape)
        in_out[...] = (grad_res[...] + grads).astype(jnp.bfloat16)


def project_back(store, slots, moment, scalars, center, below, above, grad_res, params):
    rows, width = grad_res.shape
    gain_one, packed = params[:2]
    at_tile = lambda j: (0, j)
    at_start = lambda j: (0, 0)
    halo_spec = pl.BlockSpec((2, HALO, WIDE), lambda j, s: (0, 0, j))
    return slot_call(
        project_back_kernel,
        (width // WIDE,),
        scalars,
        [store["grad_queries"], center, below, above, store["source"], gain_one, grad_res]
        + [packed] * 3,
        [
            pl.BlockSpec((None, rows, WIDE), lambda j, s: (moment, 0, j)),
            pl.BlockSpec((2, rows, WIDE), lambda j, s: (0, 0, j)),
            halo_spec,
            halo_spec,
            pl.BlockSpec((None, rows, width), lambda j, s: (s[1], 0, 0)),
            whole_spec((1, width)),
            whole_spec((rows, width)),
        ]
        + [packed_spec(packed, number, WIDE) for number in range(3)],
        [
            ("grad_keys", (rows, width), (rows, WIDE), at_tile, jnp.bfloat16),
            ("grad_values", (rows, width), (rows, WIDE), at_tile, jnp.bfloat16),
            ("gain_one", (8, width), (8, width), at_start, jnp.float32),
        ],
        [((rows, width), jnp.bfloat16, whole_spec((rows, width)))],
        store,
        slots,
        moment,
        [pltpu.VMEM((rows, width), jnp.float32)],
        cost_of(6 * rows * width * width, 6 * width * width + 20 * rows * width),
    )


def window_bias(lengths_row, shard_no, rows, seq_len):
    ends = jnp.cumsum(lengths_row)
    first = shard_no * rows
    row = jnp.arange(rows, dtype=jnp.int32)
    place = (row // BLOCK * BLOCK)[:, None] - HALO + jnp.arange(BLOCK + 2 * HALO, dtype=jnp.int32)

    def document(position):
        return jnp.sum((position[..., None] >= ends).astype(jnp.int32), axis=-1)

    key = first + place
    allowed = (
        (jnp.abs(row[:, None] - place) <= RADIUS)
        & (key >= 0)
        & (key < seq_len)
        & (document(first + row)[:, None] == document(key))
    )
    return jnp.where(allowed, 0.0, NEVER).astype(jnp.float32)


def after(cells, *others):
    return lax.optimization_barrier((cells,) + others)[0] if others else cells


class Link:
    def __init__(self, axis, pairs, depth):
        self.axis, self.pairs, self.depth, self.sent = axis, pairs, depth, []

    def __call__(self, cells, depth=None):
        depth = self.depth if depth is None else depth
        if depth and len(self.sent) >= depth:
            cells = after(cells, self.sent[-depth])
        self.sent.append(lax.ppermute(cells, self.axis, self.pairs))
        return self.sent[-1]


def links(depth=2):
    span = lax.axis_size("seq")
    high = span // 2
    across = [(h * 2 + c, ((h + 1) % high) * 2 + c) for h in range(high) for c in range(2)]
    pairs = [(i, i ^ 1) for i in range(span)]
    rings = lax.axis_size("wt")
    along = [(i, (i + 1) % rings) for i in range(rings)]
    return Link("seq", across, depth), Link("seq", pairs, 0), Link("wt", along, 0)


def places():
    high = lax.axis_size("seq") // 2
    shard_no = lax.axis_index("seq")
    return high, shard_no // 2, shard_no % 2


class Gather:
    def __init__(self, shard, lines):
        self.across, self.swap = lines[:2]
        self.level = lax.all_gather(shard, "wt", axis=0)

    def cross(self, *others):
        self.row = [after(self.level, *others)]
        for _ in range(1, lax.axis_size("seq") // 2):
            self.row.append(self.across(self.row[-1]))
        return self

    def pieces(self, *others):
        found = {}
        for j, part in enumerate(self.row):
            part = after(part, *others) if j else part
            found[(None, j, 0)] = part
            found[(None, j, 1)] = self.swap(part)
        return found


def ring_gather(shard, lines, between):
    across, swap, along = lines
    found, current = {}, shard
    for k in range(lax.axis_size("wt")):
        current = along(current) if k else current
        if k == lax.axis_size("wt") - 1:
            between()
        cells = current
        for j in range(lax.axis_size("seq") // 2):
            if j:
                cells = across(cells, 1) if k == lax.axis_size("wt") - 1 else across(cells)
            found[(k, j, 0)] = cells
            found[(k, j, 1)] = swap(cells)
    return found


def assemble_kernel(count, plan, seat_ref, *refs):
    parts, wholes, sems = refs[:count], refs[count:-1], refs[-1]
    copies = []
    for number, (source, start, rows, seat, ring, whole, to) in enumerate(plan):
        there = wholes[whole].at[seat_ref[seat]]
        if ring is None:
            here, there = parts[source].at[:, pl.ds(start, rows)], there.at[:, pl.ds(to, rows)]
        else:
            here = parts[source].at[pl.ds(start, rows)]
            there = there.at[seat_ref[ring], pl.ds(to, rows)]
        copies.append(pltpu.make_async_copy(here, there, sems.at[number]))
    for copy in copies:
        copy.start()
    for copy in copies:
        copy.wait()


def assemble(pieces, pack):
    high, h, c = places()
    rings, z = lax.axis_size("wt"), lax.axis_index("wt")
    seats = [
        lax.rem(h - j + high, high) * 2 + (c + p) % 2 for j in range(high) for p in range(2)
    ] + [lax.rem(z - k + rings, rings) for k in range(rings)]
    sources, plan = [], []
    for (k, j, p), part in pieces.items():
        start = 0
        for whole, rows in enumerate(pack):
            ring = None if k is None else 2 * high + k
            plan.append((len(sources), start, rows, j * 2 + p, ring, whole, 0))
            start += rows
        sources.append(part)
    width, kind = sources[0].shape[-1], sources[0].dtype
    shapes = [(2 * high, rings, rows, width) for rows in pack]
    if any(rows % 16 for rows in pack):
        wholes = [jnp.zeros(shape, kind) for shape in shapes]
        for source, start, rows, seat, ring, whole, to in plan:
            part = sources[source]
            part = part[None] if ring is None else part[None, None]
            part = part[:, :, start : start + rows]
            place = (seats[seat], 0 if ring is None else seats[ring], to, 0)
            wholes[whole] = lax.dynamic_update_slice(wholes[whole], part, place)
    else:
        wholes = pl.pallas_call(
            functools.partial(assemble_kernel, len(sources), plan),
            out_shape=[jax.ShapeDtypeStruct(shape, kind) for shape in shapes],
            grid_spec=pltpu.PrefetchScalarGridSpec(
                num_scalar_prefetch=1,
                grid=(),
                in_specs=[pl.BlockSpec(memory_space=pl.ANY)] * len(sources),
                out_specs=[pl.BlockSpec(memory_space=pltpu.VMEM)] * len(shapes),
                scratch_shapes=[pltpu.SemaphoreType.DMA((len(plan),))],
            ),
            compiler_params=pltpu.CompilerParams(vmem_limit_bytes=40 * 2**20),
            cost_estimate=cost_of(0, 2 * sum(source.size * 2 for source in sources)),
        )(jnp.stack(seats).astype(jnp.int32), *sources)
    return [whole.reshape(-1, width) for whole in wholes]


def plus(left, right, kind):
    return (left.astype(jnp.float32) + right.astype(jnp.float32)).astype(kind)


class Scatter:
    def __init__(self, partial, lines, kind=jnp.bfloat16, along_first=False):
        self.across, self.swap = lines[:2]
        self.kind, self.along_first = kind, along_first
        high, h, c = places()
        self.high, self.h = high, h
        cells = partial.reshape(high, 2, -1, partial.shape[-1])
        self.mine = lax.dynamic_index_in_dim(cells, c, 1, False)
        self.received = self.swap(lax.dynamic_index_in_dim(cells, 1 - c, 1, False))
        if along_first:
            rows = self.mine.shape[1]
            rings = lax.axis_size("wt")
            whole = plus(self.mine, self.received, kind)
            whole = whole.reshape(high, rings, rows // rings, -1).swapaxes(0, 1)
            self.summed = whole.reshape(high * rows, -1)
            summed = lax.psum_scatter(self.summed, "wt", scatter_dimension=0, tiled=True)
            self.mine = summed.reshape(high, rows // rings, -1)
            self.level = None
        else:
            self.level = self.block(1)

    def block(self, j):
        place = lax.rem(self.h - j + self.high, self.high)
        mine = lax.dynamic_index_in_dim(self.mine, place, 0, False)
        if self.along_first:
            return mine
        return plus(mine, lax.dynamic_index_in_dim(self.received, place, 0, False), self.kind)

    def cross(self, *others):
        self.level = self.block(1) if self.level is None else self.level
        self.arrived = self.across(after(self.level, *others))
        return self

    def add(self, *others):
        level = self.arrived
        for j in range(2, self.high + 1):
            level = plus(after(level, *others), self.block(j), self.kind)
            if j < self.high:
                level = self.across(level)
        self.level = level
        return self

    def finish(self):
        level = self.level
        if not self.along_first:
            level = lax.psum_scatter(level, "wt", scatter_dimension=0, tiled=True)
        return level.astype(jnp.float32)


def ring_scatter(partial, lines):
    across, swap, along = lines
    high, h, c = places()
    rings, z = lax.axis_size("wt"), lax.axis_index("wt")
    cells = partial.reshape(high, 2, rings, -1, partial.shape[-1])
    mine = lax.dynamic_index_in_dim(cells, c, 1, False)
    received = swap(lax.dynamic_index_in_dim(cells, 1 - c, 1, False))
    size = (1, 1) + cells.shape[3:]

    def block(j, k):
        place = (lax.rem(h - j + high, high), lax.rem(z - k + rings, rings), 0, 0)
        return plus(
            lax.dynamic_slice(mine, place, size)[0, 0],
            lax.dynamic_slice(received, place, size)[0, 0],
            jnp.bfloat16,
        )

    total = None
    for k in range(1, rings + 1):
        level = block(1, k)
        for j in range(2, high + 1):
            level = plus(across(level), block(j, k), jnp.bfloat16)
        if total is None:
            total = level
        else:
            total = plus(along(total), level, jnp.float32 if k == rings else jnp.bfloat16)
    return total.astype(jnp.float32)


def per_device(
    inputs,
    lengths,
    cotangent,
    gain_attn,
    w_query,
    w_key,
    w_value,
    w_out,
    gain_mlp,
    w_gate,
    w_up,
    w_down,
):
    section_no = lax.axis_index("section")
    shard_no = lax.axis_index("seq")
    micro_count, rows_local, model_width = inputs.shape
    seq_len = rows_local * lax.axis_size("seq")
    is_first = (section_no == 0).astype(jnp.int32)
    slots = micro_count + 1
    bias = jnp.stack(
        [
            window_bias(lengths[number], shard_no, rows_local, seq_len)
            for number in range(micro_count)
        ]
    )

    def choose(of_first, of_second):
        return is_first * of_first + (1 - is_first) * of_second

    rows = w_query.shape[1]
    gains = jnp.pad(
        jnp.concatenate([gain_attn, gain_mlp], 1), ((0, 15), (0, model_width - 2 * rows))
    )
    lines = links()
    narrow = jnp.concatenate([w_query[0], w_key[0], w_value[0], w_out[0], gains], 0)
    gate_gather = Gather(w_gate[0], lines)
    up_gather = Gather(w_up[0], lines)
    down_gather = Gather(w_down[0], lines)
    pieces = ring_gather(narrow, lines, gate_gather.cross)
    (packed,) = assemble(pieces, [narrow.shape[0]])
    packed = packed.reshape(-1, narrow.shape[0], model_width)
    gain_rows = packed[:, 4 * rows]
    gain_one = gain_rows[:, :rows].reshape(1, -1)
    gain_two = gain_rows[:, rows : 2 * rows].reshape(1, -1)
    params = (gain_one, packed, gain_two)

    store, results, grad_sources = {}, [], []
    arrived = jnp.zeros((rows_local, model_width), jnp.bfloat16)
    for moment in range(slots):
        early, late = min(moment, micro_count - 1), max(moment - 1, 0)
        scalars = jnp.stack([is_first, is_first * 0 + moment, choose(early, late)])
        kv, tail, head = project(store, slots, moment, scalars, inputs[early], arrived, params)
        low = shifted(tail, "seq", 1)
        high = shifted(head, "seq", -1)
        if moment == 0:
            up_gather.cross()
            down_gather.cross(low, high)
            kv = after(kv, up_gather.row[-1])
            attend(store, slots, moment, scalars, kv, low, high, bias, params)
            two = store["normed_two"]
            (gate_w,) = assemble(gate_gather.pieces(kv), [rows])
            (up_w,) = assemble(up_gather.pieces(kv), [rows])
            (down_w,) = assemble(down_gather.pieces(two, gate_w, up_w), [w_down.shape[1]])
            params = params + (gate_w, up_w, down_w)
            (result,) = feed(store, slots, moment, scalars, params)
        else:
            (result,) = attend(store, slots, moment, scalars, kv, low, high, bias, params)
        results.append(result)
        if moment < micro_count:
            arrived = shifted(result, "section", 1)
    activations = jnp.stack(
        [
            jnp.where(is_first == 1, results[number], results[number + 1])
            for number in range(micro_count)
        ]
    )[None]

    def both(name, start):
        chosen = lax.dynamic_slice_in_dim(store[name], start, micro_count, 0)
        return chosen.reshape(-1, chosen.shape[-1])

    def product(left, *right):
        left = both(left, 1 - is_first)
        right = jnp.concatenate([both(name, is_first) for name in right], 1)
        return jnp.dot(left.T, right, preferred_element_type=jnp.float32).astype(jnp.bfloat16)

    arrived_grad = jnp.zeros((rows_local, model_width), jnp.bfloat16)
    for moment in range(slots):
        early, late = min(moment, micro_count - 1), max(moment - 1, 0)
        scalars = jnp.stack(
            [is_first, choose(late, min(moment + 1, micro_count)), choose(late, early)]
        )
        grad_res, grad_mixed = feed_back(
            store, slots, moment, scalars, arrived_grad, cotangent[early], params
        )
        if moment == micro_count:
            lines = links()
            out_part = product("mixed", "grad_branch")
            out_sum = Scatter(out_part, lines, along_first=True)
            gate_sum = Scatter(after(product("normed_two", "grad_gate"), out_part), lines)
            up_sum = Scatter(after(product("normed_two", "grad_up"), out_sum.summed), lines)
            gate_sum.cross(out_sum.summed)
            down_part = product("gated", "grad_result")
            grad_mixed = after(grad_mixed, down_part, up_sum.level)
            down_sum = Scatter(down_part, lines)
        center, top, bottom = attend_back(store, slots, moment, scalars, grad_mixed, bias)
        above = shifted(top, "seq", -1)
        below = shifted(bottom, "seq", 1)
        if moment == micro_count:
            up_sum.cross(above, below)
            gate_sum.add(center)
            center = after(center, gate_sum.level, down_sum.level)
        (grad_source,) = project_back(
            store, slots, moment, scalars, center, below, above, grad_res, params
        )
        grad_sources.append(grad_source)
        if moment < micro_count:
            arrived_grad = shifted(grad_source, "section", -1)
    input_grads = jnp.stack(
        [
            jnp.where(is_first == 1, grad_sources[number + 1], grad_sources[number])
            for number in range(micro_count)
        ]
    )[None]
    down_sum.cross(above, below)
    up_sum.add(grad_source)
    gain_rows = jnp.concatenate(
        [
            jnp.sum(lax.dynamic_slice_in_dim(store[name], is_first, micro_count, 0), 0)
            for name in ("gain_one", "gain_two")
        ]
    ).astype(jnp.bfloat16)
    picked = jnp.arange(2 * 8)[:, None] == jnp.arange(BLOCK)[None] * 8
    right = jnp.concatenate(
        [both(name, is_first) for name in ("grad_queries", "grad_keys", "grad_values")], 1
    )
    right = jnp.concatenate(
        [
            jnp.pad(right, ((0, 0), (0, BLOCK))),
            jnp.pad(picked.astype(jnp.bfloat16), ((0, 0), (right.shape[1], 0))),
        ]
    )
    left = after(jnp.concatenate([both("normed", 1 - is_first), gain_rows]), up_sum.level)
    qkv_part = jnp.dot(left.T, right, preferred_element_type=jnp.float32).astype(jnp.bfloat16)
    grad_up_w = up_sum.finish()
    down_sum.add(qkv_part, grad_up_w)
    qkv_all = ring_scatter(qkv_part, lines)
    grad_out_w = out_sum.cross().add().finish()
    grad_gate_w, grad_down_w = gate_sum.finish(), down_sum.finish()
    grad_query_w, grad_key_w, grad_value_w, gain_sum = (
        qkv_all[:, number * model_width : (number + 1) * model_width] for number in range(4)
    )
    return (
        activations,
        input_grads,
        gain_sum[:, 0][None],
        grad_query_w[None],
        grad_key_w[None],
        grad_value_w[None],
        grad_out_w[None],
        gain_sum[:, 1][None],
        grad_gate_w[None],
        grad_up_w[None],
        grad_down_w[None],
    )


def solution(mesh):
    placed = (
        P("wt", "seq", None),
        P("wt", None),
        P("wt", "seq", None),
        P("section", ("seq", "wt")),
        P("section", ("seq", "wt"), None),
        P("section", ("seq", "wt"), None),
        P("section", ("seq", "wt"), None),
        P("section", ("seq", "wt"), None),
        P("section", ("seq", "wt")),
        P("section", ("seq", "wt"), None),
        P("section", ("seq", "wt"), None),
        P("section", ("seq", "wt"), None),
    )
    return jax.shard_map(
        per_device,
        mesh=mesh,
        in_specs=placed,
        out_specs=(
            P("section", "wt", "seq", None),
            P("section", "wt", "seq", None),
            P("section", ("seq", "wt")),
            P("section", ("seq", "wt"), None),
            P("section", ("seq", "wt"), None),
            P("section", ("seq", "wt"), None),
            P("section", ("seq", "wt"), None),
            P("section", ("seq", "wt")),
            P("section", ("seq", "wt"), None),
            P("section", ("seq", "wt"), None),
            P("section", ("seq", "wt"), None),
        ),
        check_vma=False,
    )
```

```python
import functools

import jax
import jax.numpy as jnp
from jax import lax
from jax.experimental import pallas as pl
from jax.experimental.pallas import tpu as pltpu
from jax.sharding import PartitionSpec as P

HEAD_DIM = 64
RADIUS = 127


EPSILON = 1e-06


def shifted(shard, axis, by):
    length = lax.axis_size(axis)
    pairs = [(i, i + by) for i in range(length) if 0 <= i + by < length]
    return lax.ppermute(shard, axis, pairs)


HALO = 128
BLOCK = 128
WIDE = 256
NEVER = -1e30


def call(kernel, grid, scalars, ins, in_specs, outs, out_specs, scratch=(), aliases=None, cost=None):
    return pl.pallas_call(
        kernel,
        out_shape=outs,
        grid_spec=pltpu.PrefetchScalarGridSpec(
            num_scalar_prefetch=1,
            grid=grid,
            in_specs=in_specs,
            out_specs=out_specs,
            scratch_shapes=list(scratch),
        ),
        input_output_aliases=aliases or {},
        compiler_params=pltpu.CompilerParams(
            vmem_limit_bytes=56 * 2**20, dimension_semantics=("arbitrary",) * len(grid)
        ),
        cost_estimate=cost,
    )(scalars, *ins)


def cost_of(flops, moved, transcendentals=0):
    return pl.CostEstimate(
        flops=int(flops), bytes_accessed=int(moved), transcendentals=int(transcendentals)
    )


def nt_dot(left, right):
    return lax.dot_general(
        left, right, (((1,), (1,)), ((), ())), preferred_element_type=jnp.float32
    )


def tn_dot(left, right):
    return lax.dot_general(
        left, right, (((0,), (0,)), ((), ())), preferred_element_type=jnp.float32
    )


def dot(left, right):
    return jnp.dot(left, right, preferred_element_type=jnp.float32)


def inverse_rms(values):
    return lax.rsqrt(jnp.mean(values * values, axis=-1, keepdims=True) + EPSILON)


def flat(ref):
    cells = ref[...]
    return cells.reshape(-1, cells.shape[-1])


def packed_spec(packed, number, tile):
    rows = (packed.shape[1] - 16) // 4
    return pl.BlockSpec((packed.shape[0], rows, tile), lambda j, s: (0, number, j))


def project_kernel(idx, own, arrived, gain, wq, wk, wv, *rest):
    x_out, n_out, q_out, kv_out, tail_out, head_out = rest[-6:]

    @pl.when(pl.program_id(0) == 0)
    def _():
        picked = jnp.where(
            idx[0] == 1, own[...].astype(jnp.float32), arrived[...].astype(jnp.float32)
        )
        x_out[...] = picked.astype(jnp.bfloat16)
        n_out[...] = (picked * inverse_rms(picked) * gain[...].astype(jnp.float32)).astype(
            jnp.bfloat16
        )

    normed = n_out[...]
    kv_out[0] = dot(normed, flat(wk)).astype(jnp.bfloat16)
    kv_out[1] = dot(normed, flat(wv)).astype(jnp.bfloat16)
    q_out[...] = dot(normed, flat(wq)).astype(jnp.bfloat16)
    tail_out[...] = kv_out[:, pl.ds(kv_out.shape[1] - HALO, HALO)]
    head_out[...] = kv_out[:, pl.ds(0, HALO)]


def slot_call(kernel, grid, scalars, ins, in_specs, kept, fresh, store, slots, moment, scratch=(), cost=None):
    aliases, extra = {}, []
    outs, out_specs = [], []
    for name, shape, block, index, kind in kept:
        outs.append(jax.ShapeDtypeStruct((slots,) + shape, kind))
        if block is None:
            out_specs.append(pl.BlockSpec(memory_space=pl.ANY))
        else:
            out_specs.append(
                pl.BlockSpec((None,) + block, lambda j, s, index=index: (moment,) + index(j))
            )
        if name in store:
            aliases[1 + len(ins) + len(extra)] = len(outs) - 1
            extra.append(store[name])
    for shape, kind, spec in fresh:
        outs.append(jax.ShapeDtypeStruct(shape, kind))
        out_specs.append(spec)
    results = call(
        kernel,
        grid,
        scalars,
        list(ins) + extra,
        list(in_specs) + [pl.BlockSpec(memory_space=pl.ANY)] * len(extra),
        outs,
        out_specs,
        scratch,
        aliases,
        cost,
    )
    for (name, *_), value in zip(kept, results):
        store[name] = value
    return results[len(kept) :]


def whole_spec(shape):
    return pl.BlockSpec(shape, lambda j, s: (0,) * len(shape))


def project(store, slots, moment, scalars, own, arrived, params):
    rows, width = arrived.shape
    gain_one, packed = params[:2]
    tile = WIDE
    at_start = lambda j: (0, 0)
    halo_spec = pl.BlockSpec((2, HALO, tile), lambda j, s: (0, 0, j))
    return slot_call(
        project_kernel,
        (width // tile,),
        scalars,
        [own, arrived, gain_one, packed, packed, packed],
        [whole_spec((rows, width)), whole_spec((rows, width)), whole_spec((1, width))]
        + [packed_spec(packed, number, tile) for number in range(3)],
        [
            ("source", (rows, width), (rows, width), at_start, jnp.bfloat16),
            ("normed", (rows, width), (rows, width), at_start, jnp.bfloat16),
            ("queries", (rows, width), (rows, tile), lambda j: (0, j), jnp.bfloat16),
        ],
        [
            (
                (2, rows, width),
                jnp.bfloat16,
                pl.BlockSpec((2, rows, tile), lambda j, s: (0, 0, j)),
            ),
            ((2, HALO, width), jnp.bfloat16, halo_spec),
            ((2, HALO, width), jnp.bfloat16, halo_spec),
        ],
        store,
        slots,
        moment,
        cost=cost_of(6 * rows * width * width, 6 * width * width + 14 * rows * width),
    )


def row_blocks(rows):
    return [(start, min(BLOCK, rows - start)) for start in range(0, rows, BLOCK)]


def head_masks(kind):
    lane = lax.broadcasted_iota(jnp.int32, (1, 2 * HEAD_DIM), 1)
    low = (lane < HEAD_DIM).astype(kind)
    return (low, (1 - low).astype(kind))


def wide_tile(size):
    return max(tile for tile in range(128, 1409, 128) if size % tile == 0)


def chunks(size, tile):
    return [(start, min(tile, size - start)) for start in range(0, size, tile)]


def stacked_heads(pair):
    return jnp.concatenate([pair * mask for mask in head_masks(pair.dtype)], 0)


def unstacked_heads(stacked):
    rows = stacked.shape[0] // 2
    low = lax.broadcasted_iota(jnp.int32, (1, 2 * HEAD_DIM), 1) < HEAD_DIM
    return jnp.where(low, stacked[:rows], stacked[rows:])


def attend_step(q, kv, low, high, bias, wo, k_out, v_out, mixed_out, lse_out):
    rows = q.shape[0]
    for place, out in ((0, k_out), (1, v_out)):
        out[pl.ds(0, HALO)] = low[place]
        out[pl.ds(HALO, rows)] = kv[place]
        out[pl.ds(HALO + rows, HALO)] = high[place]
    scale = jnp.bfloat16(HEAD_DIM**-0.5)
    tiles = [
        (start, count, pair)
        for start, count in row_blocks(rows)
        for pair in range(WIDE // (2 * HEAD_DIM))
    ]
    sums = {}
    scores, powers, totals = {}, {}, {}
    for start, count, pair in tiles:
        span = count + 2 * HALO
        lanes = slice(pair * 2 * HEAD_DIM, (pair + 1) * 2 * HEAD_DIM)
        q_both = stacked_heads(q[pl.ds(start, count), lanes] * scale)
        block_bias = bias[pl.ds(start, count), :span]
        scores[start, pair] = nt_dot(
            q_both, k_out[pl.ds(start, span), lanes]
        ) + jnp.concatenate([block_bias, block_bias], 0)
    for start, count, pair in tiles:
        value = scores[start, pair]
        most = jnp.max(value, axis=-1, keepdims=True)
        power = jnp.exp(value - most)
        powers[start, pair] = power.astype(jnp.bfloat16)
        totals[start, pair] = jnp.sum(power, axis=-1, keepdims=True)
        log_sum = most + jnp.log(totals[start, pair])
        sums[start, pair] = (log_sum[:count], log_sum[count:])
    for start, count, pair in tiles:
        span = count + 2 * HALO
        lanes = slice(pair * 2 * HEAD_DIM, (pair + 1) * 2 * HEAD_DIM)
        mixed = dot(powers[start, pair], v_out[pl.ds(start, span), lanes])
        mixed = mixed * (1.0 / totals[start, pair])
        mixed_out[pl.ds(start, count), lanes] = unstacked_heads(mixed).astype(jnp.bfloat16)
    for start, count in row_blocks(rows):
        lane = lax.broadcasted_iota(jnp.int32, (count, 2 * HEAD_DIM), 1)
        wide = jnp.zeros((count, 2 * HEAD_DIM), jnp.float32)
        for pair in range(WIDE // (2 * HEAD_DIM)):
            for number, value in enumerate(sums[start, pair]):
                wide = jnp.where(lane == 2 * pair + number, value, wide)
        lse_out[pl.ds(start, count)] = wide
    return dot(mixed_out[...], flat(wo))


def attend_steps(parts, source, gain, res_out, two_out, total, steps):
    step = pl.program_id(0)

    @pl.when(step < steps)
    def _():
        part = attend_step(*parts)

        @pl.when(step == 0)
        def _():
            total[...] = source[...].astype(jnp.float32) + part

        @pl.when(step > 0)
        def _():
            total[...] += part

        @pl.when(step == steps - 1)
        def _():
            residual = total[...]
            res_out[...] = residual
            two_out[...] = (
                residual * inverse_rms(residual) * gain[...].astype(jnp.float32)
            ).astype(jnp.bfloat16)


def attend_kernel(steps, idx, q, kv, low, high, bias, wo, source, gain, *rest):
    k_out, v_out, mixed_out, lse_out, res_out, two_out, total = rest[-7:]
    parts = (q, kv, low, high, bias, wo, k_out, v_out, mixed_out, lse_out)
    attend_steps(parts, source, gain, res_out, two_out, total, steps)


class Feed:
    def __init__(self, moment, weights, outs, held, sems):
        self.moment, self.weights, self.outs, self.held, self.sems = (
            moment,
            weights,
            outs,
            held,
            sems,
        )
        size = weights[0].shape[1]
        self.tiles = chunks(size, wide_tile(size))

    def fetch(self, number, part):
        start, size = self.tiles[number]
        place = (slice(None), pl.ds(start, size)) if part < 2 else (pl.ds(start, size),)
        return pltpu.make_async_copy(
            self.weights[part].at[place], self.held[part].at[place], self.sems.at[3 * number + part]
        )

    def start(self):
        for number in range(len(self.tiles)):
            for part in range(3):
                self.fetch(number, part).start()

    def run(self, normed, total, result):
        gate_w, up_w, down_w = self.held[:3]
        stores = []
        for number, (start, size) in enumerate(self.tiles):
            lanes = slice(start, start + size)
            self.fetch(number, 0).wait()
            gate = dot(normed, gate_w[:, lanes])
            self.fetch(number, 1).wait()
            up = dot(normed, up_w[:, lanes])
            half, _, _ = gelu_parts(gate)
            gated = (gate * half * up).astype(jnp.bfloat16)
            values = (gate.astype(jnp.bfloat16), up.astype(jnp.bfloat16), gated)
            for part, value in enumerate(values):
                held = self.held[3 + part]
                held[:, lanes] = value
                copy = pltpu.make_async_copy(
                    held.at[:, pl.ds(start, size)],
                    self.outs[part].at[self.moment, :, pl.ds(start, size)],
                    self.sems.at[3 * len(self.tiles) + 3 * number + part],
                )
                copy.start()
                stores.append(copy)
            self.fetch(number, 2).wait()
            total[...] += dot(gated, down_w[lanes])
        result[...] = total[...].astype(jnp.bfloat16)
        for copy in stores:
            copy.wait()


def feed_kernel(moment, idx, two, residual, wg, wu, wd, *rest):
    outs, result, total, held, sems = rest[-12:-9], rest[-9], rest[-8], rest[-7:-1], rest[-1]
    feed = Feed(moment, (wg, wu, wd), outs, held, sems)
    feed.start()
    total[...] = residual[...]
    feed.run(two[...], total, result)


def attend_feed_kernel(
    moment, steps, idx, q, kv, low, high, bias, wo, source, gain, wg, wu, wd, *rest
):
    k_out, v_out, mixed_out, lse_out, res_out, two_out = rest[-18:-12]
    outs, result, total, held, sems = rest[-12:-9], rest[-9], rest[-8], rest[-7:-1], rest[-1]
    feed = Feed(moment, (wg, wu, wd), outs, held, sems)
    pl.when(pl.program_id(0) == 0)(feed.start)
    parts = (q, kv, low, high, bias, wo, k_out, v_out, mixed_out, lse_out)
    attend_steps(parts, source, gain, res_out, two_out, total, steps)

    @pl.when(pl.program_id(0) == steps)
    def _():
        feed.run(two_out[...], total, result)


def attend(store, slots, moment, scalars, kv, low, high, bias, params):
    rows, width = kv.shape[1:]
    packed, gain_two = params[1:3]
    weights = params[3:]
    shard = (packed.shape[1] - 16) // 4
    ext = rows + 2 * HALO
    quads = width // WIDE
    last = lambda j: jnp.minimum(j, quads - 1)
    at_start = lambda j: (0, 0)
    at_tile = lambda j: (0, last(j))
    halo_spec = pl.BlockSpec((2, HALO, WIDE), lambda j, s: (0, 0, last(j)))
    fed = feed_parts(rows, width, weights) if weights else ([], [], [], 0)
    kernel = functools.partial(attend_feed_kernel, moment) if weights else attend_kernel
    return slot_call(
        functools.partial(kernel, quads),
        (quads + (1 if weights else 0),),
        scalars,
        [store["queries"], kv, low, high, bias, packed, store["source"], gain_two, *weights],
        [
            pl.BlockSpec((None, rows, WIDE), lambda j, s: (moment, 0, last(j))),
            pl.BlockSpec((2, rows, WIDE), lambda j, s: (0, 0, last(j))),
            halo_spec,
            halo_spec,
            pl.BlockSpec((None,) + bias.shape[1:], lambda j, s: (s[2], 0, 0)),
            pl.BlockSpec((WIDE // shard, shard, width), lambda j, s: (last(j), 3, 0)),
            pl.BlockSpec((None, rows, width), lambda j, s: (moment, 0, 0)),
            whole_spec((1, width)),
        ]
        + [pl.BlockSpec(memory_space=pl.ANY)] * len(weights),
        [
            ("keys", (ext, width), (ext, WIDE), at_tile, jnp.bfloat16),
            ("values", (ext, width), (ext, WIDE), at_tile, jnp.bfloat16),
            ("mixed", (rows, width), (rows, WIDE), at_tile, jnp.bfloat16),
            ("lse", (rows, quads * BLOCK), (rows, BLOCK), at_tile, jnp.float32),
            ("residual", (rows, width), (rows, width), at_start, jnp.float32),
            ("normed_two", (rows, width), (rows, width), at_start, jnp.bfloat16),
        ]
        + fed[0],
        fed[1],
        store,
        slots,
        moment,
        [pltpu.VMEM((rows, width), jnp.float32)] + fed[2],
        cost_of(
            width * rows * ((BLOCK + 2 * HALO) * 8 + width * 2) + fed[3],
            2 * width * width + 20 * rows * width + fed[3] // rows,
        ),
    )


def feed_parts(rows, width, weights):
    hidden = weights[0].shape[1]
    tiles = len(chunks(hidden, wide_tile(hidden)))
    return (
        [(name, (rows, hidden), None, None, jnp.bfloat16) for name in ("gate", "up", "gated")],
        [((rows, width), jnp.bfloat16, whole_spec((rows, width)))],
        [pltpu.VMEM(weight.shape, jnp.bfloat16) for weight in weights]
        + [pltpu.VMEM((rows, hidden), jnp.bfloat16)] * 3
        + [pltpu.SemaphoreType.DMA((6 * tiles,))],
        6 * rows * width * hidden,
    )


def feed(store, slots, moment, scalars, params):
    weights = params[3:]
    rows, width = store["residual"].shape[1:]
    fed = feed_parts(rows, width, weights)
    return slot_call(
        functools.partial(feed_kernel, moment),
        (1,),
        scalars,
        [store["normed_two"], store["residual"], *weights],
        [pl.BlockSpec((None, rows, width), lambda j, s: (moment, 0, 0))] * 2
        + [pl.BlockSpec(memory_space=pl.ANY)] * 3,
        fed[0],
        fed[1],
        store,
        slots,
        moment,
        [pltpu.VMEM((rows, width), jnp.float32)] + fed[2],
        cost_of(fed[3], fed[3] // rows + 10 * rows * width),
    )


def gelu_parts(gate):
    root = 0.7978845608028654
    bend = jnp.tanh(root * (gate + 0.044715 * gate * gate * gate))
    return 0.5 * (1.0 + bend), bend, root


def feed_back_kernel(idx, arrived, own, gate, up, residual, gain, wd, wg, wu, wo, *rest):
    g_out, dg_out, du_out, branch_out, gain_out, res_out, mixed_out, total = rest[-8:]
    step = pl.program_id(0)

    @pl.when(step == 0)
    def _():
        g_out[...] = jnp.where(
            idx[0] == 1, arrived[...].astype(jnp.float32), own[...].astype(jnp.float32)
        ).astype(jnp.bfloat16)

    gate_pre = gate[...].astype(jnp.float32)
    up_pre = up[...].astype(jnp.float32)
    grad_gated = nt_dot(g_out[...], wd[...])
    half, bend, root = gelu_parts(gate_pre)
    slope = half + 0.5 * gate_pre * (1.0 - bend * bend) * root * (
        1.0 + 3.0 * 0.044715 * gate_pre * gate_pre
    )
    grad_gate = (grad_gated * up_pre * slope).astype(jnp.bfloat16)
    grad_up = (grad_gated * gate_pre * half).astype(jnp.bfloat16)
    dg_out[...] = grad_gate
    du_out[...] = grad_up
    part = nt_dot(grad_gate, wg[...]) + nt_dot(grad_up, wu[...])

    @pl.when(step == 0)
    def _():
        total[...] = part

    @pl.when(step > 0)
    def _():
        total[...] += part

    @pl.when(step == pl.num_programs(0) - 1)
    def _():
        grads, grad_gain = norm_back(total[...], residual[...], gain[...].astype(jnp.float32))
        gain_out[...] = jnp.broadcast_to(grad_gain, gain_out.shape)
        grad_residual = g_out[...].astype(jnp.float32) + grads
        res_out[...] = grad_residual
        branch = grad_residual.astype(jnp.bfloat16)
        branch_out[...] = branch
        mixed_out[...] = nt_dot(branch, flat(wo)).astype(jnp.bfloat16)


def norm_back(grads, values, gain):
    scale = inverse_rms(values)
    pulled = grads * gain
    mean = jnp.mean(pulled * values, axis=-1, keepdims=True)
    return (
        scale * pulled - values * (scale * scale * scale * mean),
        jnp.sum(grads * values * scale, axis=0, keepdims=True),
    )


def feed_back(store, slots, moment, scalars, arrived, own, params):
    packed, gain_two, gate_w, up_w, down_w = params[1:]
    rows, width = arrived.shape
    hidden = gate_w.shape[1]
    tile = wide_tile(hidden)
    at_tile = lambda j: (0, j)
    at_start = lambda j: (0, 0)
    taken_tile = pl.BlockSpec((None, rows, tile), lambda j, s: (s[1], 0, j))
    return slot_call(
        feed_back_kernel,
        (hidden // tile,),
        scalars,
        [arrived, own, store["gate"], store["up"], store["residual"], gain_two]
        + [down_w, gate_w, up_w, packed],
        [whole_spec((rows, width)), whole_spec((rows, width)), taken_tile, taken_tile]
        + [pl.BlockSpec((None, rows, width), lambda j, s: (s[1], 0, 0)), whole_spec((1, width))]
        + [pl.BlockSpec((tile, width), lambda j, s: (j, 0))]
        + [pl.BlockSpec((width, tile), lambda j, s: (0, j))] * 2
        + [
            pl.BlockSpec(
                (packed.shape[0], (packed.shape[1] - 16) // 4, width), lambda j, s: (0, 3, 0)
            )
        ],
        [
            ("grad_result", (rows, width), (rows, width), at_start, jnp.bfloat16),
            ("grad_gate", (rows, hidden), (rows, tile), at_tile, jnp.bfloat16),
            ("grad_up", (rows, hidden), (rows, tile), at_tile, jnp.bfloat16),
            ("grad_branch", (rows, width), (rows, width), at_start, jnp.bfloat16),
            ("gain_two", (8, width), (8, width), at_start, jnp.float32),
        ],
        [
            ((rows, width), jnp.float32, whole_spec((rows, width))),
            ((rows, width), jnp.bfloat16, whole_spec((rows, width))),
        ],
        store,
        slots,
        moment,
        [pltpu.VMEM((rows, width), jnp.float32)],
        cost_of(6 * rows * width * hidden + 2 * rows * width * width, 6 * width * hidden),
    )


def attend_back_kernel(idx, q, keys, values, mixed, lse, grad_mixed, bias, *rest):
    q_out, center, top, bottom, k_total, v_total = rest[-6:]
    rows = q.shape[0]
    scale = jnp.bfloat16(HEAD_DIM**-0.5)
    k_total[...] = jnp.zeros_like(k_total)
    v_total[...] = jnp.zeros_like(v_total)
    tiles = [
        (start, count, slice(pair * 2 * HEAD_DIM, (pair + 1) * 2 * HEAD_DIM), pair)
        for start, count in row_blocks(rows)
        for pair in range(WIDE // (2 * HEAD_DIM))
    ]
    held = {}
    for start, count, lanes, pair in tiles:
        span = count + 2 * HALO
        q_both = stacked_heads(q[pl.ds(start, count), lanes] * scale)
        g_both = stacked_heads(grad_mixed[pl.ds(start, count), lanes])
        scores = nt_dot(q_both, keys[pl.ds(start, span), lanes])
        grad_probs = nt_dot(g_both, values[pl.ds(start, span), lanes])
        held[start, pair] = (q_both, g_both, scores, grad_probs)
    for start, count, lanes, pair in tiles:
        span = count + 2 * HALO
        q_both, g_both, scores, grad_probs = held[start, pair]
        block_bias = bias[pl.ds(start, count), :span]
        both_bias = jnp.concatenate([block_bias, block_bias], 0)
        m_pair = mixed[pl.ds(start, count), lanes].astype(jnp.float32)
        log_sum = jnp.concatenate(
            [lse[pl.ds(start, count), 2 * pair + n : 2 * pair + n + 1] for n in range(2)], 0
        )
        probs = jnp.exp(scores + (both_bias - log_sum))
        mean = jnp.sum(
            g_both.astype(jnp.float32) * jnp.concatenate([m_pair, m_pair], 0),
            axis=-1,
            keepdims=True,
        )
        grad_scores = (probs * (grad_probs - mean)).astype(jnp.bfloat16)
        held[start, pair] = (q_both, g_both, probs.astype(jnp.bfloat16), grad_scores)
    for start, count, lanes, pair in tiles:
        span = count + 2 * HALO
        q_both, g_both, probs, grad_scores = held[start, pair]
        grad_q = dot(grad_scores, keys[pl.ds(start, span), lanes])
        q_out[pl.ds(start, count), lanes] = (
            unstacked_heads(grad_q) * (HEAD_DIM**-0.5)
        ).astype(jnp.bfloat16)
        k_total[pl.ds(start, span), lanes] += tn_dot(grad_scores, q_both)
        v_total[pl.ds(start, span), lanes] += tn_dot(probs, g_both)
    for place, total in ((0, k_total), (1, v_total)):
        top[place] = total[pl.ds(0, HALO)].astype(jnp.bfloat16)
        center[place] = total[pl.ds(HALO, rows)]
        bottom[place] = total[pl.ds(HALO + rows, HALO)].astype(jnp.bfloat16)


def attend_back(store, slots, moment, scalars, grad_mixed, bias):
    rows, width = grad_mixed.shape
    ext = rows + 2 * HALO
    taken = pl.BlockSpec((None, rows, WIDE), lambda j, s: (s[1], 0, j))
    taken_ext = pl.BlockSpec((None, ext, WIDE), lambda j, s: (s[1], 0, j))
    halo_spec = pl.BlockSpec((2, HALO, WIDE), lambda j, s: (0, 0, j))
    work = width * rows * (BLOCK + 2 * HALO) * 2
    return slot_call(
        attend_back_kernel,
        (width // WIDE,),
        scalars,
        [store["queries"], store["keys"], store["values"], store["mixed"], store["lse"]]
        + [grad_mixed, bias],
        [
            taken,
            taken_ext,
            taken_ext,
            taken,
            pl.BlockSpec((None, rows, BLOCK), lambda j, s: (s[1], 0, j)),
            pl.BlockSpec((rows, WIDE), lambda j, s: (0, j)),
            pl.BlockSpec((None,) + bias.shape[1:], lambda j, s: (s[2], 0, 0)),
        ],
        [("grad_queries", (rows, width), (rows, WIDE), lambda j: (0, j), jnp.bfloat16)],
        [
            (
                (2, rows, width),
                jnp.float32,
                pl.BlockSpec((2, rows, WIDE), lambda j, s: (0, 0, j)),
            ),
            ((2, HALO, width), jnp.bfloat16, halo_spec),
            ((2, HALO, width), jnp.bfloat16, halo_spec),
        ],
        store,
        slots,
        moment,
        [pltpu.VMEM((ext, WIDE), jnp.float32)] * 2,
        cost_of(work * 20, 24 * rows * width),
    )


def project_back_kernel(
    idx, grad_q, center, below, above, source, gain, grad_res, wq, wk, wv, *rest
):
    k_out, v_out, gain_out, in_out, total = rest[-5:]
    step = pl.program_id(0)
    rows = source.shape[0]
    for place, out in ((0, k_out), (1, v_out)):
        head = center[place, pl.ds(0, HALO)] + below[place].astype(jnp.float32)
        tail = center[place, pl.ds(rows - HALO, HALO)] + above[place].astype(jnp.float32)
        out[pl.ds(0, HALO)] = head.astype(jnp.bfloat16)
        out[pl.ds(HALO, rows - 2 * HALO)] = center[place, pl.ds(HALO, rows - 2 * HALO)].astype(
            jnp.bfloat16
        )
        out[pl.ds(rows - HALO, HALO)] = tail.astype(jnp.bfloat16)
    part = nt_dot(grad_q[...], flat(wq))
    part += nt_dot(k_out[...], flat(wk)) + nt_dot(v_out[...], flat(wv))

    @pl.when(step == 0)
    def _():
        total[...] = part

    @pl.when(step > 0)
    def _():
        total[...] += part

    @pl.when(step == pl.num_programs(0) - 1)
    def _():
        grads, grad_gain = norm_back(
            total[...], source[...].astype(jnp.float32), gain[...].astype(jnp.float32)
        )
        gain_out[...] = jnp.broadcast_to(grad_gain, gain_out.shape)
        in_out[...] = (grad_res[...] + grads).astype(jnp.bfloat16)


def project_back(store, slots, moment, scalars, center, below, above, grad_res, params):
    rows, width = grad_res.shape
    gain_one, packed = params[:2]
    at_tile = lambda j: (0, j)
    at_start = lambda j: (0, 0)
    halo_spec = pl.BlockSpec((2, HALO, WIDE), lambda j, s: (0, 0, j))
    return slot_call(
        project_back_kernel,
        (width // WIDE,),
        scalars,
        [store["grad_queries"], center, below, above, store["source"], gain_one, grad_res]
        + [packed] * 3,
        [
            pl.BlockSpec((None, rows, WIDE), lambda j, s: (moment, 0, j)),
            pl.BlockSpec((2, rows, WIDE), lambda j, s: (0, 0, j)),
            halo_spec,
            halo_spec,
            pl.BlockSpec((None, rows, width), lambda j, s: (s[1], 0, 0)),
            whole_spec((1, width)),
            whole_spec((rows, width)),
        ]
        + [packed_spec(packed, number, WIDE) for number in range(3)],
        [
            ("grad_keys", (rows, width), (rows, WIDE), at_tile, jnp.bfloat16),
            ("grad_values", (rows, width), (rows, WIDE), at_tile, jnp.bfloat16),
            ("gain_one", (8, width), (8, width), at_start, jnp.float32),
        ],
        [((rows, width), jnp.bfloat16, whole_spec((rows, width)))],
        store,
        slots,
        moment,
        [pltpu.VMEM((rows, width), jnp.float32)],
        cost_of(6 * rows * width * width, 6 * width * width + 20 * rows * width),
    )


def window_bias(lengths_row, shard_no, rows, seq_len):
    ends = jnp.cumsum(lengths_row)
    first = shard_no * rows
    row = jnp.arange(rows, dtype=jnp.int32)
    place = (row // BLOCK * BLOCK)[:, None] - HALO + jnp.arange(BLOCK + 2 * HALO, dtype=jnp.int32)

    def document(position):
        return jnp.sum((position[..., None] >= ends).astype(jnp.int32), axis=-1)

    key = first + place
    allowed = (
        (jnp.abs(row[:, None] - place) <= RADIUS)
        & (key >= 0)
        & (key < seq_len)
        & (document(first + row)[:, None] == document(key))
    )
    return jnp.where(allowed, 0.0, NEVER).astype(jnp.float32)


def after(cells, *others):
    return lax.optimization_barrier((cells,) + others)[0] if others else cells


class Link:
    def __init__(self, axis, pairs, depth):
        self.axis, self.pairs, self.depth, self.sent = axis, pairs, depth, []

    def __call__(self, cells, depth=None):
        depth = self.depth if depth is None else depth
        if depth and len(self.sent) >= depth:
            cells = after(cells, self.sent[-depth])
        self.sent.append(lax.ppermute(cells, self.axis, self.pairs))
        return self.sent[-1]


def links(depth=2):
    span = lax.axis_size("seq")
    high = span // 2
    across = [(h * 2 + c, ((h + 1) % high) * 2 + c) for h in range(high) for c in range(2)]
    pairs = [(i, i ^ 1) for i in range(span)]
    rings = lax.axis_size("wt")
    along = [(i, (i + 1) % rings) for i in range(rings)]
    return Link("seq", across, depth), Link("seq", pairs, 0), Link("wt", along, 0)


def places():
    high = lax.axis_size("seq") // 2
    shard_no = lax.axis_index("seq")
    return high, shard_no // 2, shard_no % 2


class Gather:
    def __init__(self, shard, lines):
        self.across, self.swap = lines[:2]
        self.level = lax.all_gather(shard, "wt", axis=0)

    def cross(self, *others):
        self.row = [after(self.level, *others)]
        for _ in range(1, lax.axis_size("seq") // 2):
            self.row.append(self.across(self.row[-1]))
        return self

    def pieces(self, *others):
        found = {}
        for j, part in enumerate(self.row):
            part = after(part, *others) if j else part
            found[(None, j, 0)] = part
            found[(None, j, 1)] = self.swap(part)
        return found


def ring_gather(shard, lines, between):
    across, swap, along = lines
    found, current = {}, shard
    for k in range(lax.axis_size("wt")):
        current = along(current) if k else current
        if k == lax.axis_size("wt") - 1:
            between()
        cells = current
        for j in range(lax.axis_size("seq") // 2):
            if j:
                cells = across(cells, 1) if k == lax.axis_size("wt") - 1 else across(cells)
            found[(k, j, 0)] = cells
            found[(k, j, 1)] = swap(cells)
    return found


def assemble_kernel(count, plan, seat_ref, *refs):
    parts, wholes, sems = refs[:count], refs[count:-1], refs[-1]
    copies = []
    for number, (source, start, rows, seat, ring, whole, to) in enumerate(plan):
        there = wholes[whole].at[seat_ref[seat]]
        if ring is None:
            here, there = parts[source].at[:, pl.ds(start, rows)], there.at[:, pl.ds(to, rows)]
        else:
            here = parts[source].at[pl.ds(start, rows)]
            there = there.at[seat_ref[ring], pl.ds(to, rows)]
        copies.append(pltpu.make_async_copy(here, there, sems.at[number]))
    for copy in copies:
        copy.start()
    for copy in copies:
        copy.wait()


def assemble(pieces, pack):
    high, h, c = places()
    rings, z = lax.axis_size("wt"), lax.axis_index("wt")
    seats = [
        lax.rem(h - j + high, high) * 2 + (c + p) % 2 for j in range(high) for p in range(2)
    ] + [lax.rem(z - k + rings, rings) for k in range(rings)]
    sources, plan = [], []
    for (k, j, p), part in pieces.items():
        start = 0
        for whole, rows in enumerate(pack):
            ring = None if k is None else 2 * high + k
            plan.append((len(sources), start, rows, j * 2 + p, ring, whole, 0))
            start += rows
        sources.append(part)
    width, kind = sources[0].shape[-1], sources[0].dtype
    shapes = [(2 * high, rings, rows, width) for rows in pack]
    if any(rows % 16 for rows in pack):
        wholes = [jnp.zeros(shape, kind) for shape in shapes]
        for source, start, rows, seat, ring, whole, to in plan:
            part = sources[source]
            part = part[None] if ring is None else part[None, None]
            part = part[:, :, start : start + rows]
            place = (seats[seat], 0 if ring is None else seats[ring], to, 0)
            wholes[whole] = lax.dynamic_update_slice(wholes[whole], part, place)
    else:
        wholes = pl.pallas_call(
            functools.partial(assemble_kernel, len(sources), plan),
            out_shape=[jax.ShapeDtypeStruct(shape, kind) for shape in shapes],
            grid_spec=pltpu.PrefetchScalarGridSpec(
                num_scalar_prefetch=1,
                grid=(),
                in_specs=[pl.BlockSpec(memory_space=pl.ANY)] * len(sources),
                out_specs=[pl.BlockSpec(memory_space=pltpu.VMEM)] * len(shapes),
                scratch_shapes=[pltpu.SemaphoreType.DMA((len(plan),))],
            ),
            compiler_params=pltpu.CompilerParams(vmem_limit_bytes=40 * 2**20),
            cost_estimate=cost_of(0, 2 * sum(source.size * 2 for source in sources)),
        )(jnp.stack(seats).astype(jnp.int32), *sources)
    return [whole.reshape(-1, width) for whole in wholes]


def plus(left, right, kind):
    return (left.astype(jnp.float32) + right.astype(jnp.float32)).astype(kind)


class Scatter:
    def __init__(self, partial, lines, kind=jnp.bfloat16, along_first=False):
        self.across, self.swap = lines[:2]
        self.kind, self.along_first = kind, along_first
        high, h, c = places()
        self.high, self.h = high, h
        cells = partial.reshape(high, 2, -1, partial.shape[-1])
        self.mine = lax.dynamic_index_in_dim(cells, c, 1, False)
        self.received = self.swap(lax.dynamic_index_in_dim(cells, 1 - c, 1, False))
        if along_first:
            rows = self.mine.shape[1]
            rings = lax.axis_size("wt")
            whole = plus(self.mine, self.received, kind)
            whole = whole.reshape(high, rings, rows // rings, -1).swapaxes(0, 1)
            self.summed = whole.reshape(high * rows, -1)
            summed = lax.psum_scatter(self.summed, "wt", scatter_dimension=0, tiled=True)
            self.mine = summed.reshape(high, rows // rings, -1)
            self.level = None
        else:
            self.level = self.block(1)

    def block(self, j):
        place = lax.rem(self.h - j + self.high, self.high)
        mine = lax.dynamic_index_in_dim(self.mine, place, 0, False)
        if self.along_first:
            return mine
        return plus(mine, lax.dynamic_index_in_dim(self.received, place, 0, False), self.kind)

    def cross(self, *others):
        self.level = self.block(1) if self.level is None else self.level
        self.sent = after(self.level, *others)
        self.arrived = self.across(self.sent)
        return self

    def add(self, *others):
        level = self.arrived
        for j in range(2, self.high + 1):
            level = plus(after(level, *others), self.block(j), self.kind)
            if j < self.high:
                level = self.across(level)
        self.level = level
        return self

    def finish(self):
        level = self.level
        if not self.along_first:
            level = lax.psum_scatter(level, "wt", scatter_dimension=0, tiled=True)
        return level.astype(jnp.float32)


def ring_scatter(partial, lines):
    across, swap, along = lines
    high, h, c = places()
    rings, z = lax.axis_size("wt"), lax.axis_index("wt")
    cells = partial.reshape(high, 2, rings, -1, partial.shape[-1])
    mine = lax.dynamic_index_in_dim(cells, c, 1, False)
    received = swap(lax.dynamic_index_in_dim(cells, 1 - c, 1, False))
    size = (1, 1) + cells.shape[3:]

    def block(j, k):
        place = (lax.rem(h - j + high, high), lax.rem(z - k + rings, rings), 0, 0)
        return plus(
            lax.dynamic_slice(mine, place, size)[0, 0],
            lax.dynamic_slice(received, place, size)[0, 0],
            jnp.bfloat16,
        )

    total = None
    for k in range(1, rings + 1):
        level = block(1, k)
        for j in range(2, high + 1):
            level = plus(across(level), block(j, k), jnp.bfloat16)
        if total is None:
            total = level
        else:
            total = plus(along(total), level, jnp.float32 if k == rings else jnp.bfloat16)
    return total.astype(jnp.float32)


def per_device(
    inputs,
    lengths,
    cotangent,
    gain_attn,
    w_query,
    w_key,
    w_value,
    w_out,
    gain_mlp,
    w_gate,
    w_up,
    w_down,
):
    section_no = lax.axis_index("section")
    shard_no = lax.axis_index("seq")
    micro_count, rows_local, model_width = inputs.shape
    seq_len = rows_local * lax.axis_size("seq")
    is_first = (section_no == 0).astype(jnp.int32)
    slots = micro_count + 1
    bias = jnp.stack(
        [
            window_bias(lengths[number], shard_no, rows_local, seq_len)
            for number in range(micro_count)
        ]
    )

    def choose(of_first, of_second):
        return is_first * of_first + (1 - is_first) * of_second

    rows = w_query.shape[1]
    gains = jnp.pad(
        jnp.concatenate([gain_attn, gain_mlp], 1), ((0, 15), (0, model_width - 2 * rows))
    )
    lines = links()
    narrow = jnp.concatenate([w_query[0], w_key[0], w_value[0], w_out[0], gains], 0)
    gate_gather = Gather(w_gate[0], lines)
    up_gather = Gather(w_up[0], lines)
    down_gather = Gather(w_down[0], lines)
    pieces = ring_gather(narrow, lines, gate_gather.cross)
    (packed,) = assemble(pieces, [narrow.shape[0]])
    packed = packed.reshape(-1, narrow.shape[0], model_width)
    gain_rows = packed[:, 4 * rows]
    gain_one = gain_rows[:, :rows].reshape(1, -1)
    gain_two = gain_rows[:, rows : 2 * rows].reshape(1, -1)
    params = (gain_one, packed, gain_two)

    store, results, grad_sources, sums = {}, [], [], {}
    arrived = [jnp.zeros((rows_local, model_width), jnp.bfloat16)]
    arrived_grad = [arrived[0]]

    def forward(moment, params):
        early, late = min(moment, micro_count - 1), max(moment - 1, 0)
        scalars = jnp.stack([is_first, is_first * 0 + moment, choose(early, late)])
        layer_in = after(arrived[moment], *grad_sources[-1:])
        kv, tail, head = project(store, slots, moment, scalars, inputs[early], layer_in, params)
        low = shifted(tail, "seq", 1)
        high = shifted(head, "seq", -1)
        if moment == 0:
            up_gather.cross()
            down_gather.cross(low, high)
            kv = after(kv, up_gather.row[-1])
            attend(store, slots, moment, scalars, kv, low, high, bias, params)
            two = store["normed_two"]
            (gate_w,) = assemble(gate_gather.pieces(kv), [rows])
            (up_w,) = assemble(up_gather.pieces(kv), [rows])
            (down_w,) = assemble(down_gather.pieces(two, gate_w, up_w), [w_down.shape[1]])
            params = params + (gate_w, up_w, down_w)
            (result,) = feed(store, slots, moment, scalars, params)
        else:
            (result,) = attend(store, slots, moment, scalars, kv, low, high, bias, params)
        results.append(result)
        if moment < micro_count:
            arrived.append(shifted(result, "section", 1))
        return params

    def both(name, start):
        chosen = lax.dynamic_slice_in_dim(store[name], start, micro_count, 0)
        return chosen.reshape(-1, chosen.shape[-1])

    def product(left, right, then=()):
        left = after(both(left, 1 - is_first), *then)
        return jnp.dot(
            left.T, both(right, is_first), preferred_element_type=jnp.float32
        ).astype(jnp.bfloat16)

    def backward(moment):
        early, late = min(moment, micro_count - 1), max(moment - 1, 0)
        scalars = jnp.stack(
            [is_first, choose(late, min(moment + 1, micro_count)), choose(late, early)]
        )
        grad_res, grad_mixed = feed_back(
            store, slots, moment, scalars, arrived_grad[moment], cotangent[early], params
        )
        if moment == micro_count:
            lines = links()
            gate_part = product("normed_two", "grad_gate")
            gate_sum = Scatter(gate_part, lines)
            out_part = product("mixed", "grad_branch", then=(gate_part,))
            out_sum = Scatter(out_part, lines, along_first=True)
            up_part = product("normed_two", "grad_up", then=(out_part,))
            up_sum = Scatter(up_part, lines)
            gate_sum.cross(up_part)
            down_part = product("gated", "grad_result", then=(gate_sum.sent, out_sum.summed))
            down_sum = Scatter(down_part, lines)
            grad_mixed = after(grad_mixed, down_part, up_sum.level)
        center, top, bottom = attend_back(store, slots, moment, scalars, grad_mixed, bias)
        above = shifted(top, "seq", -1)
        below = shifted(bottom, "seq", 1)
        if moment == micro_count:
            up_sum.cross(above, below)
            gate_sum.add(center)
            center = after(center, gate_sum.level, down_sum.level)
            down_sum.cross(above, below)
            sums.update(lines=lines, gate=gate_sum, up=up_sum, down=down_sum, out=out_sum)
        (grad_source,) = project_back(
            store, slots, moment, scalars, center, below, above, grad_res, params
        )
        grad_sources.append(grad_source)
        if moment < micro_count:
            arrived_grad.append(shifted(grad_source, "section", -1))

    params = forward(0, params)
    for moment in range(1, slots):
        forward(moment, params)
        backward(moment - 1)
    backward(micro_count)

    activations = jnp.stack(
        [
            jnp.where(is_first == 1, results[number], results[number + 1])
            for number in range(micro_count)
        ]
    )[None]
    input_grads = jnp.stack(
        [
            jnp.where(is_first == 1, grad_sources[number + 1], grad_sources[number])
            for number in range(micro_count)
        ]
    )[None]
    lines, gate_sum, up_sum, down_sum, out_sum = (
        sums[name] for name in ("lines", "gate", "up", "down", "out")
    )
    up_sum.add(grad_sources[-1])
    gain_rows = jnp.concatenate(
        [
            jnp.sum(lax.dynamic_slice_in_dim(store[name], is_first, micro_count, 0), 0)
            for name in ("gain_one", "gain_two")
        ]
    ).astype(jnp.bfloat16)
    picked = jnp.arange(2 * 8)[:, None] == jnp.arange(BLOCK)[None] * 8
    right = jnp.concatenate(
        [both(name, is_first) for name in ("grad_queries", "grad_keys", "grad_values")], 1
    )
    right = jnp.concatenate(
        [
            jnp.pad(right, ((0, 0), (0, BLOCK))),
            jnp.pad(picked.astype(jnp.bfloat16), ((0, 0), (right.shape[1], 0))),
        ]
    )
    left = after(jnp.concatenate([both("normed", 1 - is_first), gain_rows]), up_sum.level)
    qkv_part = jnp.dot(left.T, right, preferred_element_type=jnp.float32).astype(jnp.bfloat16)
    grad_up_w = up_sum.finish()
    down_sum.add(qkv_part, grad_up_w)
    qkv_all = ring_scatter(qkv_part, lines)
    grad_out_w = out_sum.cross().add().finish()
    grad_gate_w, grad_down_w = gate_sum.finish(), down_sum.finish()
    grad_query_w, grad_key_w, grad_value_w, gain_sum = (
        qkv_all[:, number * model_width : (number + 1) * model_width] for number in range(4)
    )
    return (
        activations,
        input_grads,
        gain_sum[:, 0][None],
        grad_query_w[None],
        grad_key_w[None],
        grad_value_w[None],
        grad_out_w[None],
        gain_sum[:, 1][None],
        grad_gate_w[None],
        grad_up_w[None],
        grad_down_w[None],
    )


def solution(mesh):
    placed = (
        P("wt", "seq", None),
        P("wt", None),
        P("wt", "seq", None),
        P("section", ("seq", "wt")),
        P("section", ("seq", "wt"), None),
        P("section", ("seq", "wt"), None),
        P("section", ("seq", "wt"), None),
        P("section", ("seq", "wt"), None),
        P("section", ("seq", "wt")),
        P("section", ("seq", "wt"), None),
        P("section", ("seq", "wt"), None),
        P("section", ("seq", "wt"), None),
    )
    return jax.shard_map(
        per_device,
        mesh=mesh,
        in_specs=placed,
        out_specs=(
            P("section", "wt", "seq", None),
            P("section", "wt", "seq", None),
            P("section", ("seq", "wt")),
            P("section", ("seq", "wt"), None),
            P("section", ("seq", "wt"), None),
            P("section", ("seq", "wt"), None),
            P("section", ("seq", "wt"), None),
            P("section", ("seq", "wt")),
            P("section", ("seq", "wt"), None),
            P("section", ("seq", "wt"), None),
            P("section", ("seq", "wt"), None),
        ),
        check_vma=False,
    )
```

```python
import functools

import jax
import jax.numpy as jnp
from jax import lax
from jax.experimental import pallas as pl
from jax.experimental.pallas import tpu as pltpu
from jax.sharding import PartitionSpec as P

HEAD_DIM = 64
RADIUS = 127


EPSILON = 1e-06


def shifted(shard, axis, by):
    length = lax.axis_size(axis)
    pairs = [(i, i + by) for i in range(length) if 0 <= i + by < length]
    return lax.ppermute(shard, axis, pairs)


HALO = 128
BLOCK = 128
WIDE = 256
NEVER = -1e30


def call(kernel, grid, scalars, ins, in_specs, outs, out_specs, scratch=(), aliases=None, cost=None):
    return pl.pallas_call(
        kernel,
        out_shape=outs,
        grid_spec=pltpu.PrefetchScalarGridSpec(
            num_scalar_prefetch=1,
            grid=grid,
            in_specs=in_specs,
            out_specs=out_specs,
            scratch_shapes=list(scratch),
        ),
        input_output_aliases=aliases or {},
        compiler_params=pltpu.CompilerParams(
            vmem_limit_bytes=56 * 2**20, dimension_semantics=("arbitrary",) * len(grid)
        ),
        cost_estimate=cost,
    )(scalars, *ins)


def cost_of(flops, moved, transcendentals=0):
    return pl.CostEstimate(
        flops=int(flops), bytes_accessed=int(moved), transcendentals=int(transcendentals)
    )


def nt_dot(left, right):
    return lax.dot_general(
        left, right, (((1,), (1,)), ((), ())), preferred_element_type=jnp.float32
    )


def tn_dot(left, right):
    return lax.dot_general(
        left, right, (((0,), (0,)), ((), ())), preferred_element_type=jnp.float32
    )


def dot(left, right):
    return jnp.dot(left, right, preferred_element_type=jnp.float32)


def inverse_rms(values):
    return lax.rsqrt(jnp.mean(values * values, axis=-1, keepdims=True) + EPSILON)


def flat(ref):
    cells = ref[...]
    return cells.reshape(-1, cells.shape[-1])


def packed_spec(packed, number, tile):
    rows = (packed.shape[1] - 16) // 4
    return pl.BlockSpec((packed.shape[0], rows, tile), lambda j, s: (0, number, j))


def project_kernel(idx, own, arrived, gain, wq, wk, wv, *rest):
    x_out, n_out, q_out, kv_out, tail_out, head_out = rest[-6:]

    @pl.when(pl.program_id(0) == 0)
    def _():
        picked = jnp.where(
            idx[0] == 1, own[...].astype(jnp.float32), arrived[...].astype(jnp.float32)
        )
        x_out[...] = picked.astype(jnp.bfloat16)
        n_out[...] = (picked * inverse_rms(picked) * gain[...].astype(jnp.float32)).astype(
            jnp.bfloat16
        )

    normed = n_out[...]
    kv_out[0] = dot(normed, flat(wk)).astype(jnp.bfloat16)
    kv_out[1] = dot(normed, flat(wv)).astype(jnp.bfloat16)
    q_out[...] = dot(normed, flat(wq)).astype(jnp.bfloat16)
    tail_out[...] = kv_out[:, pl.ds(kv_out.shape[1] - HALO, HALO)]
    head_out[...] = kv_out[:, pl.ds(0, HALO)]


def slot_call(kernel, grid, scalars, ins, in_specs, kept, fresh, store, slots, moment, scratch=(), cost=None):
    aliases, extra = {}, []
    outs, out_specs = [], []
    for name, shape, block, index, kind, *own in kept:
        slot = own[0] if own else moment
        outs.append(jax.ShapeDtypeStruct((slots,) + shape, kind))
        if block is None:
            out_specs.append(pl.BlockSpec(memory_space=pl.ANY))
        else:
            out_specs.append(
                pl.BlockSpec(
                    (None,) + block, lambda j, s, index=index, slot=slot: (slot,) + index(j)
                )
            )
        if name in store:
            aliases[1 + len(ins) + len(extra)] = len(outs) - 1
            extra.append(store[name])
    for shape, kind, spec in fresh:
        outs.append(jax.ShapeDtypeStruct(shape, kind))
        out_specs.append(spec)
    results = call(
        kernel,
        grid,
        scalars,
        list(ins) + extra,
        list(in_specs) + [pl.BlockSpec(memory_space=pl.ANY)] * len(extra),
        outs,
        out_specs,
        scratch,
        aliases,
        cost,
    )
    for (name, *_), value in zip(kept, results):
        store[name] = value
    return results[len(kept) :]


def whole_spec(shape):
    return pl.BlockSpec(shape, lambda j, s: (0,) * len(shape))


def project(store, slots, moment, scalars, own, arrived, params):
    rows, width = arrived.shape
    gain_one, packed = params[:2]
    tile = WIDE
    at_start = lambda j: (0, 0)
    halo_spec = pl.BlockSpec((2, HALO, tile), lambda j, s: (0, 0, j))
    return slot_call(
        project_kernel,
        (width // tile,),
        scalars,
        [own, arrived, gain_one, packed, packed, packed],
        [whole_spec((rows, width)), whole_spec((rows, width)), whole_spec((1, width))]
        + [packed_spec(packed, number, tile) for number in range(3)],
        [
            ("source", (rows, width), (rows, width), at_start, jnp.bfloat16),
            ("normed", (rows, width), (rows, width), at_start, jnp.bfloat16),
            ("queries", (rows, width), (rows, tile), lambda j: (0, j), jnp.bfloat16),
        ],
        [
            (
                (2, rows, width),
                jnp.bfloat16,
                pl.BlockSpec((2, rows, tile), lambda j, s: (0, 0, j)),
            ),
            ((2, HALO, width), jnp.bfloat16, halo_spec),
            ((2, HALO, width), jnp.bfloat16, halo_spec),
        ],
        store,
        slots,
        moment,
        cost=cost_of(6 * rows * width * width, 6 * width * width + 14 * rows * width),
    )


def row_blocks(rows):
    return [(start, min(BLOCK, rows - start)) for start in range(0, rows, BLOCK)]


def head_masks(kind):
    lane = lax.broadcasted_iota(jnp.int32, (1, 2 * HEAD_DIM), 1)
    low = (lane < HEAD_DIM).astype(kind)
    return (low, (1 - low).astype(kind))


def wide_tile(size):
    return max(tile for tile in range(128, 1409, 128) if size % tile == 0)


def chunks(size, tile):
    return [(start, min(tile, size - start)) for start in range(0, size, tile)]


def stacked_heads(pair):
    return jnp.concatenate([pair * mask for mask in head_masks(pair.dtype)], 0)


def unstacked_heads(stacked):
    rows = stacked.shape[0] // 2
    low = lax.broadcasted_iota(jnp.int32, (1, 2 * HEAD_DIM), 1) < HEAD_DIM
    return jnp.where(low, stacked[:rows], stacked[rows:])


def attend_step(q, kv, low, high, bias, wo, k_out, v_out, mixed_out, lse_out):
    rows = q.shape[0]
    for place, out in ((0, k_out), (1, v_out)):
        out[pl.ds(0, HALO)] = low[place]
        out[pl.ds(HALO, rows)] = kv[place]
        out[pl.ds(HALO + rows, HALO)] = high[place]
    scale = jnp.bfloat16(HEAD_DIM**-0.5)
    tiles = [
        (start, count, pair)
        for start, count in row_blocks(rows)
        for pair in range(WIDE // (2 * HEAD_DIM))
    ]
    sums = {}
    scores, powers, totals = {}, {}, {}
    for start, count, pair in tiles:
        span = count + 2 * HALO
        lanes = slice(pair * 2 * HEAD_DIM, (pair + 1) * 2 * HEAD_DIM)
        q_both = stacked_heads(q[pl.ds(start, count), lanes] * scale)
        block_bias = bias[pl.ds(start, count), :span]
        scores[start, pair] = nt_dot(
            q_both, k_out[pl.ds(start, span), lanes]
        ) + jnp.concatenate([block_bias, block_bias], 0)
    for start, count, pair in tiles:
        value = scores[start, pair]
        most = jnp.max(value, axis=-1, keepdims=True)
        power = jnp.exp(value - most)
        powers[start, pair] = power.astype(jnp.bfloat16)
        totals[start, pair] = jnp.sum(power, axis=-1, keepdims=True)
        log_sum = most + jnp.log(totals[start, pair])
        sums[start, pair] = (log_sum[:count], log_sum[count:])
    for start, count, pair in tiles:
        span = count + 2 * HALO
        lanes = slice(pair * 2 * HEAD_DIM, (pair + 1) * 2 * HEAD_DIM)
        mixed = dot(powers[start, pair], v_out[pl.ds(start, span), lanes])
        mixed = mixed * (1.0 / totals[start, pair])
        mixed_out[pl.ds(start, count), lanes] = unstacked_heads(mixed).astype(jnp.bfloat16)
    for start, count in row_blocks(rows):
        lane = lax.broadcasted_iota(jnp.int32, (count, 2 * HEAD_DIM), 1)
        wide = jnp.zeros((count, 2 * HEAD_DIM), jnp.float32)
        for pair in range(WIDE // (2 * HEAD_DIM)):
            for number, value in enumerate(sums[start, pair]):
                wide = jnp.where(lane == 2 * pair + number, value, wide)
        lse_out[pl.ds(start, count)] = wide
    return dot(mixed_out[...], flat(wo))


def attend_steps(parts, source, gain, res_out, two_out, total, steps):
    step = pl.program_id(0)

    @pl.when(step < steps)
    def _():
        part = attend_step(*parts)

        @pl.when(step == 0)
        def _():
            total[...] = source[...].astype(jnp.float32) + part

        @pl.when(step > 0)
        def _():
            total[...] += part

        @pl.when(step == steps - 1)
        def _():
            residual = total[...]
            res_out[...] = residual
            two_out[...] = (
                residual * inverse_rms(residual) * gain[...].astype(jnp.float32)
            ).astype(jnp.bfloat16)


def attend_kernel(steps, idx, q, kv, low, high, bias, wo, source, gain, *rest):
    k_out, v_out, mixed_out, lse_out, res_out, two_out, total = rest[-7:]
    parts = (q, kv, low, high, bias, wo, k_out, v_out, mixed_out, lse_out)
    attend_steps(parts, source, gain, res_out, two_out, total, steps)


class Feed:
    def __init__(self, moment, weights, outs, held, sems):
        self.moment, self.weights, self.outs, self.held, self.sems = (
            moment,
            weights,
            outs,
            held,
            sems,
        )
        size = weights[0].shape[1]
        self.tiles = chunks(size, wide_tile(size))

    def fetch(self, number, part):
        start, size = self.tiles[number]
        place = (slice(None), pl.ds(start, size)) if part < 2 else (pl.ds(start, size),)
        return pltpu.make_async_copy(
            self.weights[part].at[place], self.held[part].at[place], self.sems.at[3 * number + part]
        )

    def start(self):
        for number in range(len(self.tiles)):
            for part in range(3):
                self.fetch(number, part).start()

    def run(self, normed, total, result):
        gate_w, up_w, down_w = self.held[:3]
        stores = []
        for number, (start, size) in enumerate(self.tiles):
            lanes = slice(start, start + size)
            self.fetch(number, 0).wait()
            gate = dot(normed, gate_w[:, lanes])
            self.fetch(number, 1).wait()
            up = dot(normed, up_w[:, lanes])
            half, _, _ = gelu_parts(gate)
            gated = (gate * half * up).astype(jnp.bfloat16)
            values = (gate.astype(jnp.bfloat16), up.astype(jnp.bfloat16), gated)
            for part, value in enumerate(values):
                held = self.held[3 + part]
                held[:, lanes] = value
                copy = pltpu.make_async_copy(
                    held.at[:, pl.ds(start, size)],
                    self.outs[part].at[self.moment, :, pl.ds(start, size)],
                    self.sems.at[3 * len(self.tiles) + 3 * number + part],
                )
                copy.start()
                stores.append(copy)
            self.fetch(number, 2).wait()
            total[...] += dot(gated, down_w[lanes])
        result[...] = total[...].astype(jnp.bfloat16)
        for copy in stores:
            copy.wait()


def feed_kernel(moment, idx, two, residual, wg, wu, wd, *rest):
    outs, result, total, held, sems = rest[-12:-9], rest[-9], rest[-8], rest[-7:-1], rest[-1]
    feed = Feed(moment, (wg, wu, wd), outs, held, sems)
    feed.start()
    total[...] = residual[...]
    feed.run(two[...], total, result)


def attend_feed_kernel(
    moment, steps, idx, q, kv, low, high, bias, wo, source, gain, wg, wu, wd, *rest
):
    k_out, v_out, mixed_out, lse_out, res_out, two_out = rest[-18:-12]
    outs, result, total, held, sems = rest[-12:-9], rest[-9], rest[-8], rest[-7:-1], rest[-1]
    feed = Feed(moment, (wg, wu, wd), outs, held, sems)
    pl.when(pl.program_id(0) == 0)(feed.start)
    parts = (q, kv, low, high, bias, wo, k_out, v_out, mixed_out, lse_out)
    attend_steps(parts, source, gain, res_out, two_out, total, steps)

    @pl.when(pl.program_id(0) == steps)
    def _():
        feed.run(two_out[...], total, result)


def attend_feed_back_kernel(
    moment, steps, extras, idx, q, kv, low, high, bias, wo, source, gain, wg, wu, wd, *rest
):
    arrived, own, packed = rest[:3]
    older = rest[3 : 3 + extras]
    k_out, v_out, mixed_out, lse_out, res_out, two_out = rest[3 + extras : 9 + extras]
    outs, g_out = rest[9 + extras : 12 + extras], rest[12 + extras]
    grad_outs = rest[13 + extras : 15 + extras]
    branch_out, gain_out, result, grad_out, grad_mixed = rest[15 + extras : 20 + extras]
    total, held, sems = rest[20 + extras], rest[21 + extras : 27 + extras], rest[27 + extras]
    gate_back, up_back, res_back, dg_all, du_all, g_arrived, g_own, wo_all, more = rest[28 + extras :]
    feed = Feed(moment, (wg, wu, wd), outs, held, sems)
    taken = idx[1]
    shard = wo_all.shape[1]
    fixed = [
        (arrived, g_arrived),
        (own, g_own),
        (packed.at[:, pl.ds(3 * shard, shard)], wo_all),
    ]
    kept = [
        (older[6].at[taken], gate_back),
        (older[7].at[taken], up_back),
        (older[4].at[taken], res_back),
    ]

    def copy(number):
        here, there = (fixed + kept)[number]
        return pltpu.make_async_copy(here, there, more.at[number])

    @pl.when(pl.program_id(0) == 0)
    def _():
        feed.start()
        for number in range(3):
            copy(number).start()

        @pl.when(taken != moment)
        def _():
            for number in range(3, 6):
                copy(number).start()

    parts = (q, kv, low, high, bias, wo, k_out, v_out, mixed_out, lse_out)
    attend_steps(parts, source, gain, res_out, two_out, total, steps)

    @pl.when(pl.program_id(0) == steps)
    def _():
        feed.run(two_out[...], total, result)

        @pl.when(taken != moment)
        def _():
            for number in range(3, 6):
                copy(number).wait()

        @pl.when(taken == moment)
        def _():
            gate_back[...] = held[3][...]
            up_back[...] = held[4][...]
            res_back[...] = res_out[...]

        for number in range(3):
            copy(number).wait()
        grads = jnp.where(
            idx[0] == 1, g_arrived[...].astype(jnp.float32), g_own[...].astype(jnp.float32)
        ).astype(jnp.bfloat16)
        g_out[...] = grads
        gate_w, up_w, down_w = held[:3]
        stores = []
        for number, (start, size) in enumerate(feed.tiles):
            lanes = slice(start, start + size)
            grad_gate, grad_up = feed_grads(
                nt_dot(grads, down_w[lanes]), gate_back[:, lanes], up_back[:, lanes]
            )
            for part, (value, all_of) in enumerate(((grad_gate, dg_all), (grad_up, du_all))):
                all_of[:, lanes] = value
                store = pltpu.make_async_copy(
                    all_of.at[:, pl.ds(start, size)],
                    grad_outs[part].at[moment - 1, :, pl.ds(start, size)],
                    more.at[6 + 2 * number + part],
                )
                store.start()
                stores.append(store)
            part = nt_dot(grad_gate, gate_w[:, lanes]) + nt_dot(grad_up, up_w[:, lanes])
            if number:
                total[...] += part
            else:
                total[...] = part
        pulled, grad_gain = norm_back(
            total[...], res_back[...], gain[...].astype(jnp.float32)
        )
        gain_out[...] = jnp.broadcast_to(grad_gain, gain_out.shape)
        grad_residual = grads.astype(jnp.float32) + pulled
        grad_out[...] = grad_residual
        branch = grad_residual.astype(jnp.bfloat16)
        branch_out[...] = branch
        grad_mixed[...] = nt_dot(branch, flat(wo_all)).astype(jnp.bfloat16)
        for store in stores:
            store.wait()


def attend(store, slots, moment, scalars, kv, low, high, bias, params, back=None):
    rows, width = kv.shape[1:]
    packed, gain_two = params[1:3]
    weights = params[3:]
    shard = (packed.shape[1] - 16) // 4
    ext = rows + 2 * HALO
    quads = width // WIDE
    last = lambda j: jnp.minimum(j, quads - 1)
    at_start = lambda j: (0, 0)
    at_tile = lambda j: (0, last(j))
    halo_spec = pl.BlockSpec((2, HALO, WIDE), lambda j, s: (0, 0, last(j)))
    fed = feed_parts(rows, width, weights) if weights else ([], [], [], 0)
    kernel = functools.partial(attend_feed_kernel, moment) if weights else attend_kernel
    kernel = functools.partial(kernel, quads)
    back_ins, kept, fresh, scratch = [], [], [], []
    if back is not None:
        back_ins = [*back, packed]
        hidden = weights[0].shape[1]
        kept = [
            ("grad_result", (rows, width), (rows, width), at_start, jnp.bfloat16, moment - 1),
            ("grad_gate", (rows, hidden), None, None, jnp.bfloat16),
            ("grad_up", (rows, hidden), None, None, jnp.bfloat16),
            ("grad_branch", (rows, width), (rows, width), at_start, jnp.bfloat16, moment - 1),
            ("gain_two", (8, width), (8, width), at_start, jnp.float32, moment - 1),
        ]
        fresh = [
            ((rows, width), jnp.float32, whole_spec((rows, width))),
            ((rows, width), jnp.bfloat16, whole_spec((rows, width))),
        ]
        scratch = (
            [pltpu.VMEM((rows, hidden), jnp.bfloat16)] * 2
            + [pltpu.VMEM((rows, width), jnp.float32)]
            + [pltpu.VMEM((rows, hidden), jnp.bfloat16)] * 2
            + [pltpu.VMEM((rows, width), jnp.bfloat16)] * 2
            + [pltpu.VMEM((packed.shape[0], shard, width), jnp.bfloat16)]
            + [pltpu.SemaphoreType.DMA((6 + 2 * len(chunks(hidden, wide_tile(hidden))),))]
        )
        extras = 9 + sum(entry[0] in store for entry in kept)
        kernel = functools.partial(attend_feed_back_kernel, moment, quads, extras)
    return slot_call(
        kernel,
        (quads + (1 if weights else 0),),
        scalars,
        [store["queries"], kv, low, high, bias, packed, store["source"], gain_two]
        + [*weights, *back_ins],
        [
            pl.BlockSpec((None, rows, WIDE), lambda j, s: (moment, 0, last(j))),
            pl.BlockSpec((2, rows, WIDE), lambda j, s: (0, 0, last(j))),
            halo_spec,
            halo_spec,
            pl.BlockSpec((None,) + bias.shape[1:], lambda j, s: (s[2], 0, 0)),
            pl.BlockSpec((WIDE // shard, shard, width), lambda j, s: (last(j), 3, 0)),
            pl.BlockSpec((None, rows, width), lambda j, s: (moment, 0, 0)),
            whole_spec((1, width)),
        ]
        + [pl.BlockSpec(memory_space=pl.ANY)] * (len(weights) + len(back_ins)),
        [
            ("keys", (ext, width), (ext, WIDE), at_tile, jnp.bfloat16),
            ("values", (ext, width), (ext, WIDE), at_tile, jnp.bfloat16),
            ("mixed", (rows, width), (rows, WIDE), at_tile, jnp.bfloat16),
            ("lse", (rows, quads * BLOCK), (rows, BLOCK), at_tile, jnp.float32),
            ("residual", (rows, width), (rows, width), at_start, jnp.float32),
            ("normed_two", (rows, width), (rows, width), at_start, jnp.bfloat16),
        ]
        + fed[0]
        + kept,
        fed[1] + fresh,
        store,
        slots,
        moment,
        [pltpu.VMEM((rows, width), jnp.float32)] + fed[2] + scratch,
        cost_of(
            width * rows * ((BLOCK + 2 * HALO) * 8 + width * 2) + fed[3],
            2 * width * width + 20 * rows * width + fed[3] // rows,
        ),
    )


def feed_parts(rows, width, weights):
    hidden = weights[0].shape[1]
    tiles = len(chunks(hidden, wide_tile(hidden)))
    return (
        [(name, (rows, hidden), None, None, jnp.bfloat16) for name in ("gate", "up", "gated")],
        [((rows, width), jnp.bfloat16, whole_spec((rows, width)))],
        [pltpu.VMEM(weight.shape, jnp.bfloat16) for weight in weights]
        + [pltpu.VMEM((rows, hidden), jnp.bfloat16)] * 3
        + [pltpu.SemaphoreType.DMA((6 * tiles,))],
        6 * rows * width * hidden,
    )


def feed(store, slots, moment, scalars, params):
    weights = params[3:]
    rows, width = store["residual"].shape[1:]
    fed = feed_parts(rows, width, weights)
    return slot_call(
        functools.partial(feed_kernel, moment),
        (1,),
        scalars,
        [store["normed_two"], store["residual"], *weights],
        [pl.BlockSpec((None, rows, width), lambda j, s: (moment, 0, 0))] * 2
        + [pl.BlockSpec(memory_space=pl.ANY)] * 3,
        fed[0],
        fed[1],
        store,
        slots,
        moment,
        [pltpu.VMEM((rows, width), jnp.float32)] + fed[2],
        cost_of(fed[3], fed[3] // rows + 10 * rows * width),
    )


def gelu_parts(gate):
    root = 0.7978845608028654
    bend = jnp.tanh(root * (gate + 0.044715 * gate * gate * gate))
    return 0.5 * (1.0 + bend), bend, root


def feed_grads(grad_gated, gate, up):
    gate, up = gate.astype(jnp.float32), up.astype(jnp.float32)
    half, bend, root = gelu_parts(gate)
    slope = half + 0.5 * gate * (1.0 - bend * bend) * root * (1.0 + 3.0 * 0.044715 * gate * gate)
    return (
        (grad_gated * up * slope).astype(jnp.bfloat16),
        (grad_gated * gate * half).astype(jnp.bfloat16),
    )


def feed_back_kernel(idx, arrived, own, gate, up, residual, gain, wd, wg, wu, wo, *rest):
    g_out, dg_out, du_out, branch_out, gain_out, res_out, mixed_out, total = rest[-8:]
    step = pl.program_id(0)

    @pl.when(step == 0)
    def _():
        g_out[...] = jnp.where(
            idx[0] == 1, arrived[...].astype(jnp.float32), own[...].astype(jnp.float32)
        ).astype(jnp.bfloat16)

    grad_gated = nt_dot(g_out[...], wd[...])
    grad_gate, grad_up = feed_grads(grad_gated, gate[...], up[...])
    dg_out[...] = grad_gate
    du_out[...] = grad_up
    part = nt_dot(grad_gate, wg[...]) + nt_dot(grad_up, wu[...])

    @pl.when(step == 0)
    def _():
        total[...] = part

    @pl.when(step > 0)
    def _():
        total[...] += part

    @pl.when(step == pl.num_programs(0) - 1)
    def _():
        grads, grad_gain = norm_back(total[...], residual[...], gain[...].astype(jnp.float32))
        gain_out[...] = jnp.broadcast_to(grad_gain, gain_out.shape)
        grad_residual = g_out[...].astype(jnp.float32) + grads
        res_out[...] = grad_residual
        branch = grad_residual.astype(jnp.bfloat16)
        branch_out[...] = branch
        mixed_out[...] = nt_dot(branch, flat(wo)).astype(jnp.bfloat16)


def norm_back(grads, values, gain):
    scale = inverse_rms(values)
    pulled = grads * gain
    mean = jnp.mean(pulled * values, axis=-1, keepdims=True)
    return (
        scale * pulled - values * (scale * scale * scale * mean),
        jnp.sum(grads * values * scale, axis=0, keepdims=True),
    )


def feed_back(store, slots, moment, scalars, arrived, own, params):
    packed, gain_two, gate_w, up_w, down_w = params[1:]
    rows, width = arrived.shape
    hidden = gate_w.shape[1]
    tile = wide_tile(hidden)
    at_tile = lambda j: (0, j)
    at_start = lambda j: (0, 0)
    taken_tile = pl.BlockSpec((None, rows, tile), lambda j, s: (s[1], 0, j))
    return slot_call(
        feed_back_kernel,
        (hidden // tile,),
        scalars,
        [arrived, own, store["gate"], store["up"], store["residual"], gain_two]
        + [down_w, gate_w, up_w, packed],
        [whole_spec((rows, width)), whole_spec((rows, width)), taken_tile, taken_tile]
        + [pl.BlockSpec((None, rows, width), lambda j, s: (s[1], 0, 0)), whole_spec((1, width))]
        + [pl.BlockSpec((tile, width), lambda j, s: (j, 0))]
        + [pl.BlockSpec((width, tile), lambda j, s: (0, j))] * 2
        + [
            pl.BlockSpec(
                (packed.shape[0], (packed.shape[1] - 16) // 4, width), lambda j, s: (0, 3, 0)
            )
        ],
        [
            ("grad_result", (rows, width), (rows, width), at_start, jnp.bfloat16),
            ("grad_gate", (rows, hidden), (rows, tile), at_tile, jnp.bfloat16),
            ("grad_up", (rows, hidden), (rows, tile), at_tile, jnp.bfloat16),
            ("grad_branch", (rows, width), (rows, width), at_start, jnp.bfloat16),
            ("gain_two", (8, width), (8, width), at_start, jnp.float32),
        ],
        [
            ((rows, width), jnp.float32, whole_spec((rows, width))),
            ((rows, width), jnp.bfloat16, whole_spec((rows, width))),
        ],
        store,
        slots,
        moment,
        [pltpu.VMEM((rows, width), jnp.float32)],
        cost_of(6 * rows * width * hidden + 2 * rows * width * width, 6 * width * hidden),
    )


def attend_back_kernel(idx, q, keys, values, mixed, lse, grad_mixed, bias, *rest):
    q_out, center, top, bottom, k_total, v_total = rest[-6:]
    rows = q.shape[0]
    scale = jnp.bfloat16(HEAD_DIM**-0.5)
    k_total[...] = jnp.zeros_like(k_total)
    v_total[...] = jnp.zeros_like(v_total)
    tiles = [
        (start, count, slice(pair * 2 * HEAD_DIM, (pair + 1) * 2 * HEAD_DIM), pair)
        for start, count in row_blocks(rows)
        for pair in range(WIDE // (2 * HEAD_DIM))
    ]
    held = {}
    for start, count, lanes, pair in tiles:
        span = count + 2 * HALO
        q_both = stacked_heads(q[pl.ds(start, count), lanes] * scale)
        g_both = stacked_heads(grad_mixed[pl.ds(start, count), lanes])
        scores = nt_dot(q_both, keys[pl.ds(start, span), lanes])
        grad_probs = nt_dot(g_both, values[pl.ds(start, span), lanes])
        held[start, pair] = (q_both, g_both, scores, grad_probs)
    for start, count, lanes, pair in tiles:
        span = count + 2 * HALO
        q_both, g_both, scores, grad_probs = held[start, pair]
        block_bias = bias[pl.ds(start, count), :span]
        both_bias = jnp.concatenate([block_bias, block_bias], 0)
        m_pair = mixed[pl.ds(start, count), lanes].astype(jnp.float32)
        log_sum = jnp.concatenate(
            [lse[pl.ds(start, count), 2 * pair + n : 2 * pair + n + 1] for n in range(2)], 0
        )
        probs = jnp.exp(scores + (both_bias - log_sum))
        mean = jnp.sum(
            g_both.astype(jnp.float32) * jnp.concatenate([m_pair, m_pair], 0),
            axis=-1,
            keepdims=True,
        )
        grad_scores = (probs * (grad_probs - mean)).astype(jnp.bfloat16)
        held[start, pair] = (q_both, g_both, probs.astype(jnp.bfloat16), grad_scores)
    for start, count, lanes, pair in tiles:
        span = count + 2 * HALO
        q_both, g_both, probs, grad_scores = held[start, pair]
        grad_q = dot(grad_scores, keys[pl.ds(start, span), lanes])
        q_out[pl.ds(start, count), lanes] = (
            unstacked_heads(grad_q) * (HEAD_DIM**-0.5)
        ).astype(jnp.bfloat16)
        k_total[pl.ds(start, span), lanes] += tn_dot(grad_scores, q_both)
        v_total[pl.ds(start, span), lanes] += tn_dot(probs, g_both)
    for place, total in ((0, k_total), (1, v_total)):
        top[place] = total[pl.ds(0, HALO)].astype(jnp.bfloat16)
        center[place] = total[pl.ds(HALO, rows)]
        bottom[place] = total[pl.ds(HALO + rows, HALO)].astype(jnp.bfloat16)


def attend_back(store, slots, moment, scalars, grad_mixed, bias):
    rows, width = grad_mixed.shape
    ext = rows + 2 * HALO
    taken = pl.BlockSpec((None, rows, WIDE), lambda j, s: (s[1], 0, j))
    taken_ext = pl.BlockSpec((None, ext, WIDE), lambda j, s: (s[1], 0, j))
    halo_spec = pl.BlockSpec((2, HALO, WIDE), lambda j, s: (0, 0, j))
    work = width * rows * (BLOCK + 2 * HALO) * 2
    return slot_call(
        attend_back_kernel,
        (width // WIDE,),
        scalars,
        [store["queries"], store["keys"], store["values"], store["mixed"], store["lse"]]
        + [grad_mixed, bias],
        [
            taken,
            taken_ext,
            taken_ext,
            taken,
            pl.BlockSpec((None, rows, BLOCK), lambda j, s: (s[1], 0, j)),
            pl.BlockSpec((rows, WIDE), lambda j, s: (0, j)),
            pl.BlockSpec((None,) + bias.shape[1:], lambda j, s: (s[2], 0, 0)),
        ],
        [("grad_queries", (rows, width), (rows, WIDE), lambda j: (0, j), jnp.bfloat16)],
        [
            (
                (2, rows, width),
                jnp.float32,
                pl.BlockSpec((2, rows, WIDE), lambda j, s: (0, 0, j)),
            ),
            ((2, HALO, width), jnp.bfloat16, halo_spec),
            ((2, HALO, width), jnp.bfloat16, halo_spec),
        ],
        store,
        slots,
        moment,
        [pltpu.VMEM((ext, WIDE), jnp.float32)] * 2,
        cost_of(work * 20, 24 * rows * width),
    )


def project_back_kernel(
    idx, grad_q, center, below, above, source, gain, grad_res, wq, wk, wv, *rest
):
    k_out, v_out, gain_out, in_out, total = rest[-5:]
    step = pl.program_id(0)
    rows = source.shape[0]
    for place, out in ((0, k_out), (1, v_out)):
        head = center[place, pl.ds(0, HALO)] + below[place].astype(jnp.float32)
        tail = center[place, pl.ds(rows - HALO, HALO)] + above[place].astype(jnp.float32)
        out[pl.ds(0, HALO)] = head.astype(jnp.bfloat16)
        out[pl.ds(HALO, rows - 2 * HALO)] = center[place, pl.ds(HALO, rows - 2 * HALO)].astype(
            jnp.bfloat16
        )
        out[pl.ds(rows - HALO, HALO)] = tail.astype(jnp.bfloat16)
    part = nt_dot(grad_q[...], flat(wq))
    part += nt_dot(k_out[...], flat(wk)) + nt_dot(v_out[...], flat(wv))

    @pl.when(step == 0)
    def _():
        total[...] = part

    @pl.when(step > 0)
    def _():
        total[...] += part

    @pl.when(step == pl.num_programs(0) - 1)
    def _():
        grads, grad_gain = norm_back(
            total[...], source[...].astype(jnp.float32), gain[...].astype(jnp.float32)
        )
        gain_out[...] = jnp.broadcast_to(grad_gain, gain_out.shape)
        in_out[...] = (grad_res[...] + grads).astype(jnp.bfloat16)


def project_back(store, slots, moment, scalars, center, below, above, grad_res, params):
    rows, width = grad_res.shape
    gain_one, packed = params[:2]
    at_tile = lambda j: (0, j)
    at_start = lambda j: (0, 0)
    halo_spec = pl.BlockSpec((2, HALO, WIDE), lambda j, s: (0, 0, j))
    return slot_call(
        project_back_kernel,
        (width // WIDE,),
        scalars,
        [store["grad_queries"], center, below, above, store["source"], gain_one, grad_res]
        + [packed] * 3,
        [
            pl.BlockSpec((None, rows, WIDE), lambda j, s: (moment, 0, j)),
            pl.BlockSpec((2, rows, WIDE), lambda j, s: (0, 0, j)),
            halo_spec,
            halo_spec,
            pl.BlockSpec((None, rows, width), lambda j, s: (s[1], 0, 0)),
            whole_spec((1, width)),
            whole_spec((rows, width)),
        ]
        + [packed_spec(packed, number, WIDE) for number in range(3)],
        [
            ("grad_keys", (rows, width), (rows, WIDE), at_tile, jnp.bfloat16),
            ("grad_values", (rows, width), (rows, WIDE), at_tile, jnp.bfloat16),
            ("gain_one", (8, width), (8, width), at_start, jnp.float32),
        ],
        [((rows, width), jnp.bfloat16, whole_spec((rows, width)))],
        store,
        slots,
        moment,
        [pltpu.VMEM((rows, width), jnp.float32)],
        cost_of(6 * rows * width * width, 6 * width * width + 20 * rows * width),
    )


def window_bias(lengths_row, shard_no, rows, seq_len):
    ends = jnp.cumsum(lengths_row)
    first = shard_no * rows
    row = jnp.arange(rows, dtype=jnp.int32)
    place = (row // BLOCK * BLOCK)[:, None] - HALO + jnp.arange(BLOCK + 2 * HALO, dtype=jnp.int32)

    def document(position):
        return jnp.sum((position[..., None] >= ends).astype(jnp.int32), axis=-1)

    key = first + place
    allowed = (
        (jnp.abs(row[:, None] - place) <= RADIUS)
        & (key >= 0)
        & (key < seq_len)
        & (document(first + row)[:, None] == document(key))
    )
    return jnp.where(allowed, 0.0, NEVER).astype(jnp.float32)


def after(cells, *others):
    return lax.optimization_barrier((cells,) + others)[0] if others else cells


class Link:
    def __init__(self, axis, pairs, depth):
        self.axis, self.pairs, self.depth, self.sent = axis, pairs, depth, []

    def __call__(self, cells, depth=None):
        depth = self.depth if depth is None else depth
        if depth and len(self.sent) >= depth:
            cells = after(cells, self.sent[-depth])
        self.sent.append(lax.ppermute(cells, self.axis, self.pairs))
        return self.sent[-1]


def links(depth=2):
    span = lax.axis_size("seq")
    high = span // 2
    across = [(h * 2 + c, ((h + 1) % high) * 2 + c) for h in range(high) for c in range(2)]
    pairs = [(i, i ^ 1) for i in range(span)]
    rings = lax.axis_size("wt")
    along = [(i, (i + 1) % rings) for i in range(rings)]
    return Link("seq", across, depth), Link("seq", pairs, 0), Link("wt", along, 0)


def places():
    high = lax.axis_size("seq") // 2
    shard_no = lax.axis_index("seq")
    return high, shard_no // 2, shard_no % 2


class Gather:
    def __init__(self, shard, lines):
        self.across, self.swap = lines[:2]
        self.level = lax.all_gather(shard, "wt", axis=0)

    def cross(self, *others):
        self.row = [after(self.level, *others)]
        for _ in range(1, lax.axis_size("seq") // 2):
            self.row.append(self.across(self.row[-1]))
        return self

    def pieces(self, *others):
        found = {}
        for j, part in enumerate(self.row):
            part = after(part, *others) if j else part
            found[(None, j, 0)] = part
            found[(None, j, 1)] = self.swap(part)
        return found


def ring_gather(shard, lines, between):
    across, swap, along = lines
    found, current = {}, shard
    for k in range(lax.axis_size("wt")):
        current = along(current) if k else current
        if k == lax.axis_size("wt") - 1:
            between()
        cells = current
        for j in range(lax.axis_size("seq") // 2):
            if j:
                cells = across(cells, 1) if k == lax.axis_size("wt") - 1 else across(cells)
            found[(k, j, 0)] = cells
            found[(k, j, 1)] = swap(cells)
    return found


def assemble_kernel(count, plan, seat_ref, *refs):
    parts, wholes, sems = refs[:count], refs[count:-1], refs[-1]
    copies = []
    for number, (source, start, rows, seat, ring, whole, to) in enumerate(plan):
        there = wholes[whole].at[seat_ref[seat]]
        if ring is None:
            here, there = parts[source].at[:, pl.ds(start, rows)], there.at[:, pl.ds(to, rows)]
        else:
            here = parts[source].at[pl.ds(start, rows)]
            there = there.at[seat_ref[ring], pl.ds(to, rows)]
        copies.append(pltpu.make_async_copy(here, there, sems.at[number]))
    for copy in copies:
        copy.start()
    for copy in copies:
        copy.wait()


def assemble(pieces, pack):
    high, h, c = places()
    rings, z = lax.axis_size("wt"), lax.axis_index("wt")
    seats = [
        lax.rem(h - j + high, high) * 2 + (c + p) % 2 for j in range(high) for p in range(2)
    ] + [lax.rem(z - k + rings, rings) for k in range(rings)]
    sources, plan = [], []
    for (k, j, p), part in pieces.items():
        start = 0
        for whole, rows in enumerate(pack):
            ring = None if k is None else 2 * high + k
            plan.append((len(sources), start, rows, j * 2 + p, ring, whole, 0))
            start += rows
        sources.append(part)
    width, kind = sources[0].shape[-1], sources[0].dtype
    shapes = [(2 * high, rings, rows, width) for rows in pack]
    if any(rows % 16 for rows in pack):
        wholes = [jnp.zeros(shape, kind) for shape in shapes]
        for source, start, rows, seat, ring, whole, to in plan:
            part = sources[source]
            part = part[None] if ring is None else part[None, None]
            part = part[:, :, start : start + rows]
            place = (seats[seat], 0 if ring is None else seats[ring], to, 0)
            wholes[whole] = lax.dynamic_update_slice(wholes[whole], part, place)
    else:
        wholes = pl.pallas_call(
            functools.partial(assemble_kernel, len(sources), plan),
            out_shape=[jax.ShapeDtypeStruct(shape, kind) for shape in shapes],
            grid_spec=pltpu.PrefetchScalarGridSpec(
                num_scalar_prefetch=1,
                grid=(),
                in_specs=[pl.BlockSpec(memory_space=pl.ANY)] * len(sources),
                out_specs=[pl.BlockSpec(memory_space=pltpu.VMEM)] * len(shapes),
                scratch_shapes=[pltpu.SemaphoreType.DMA((len(plan),))],
            ),
            compiler_params=pltpu.CompilerParams(vmem_limit_bytes=40 * 2**20),
            cost_estimate=cost_of(0, 2 * sum(source.size * 2 for source in sources)),
        )(jnp.stack(seats).astype(jnp.int32), *sources)
    return [whole.reshape(-1, width) for whole in wholes]


def plus(left, right, kind):
    return (left.astype(jnp.float32) + right.astype(jnp.float32)).astype(kind)


class Scatter:
    def __init__(self, partial, lines, kind=jnp.bfloat16, along_first=False):
        self.across, self.swap = lines[:2]
        self.kind, self.along_first = kind, along_first
        high, h, c = places()
        self.high, self.h = high, h
        cells = partial.reshape(high, 2, -1, partial.shape[-1])
        self.mine = lax.dynamic_index_in_dim(cells, c, 1, False)
        self.received = self.swap(lax.dynamic_index_in_dim(cells, 1 - c, 1, False))
        if along_first:
            rows = self.mine.shape[1]
            rings = lax.axis_size("wt")
            whole = plus(self.mine, self.received, kind)
            whole = whole.reshape(high, rings, rows // rings, -1).swapaxes(0, 1)
            self.summed = whole.reshape(high * rows, -1)
            summed = lax.psum_scatter(self.summed, "wt", scatter_dimension=0, tiled=True)
            self.mine = summed.reshape(high, rows // rings, -1)
            self.level = None
        else:
            self.level = self.block(1)

    def block(self, j):
        place = lax.rem(self.h - j + self.high, self.high)
        mine = lax.dynamic_index_in_dim(self.mine, place, 0, False)
        if self.along_first:
            return mine
        return plus(mine, lax.dynamic_index_in_dim(self.received, place, 0, False), self.kind)

    def cross(self, *others):
        self.level = self.block(1) if self.level is None else self.level
        self.sent = after(self.level, *others)
        self.arrived = self.across(self.sent)
        return self

    def add(self, *others):
        level = self.arrived
        for j in range(2, self.high + 1):
            level = plus(after(level, *others), self.block(j), self.kind)
            if j < self.high:
                level = self.across(level)
        self.level = level
        return self

    def finish(self):
        level = self.level
        if not self.along_first:
            level = lax.psum_scatter(level, "wt", scatter_dimension=0, tiled=True)
        return level.astype(jnp.float32)


def ring_scatter(partial, lines):
    across, swap, along = lines
    high, h, c = places()
    rings, z = lax.axis_size("wt"), lax.axis_index("wt")
    cells = partial.reshape(high, 2, rings, -1, partial.shape[-1])
    mine = lax.dynamic_index_in_dim(cells, c, 1, False)
    received = swap(lax.dynamic_index_in_dim(cells, 1 - c, 1, False))
    size = (1, 1) + cells.shape[3:]

    def block(j, k):
        place = (lax.rem(h - j + high, high), lax.rem(z - k + rings, rings), 0, 0)
        return plus(
            lax.dynamic_slice(mine, place, size)[0, 0],
            lax.dynamic_slice(received, place, size)[0, 0],
            jnp.bfloat16,
        )

    total = None
    for k in range(1, rings + 1):
        level = block(1, k)
        for j in range(2, high + 1):
            level = plus(across(level), block(j, k), jnp.bfloat16)
        if total is None:
            total = level
        else:
            total = plus(along(total), level, jnp.float32 if k == rings else jnp.bfloat16)
    return total.astype(jnp.float32)


def per_device(
    inputs,
    lengths,
    cotangent,
    gain_attn,
    w_query,
    w_key,
    w_value,
    w_out,
    gain_mlp,
    w_gate,
    w_up,
    w_down,
):
    section_no = lax.axis_index("section")
    shard_no = lax.axis_index("seq")
    micro_count, rows_local, model_width = inputs.shape
    seq_len = rows_local * lax.axis_size("seq")
    is_first = (section_no == 0).astype(jnp.int32)
    slots = micro_count + 1
    bias = jnp.stack(
        [
            window_bias(lengths[number], shard_no, rows_local, seq_len)
            for number in range(micro_count)
        ]
    )

    def choose(of_first, of_second):
        return is_first * of_first + (1 - is_first) * of_second

    rows = w_query.shape[1]
    gains = jnp.pad(
        jnp.concatenate([gain_attn, gain_mlp], 1), ((0, 15), (0, model_width - 2 * rows))
    )
    lines = links()
    narrow = jnp.concatenate([w_query[0], w_key[0], w_value[0], w_out[0], gains], 0)
    gate_gather = Gather(w_gate[0], lines)
    up_gather = Gather(w_up[0], lines)
    down_gather = Gather(w_down[0], lines)
    pieces = ring_gather(narrow, lines, gate_gather.cross)
    (packed,) = assemble(pieces, [narrow.shape[0]])
    packed = packed.reshape(-1, narrow.shape[0], model_width)
    gain_rows = packed[:, 4 * rows]
    gain_one = gain_rows[:, :rows].reshape(1, -1)
    gain_two = gain_rows[:, rows : 2 * rows].reshape(1, -1)
    params = (gain_one, packed, gain_two)

    store, results, grad_sources, sums = {}, [], [], {}
    arrived = [jnp.zeros((rows_local, model_width), jnp.bfloat16)]
    arrived_grad = [arrived[0]]

    def taken_slot(moment):
        return choose(max(moment - 1, 0), min(moment + 1, micro_count))

    def forward(moment, params):
        early, late = min(moment, micro_count - 1), max(moment - 1, 0)
        scalars = jnp.stack([is_first, taken_slot(moment - 1), choose(early, late)])
        started = None
        layer_in = after(arrived[moment], *grad_sources[-1:])
        kv, tail, head = project(store, slots, moment, scalars, inputs[early], layer_in, params)
        low = shifted(tail, "seq", 1)
        high = shifted(head, "seq", -1)
        if moment == 0:
            up_gather.cross()
            down_gather.cross(low, high)
            kv = after(kv, up_gather.row[-1])
            attend(store, slots, moment, scalars, kv, low, high, bias, params)
            two = store["normed_two"]
            (gate_w,) = assemble(gate_gather.pieces(kv), [rows])
            (up_w,) = assemble(up_gather.pieces(kv), [rows])
            (down_w,) = assemble(down_gather.pieces(two, gate_w, up_w), [w_down.shape[1]])
            params = params + (gate_w, up_w, down_w)
            (result,) = feed(store, slots, moment, scalars, params)
        else:
            back = (arrived_grad[moment - 1], cotangent[min(moment - 1, micro_count - 1)])
            result, *started = attend(
                store, slots, moment, scalars, kv, low, high, bias, params, back
            )
        results.append(result)
        if moment < micro_count:
            arrived.append(shifted(result, "section", 1))
        return params, started

    def both(name, start):
        chosen = lax.dynamic_slice_in_dim(store[name], start, micro_count, 0)
        return chosen.reshape(-1, chosen.shape[-1])

    def product(left, right, then=()):
        left = after(both(left, 1 - is_first), *then)
        return jnp.dot(
            left.T, both(right, is_first), preferred_element_type=jnp.float32
        ).astype(jnp.bfloat16)

    def backward(moment, started=None):
        early, late = min(moment, micro_count - 1), max(moment - 1, 0)
        scalars = jnp.stack(
            [is_first, taken_slot(moment), choose(late, early)]
        )
        grad_res, grad_mixed = started or feed_back(
            store, slots, moment, scalars, arrived_grad[moment], cotangent[early], params
        )
        if moment == micro_count:
            lines = links()
            gate_part = product("normed_two", "grad_gate")
            gate_sum = Scatter(gate_part, lines)
            out_part = product("mixed", "grad_branch", then=(gate_part,))
            out_sum = Scatter(out_part, lines, along_first=True)
            up_part = product("normed_two", "grad_up", then=(out_part,))
            up_sum = Scatter(up_part, lines)
            gate_sum.cross(up_part)
            down_part = product("gated", "grad_result", then=(gate_sum.sent, out_sum.summed))
            down_sum = Scatter(down_part, lines)
            grad_mixed = after(grad_mixed, down_part, up_sum.level)
        center, top, bottom = attend_back(store, slots, moment, scalars, grad_mixed, bias)
        above = shifted(top, "seq", -1)
        below = shifted(bottom, "seq", 1)
        if moment == micro_count:
            up_sum.cross(above, below)
            gate_sum.add(center)
            center = after(center, gate_sum.level, down_sum.level)
            down_sum.cross(above, below)
            sums.update(lines=lines, gate=gate_sum, up=up_sum, down=down_sum, out=out_sum)
        (grad_source,) = project_back(
            store, slots, moment, scalars, center, below, above, grad_res, params
        )
        grad_sources.append(grad_source)
        if moment < micro_count:
            arrived_grad.append(shifted(grad_source, "section", -1))

    params, _ = forward(0, params)
    for moment in range(1, slots):
        _, started = forward(moment, params)
        backward(moment - 1, started)
    backward(micro_count)

    activations = jnp.stack(
        [
            jnp.where(is_first == 1, results[number], results[number + 1])
            for number in range(micro_count)
        ]
    )[None]
    input_grads = jnp.stack(
        [
            jnp.where(is_first == 1, grad_sources[number + 1], grad_sources[number])
            for number in range(micro_count)
        ]
    )[None]
    lines, gate_sum, up_sum, down_sum, out_sum = (
        sums[name] for name in ("lines", "gate", "up", "down", "out")
    )
    up_sum.add(grad_sources[-1])
    gain_rows = jnp.concatenate(
        [
            jnp.sum(lax.dynamic_slice_in_dim(store[name], is_first, micro_count, 0), 0)
            for name in ("gain_one", "gain_two")
        ]
    ).astype(jnp.bfloat16)
    picked = jnp.arange(2 * 8)[:, None] == jnp.arange(BLOCK)[None] * 8
    right = jnp.concatenate(
        [both(name, is_first) for name in ("grad_queries", "grad_keys", "grad_values")], 1
    )
    right = jnp.concatenate(
        [
            jnp.pad(right, ((0, 0), (0, BLOCK))),
            jnp.pad(picked.astype(jnp.bfloat16), ((0, 0), (right.shape[1], 0))),
        ]
    )
    left = after(jnp.concatenate([both("normed", 1 - is_first), gain_rows]), up_sum.level)
    qkv_part = jnp.dot(left.T, right, preferred_element_type=jnp.float32).astype(jnp.bfloat16)
    grad_up_w = up_sum.finish()
    down_sum.add(qkv_part, grad_up_w)
    qkv_all = ring_scatter(qkv_part, lines)
    grad_out_w = out_sum.cross().add().finish()
    grad_gate_w, grad_down_w = gate_sum.finish(), down_sum.finish()
    grad_query_w, grad_key_w, grad_value_w, gain_sum = (
        qkv_all[:, number * model_width : (number + 1) * model_width] for number in range(4)
    )
    return (
        activations,
        input_grads,
        gain_sum[:, 0][None],
        grad_query_w[None],
        grad_key_w[None],
        grad_value_w[None],
        grad_out_w[None],
        gain_sum[:, 1][None],
        grad_gate_w[None],
        grad_up_w[None],
        grad_down_w[None],
    )


def solution(mesh):
    placed = (
        P("wt", "seq", None),
        P("wt", None),
        P("wt", "seq", None),
        P("section", ("seq", "wt")),
        P("section", ("seq", "wt"), None),
        P("section", ("seq", "wt"), None),
        P("section", ("seq", "wt"), None),
        P("section", ("seq", "wt"), None),
        P("section", ("seq", "wt")),
        P("section", ("seq", "wt"), None),
        P("section", ("seq", "wt"), None),
        P("section", ("seq", "wt"), None),
    )
    return jax.shard_map(
        per_device,
        mesh=mesh,
        in_specs=placed,
        out_specs=(
            P("section", "wt", "seq", None),
            P("section", "wt", "seq", None),
            P("section", ("seq", "wt")),
            P("section", ("seq", "wt"), None),
            P("section", ("seq", "wt"), None),
            P("section", ("seq", "wt"), None),
            P("section", ("seq", "wt"), None),
            P("section", ("seq", "wt")),
            P("section", ("seq", "wt"), None),
            P("section", ("seq", "wt"), None),
            P("section", ("seq", "wt"), None),
        ),
        check_vma=False,
    )
```

```python
import functools

import jax
import jax.numpy as jnp
from jax import lax
from jax.experimental import pallas as pl
from jax.experimental.pallas import tpu as pltpu
from jax.sharding import PartitionSpec as P

HEAD_DIM = 64
RADIUS = 127


EPSILON = 1e-06


def shifted(shard, axis, by):
    length = lax.axis_size(axis)
    pairs = [(i, i + by) for i in range(length) if 0 <= i + by < length]
    return lax.ppermute(shard, axis, pairs)


HALO = 128
BLOCK = 128
WIDE = 256
BROAD = 512
NEVER = -1e30


def call(kernel, grid, scalars, ins, in_specs, outs, out_specs, scratch=(), aliases=None, cost=None):
    return pl.pallas_call(
        kernel,
        out_shape=outs,
        grid_spec=pltpu.PrefetchScalarGridSpec(
            num_scalar_prefetch=1,
            grid=grid,
            in_specs=in_specs,
            out_specs=out_specs,
            scratch_shapes=list(scratch),
        ),
        input_output_aliases=aliases or {},
        compiler_params=pltpu.CompilerParams(
            vmem_limit_bytes=56 * 2**20, dimension_semantics=("arbitrary",) * len(grid)
        ),
        cost_estimate=cost,
    )(scalars, *ins)


def cost_of(flops, moved, transcendentals=0):
    return pl.CostEstimate(
        flops=int(flops), bytes_accessed=int(moved), transcendentals=int(transcendentals)
    )


def nt_dot(left, right):
    return lax.dot_general(
        left, right, (((1,), (1,)), ((), ())), preferred_element_type=jnp.float32
    )


def tn_dot(left, right):
    return lax.dot_general(
        left, right, (((0,), (0,)), ((), ())), preferred_element_type=jnp.float32
    )


def dot(left, right):
    return jnp.dot(left, right, preferred_element_type=jnp.float32)


def inverse_rms(values):
    return lax.rsqrt(jnp.mean(values * values, axis=-1, keepdims=True) + EPSILON)


def flat(ref):
    cells = ref[...]
    return cells.reshape(-1, cells.shape[-1])


def packed_spec(packed, number, tile):
    rows = (packed.shape[1] - 16) // 4
    return pl.BlockSpec((packed.shape[0], rows, tile), lambda j, s: (0, number, j))


def project_kernel(idx, own, arrived, gain, wq, wk, wv, *rest):
    x_out, n_out, q_out, kv_out, tail_out, head_out = rest[-6:]

    @pl.when(pl.program_id(0) == 0)
    def _():
        picked = jnp.where(
            idx[0] == 1, own[...].astype(jnp.float32), arrived[...].astype(jnp.float32)
        )
        x_out[...] = picked.astype(jnp.bfloat16)
        n_out[...] = (picked * inverse_rms(picked) * gain[...].astype(jnp.float32)).astype(
            jnp.bfloat16
        )

    normed = n_out[...]
    kv_out[0] = dot(normed, flat(wk)).astype(jnp.bfloat16)
    kv_out[1] = dot(normed, flat(wv)).astype(jnp.bfloat16)
    q_out[...] = dot(normed, flat(wq)).astype(jnp.bfloat16)
    tail_out[...] = kv_out[:, pl.ds(kv_out.shape[1] - HALO, HALO)]
    head_out[...] = kv_out[:, pl.ds(0, HALO)]


def slot_call(kernel, grid, scalars, ins, in_specs, kept, fresh, store, slots, moment, scratch=(), cost=None):
    aliases, extra = {}, []
    outs, out_specs = [], []
    for name, shape, block, index, kind, *own in kept:
        slot = own[0] if own else moment
        outs.append(jax.ShapeDtypeStruct((slots,) + shape, kind))
        if block is None:
            out_specs.append(pl.BlockSpec(memory_space=pl.ANY))
        else:
            out_specs.append(
                pl.BlockSpec(
                    (None,) + block, lambda j, s, index=index, slot=slot: (slot,) + index(j)
                )
            )
        if name in store:
            aliases[1 + len(ins) + len(extra)] = len(outs) - 1
            extra.append(store[name])
    for shape, kind, spec in fresh:
        outs.append(jax.ShapeDtypeStruct(shape, kind))
        out_specs.append(spec)
    results = call(
        kernel,
        grid,
        scalars,
        list(ins) + extra,
        list(in_specs) + [pl.BlockSpec(memory_space=pl.ANY)] * len(extra),
        outs,
        out_specs,
        scratch,
        aliases,
        cost,
    )
    for (name, *_), value in zip(kept, results):
        store[name] = value
    return results[len(kept) :]


def whole_spec(shape):
    return pl.BlockSpec(shape, lambda j, s: (0,) * len(shape))


def project(store, slots, moment, scalars, own, arrived, params):
    rows, width = arrived.shape
    gain_one, packed = params[:2]
    tile = BROAD
    at_start = lambda j: (0, 0)
    halo_spec = pl.BlockSpec((2, HALO, tile), lambda j, s: (0, 0, j))
    return slot_call(
        project_kernel,
        (width // tile,),
        scalars,
        [own, arrived, gain_one, packed, packed, packed],
        [whole_spec((rows, width)), whole_spec((rows, width)), whole_spec((1, width))]
        + [packed_spec(packed, number, tile) for number in range(3)],
        [
            ("source", (rows, width), (rows, width), at_start, jnp.bfloat16),
            ("normed", (rows, width), (rows, width), at_start, jnp.bfloat16),
            ("queries", (rows, width), (rows, tile), lambda j: (0, j), jnp.bfloat16),
        ],
        [
            (
                (2, rows, width),
                jnp.bfloat16,
                pl.BlockSpec((2, rows, tile), lambda j, s: (0, 0, j)),
            ),
            ((2, HALO, width), jnp.bfloat16, halo_spec),
            ((2, HALO, width), jnp.bfloat16, halo_spec),
        ],
        store,
        slots,
        moment,
        cost=cost_of(6 * rows * width * width, 6 * width * width + 14 * rows * width),
    )


def row_blocks(rows):
    return [(start, min(BLOCK, rows - start)) for start in range(0, rows, BLOCK)]


def head_masks(kind):
    lane = lax.broadcasted_iota(jnp.int32, (1, 2 * HEAD_DIM), 1)
    low = (lane < HEAD_DIM).astype(kind)
    return (low, (1 - low).astype(kind))


def wide_tile(size):
    return max(tile for tile in range(128, 1409, 128) if size % tile == 0)


def chunks(size, tile):
    return [(start, min(tile, size - start)) for start in range(0, size, tile)]


def stacked_heads(pair):
    return jnp.concatenate([pair * mask for mask in head_masks(pair.dtype)], 0)


def unstacked_heads(stacked):
    rows = stacked.shape[0] // 2
    low = lax.broadcasted_iota(jnp.int32, (1, 2 * HEAD_DIM), 1) < HEAD_DIM
    return jnp.where(low, stacked[:rows], stacked[rows:])


def attend_step(q, kv, low, high, bias, wo, k_out, v_out, mixed_out, lse_out):
    rows = q.shape[0]
    for place, out in ((0, k_out), (1, v_out)):
        out[pl.ds(0, HALO)] = low[place]
        out[pl.ds(HALO, rows)] = kv[place]
        out[pl.ds(HALO + rows, HALO)] = high[place]
    scale = jnp.bfloat16(HEAD_DIM**-0.5)
    tiles = [
        (start, count, pair)
        for start, count in row_blocks(rows)
        for pair in range(WIDE // (2 * HEAD_DIM))
    ]
    sums = {}
    scores, powers, totals = {}, {}, {}
    for start, count, pair in tiles:
        span = count + 2 * HALO
        lanes = slice(pair * 2 * HEAD_DIM, (pair + 1) * 2 * HEAD_DIM)
        q_both = stacked_heads(q[pl.ds(start, count), lanes] * scale)
        block_bias = bias[pl.ds(start, count), :span]
        scores[start, pair] = nt_dot(
            q_both, k_out[pl.ds(start, span), lanes]
        ) + jnp.concatenate([block_bias, block_bias], 0)
    for start, count, pair in tiles:
        value = scores[start, pair]
        most = jnp.max(value, axis=-1, keepdims=True)
        power = jnp.exp(value - most)
        powers[start, pair] = power.astype(jnp.bfloat16)
        totals[start, pair] = jnp.sum(power, axis=-1, keepdims=True)
        log_sum = most + jnp.log(totals[start, pair])
        sums[start, pair] = (log_sum[:count], log_sum[count:])
    for start, count, pair in tiles:
        span = count + 2 * HALO
        lanes = slice(pair * 2 * HEAD_DIM, (pair + 1) * 2 * HEAD_DIM)
        mixed = dot(powers[start, pair], v_out[pl.ds(start, span), lanes])
        mixed = mixed * (1.0 / totals[start, pair])
        mixed_out[pl.ds(start, count), lanes] = unstacked_heads(mixed).astype(jnp.bfloat16)
    for start, count in row_blocks(rows):
        lane = lax.broadcasted_iota(jnp.int32, (count, 2 * HEAD_DIM), 1)
        wide = jnp.zeros((count, 2 * HEAD_DIM), jnp.float32)
        for pair in range(WIDE // (2 * HEAD_DIM)):
            for number, value in enumerate(sums[start, pair]):
                wide = jnp.where(lane == 2 * pair + number, value, wide)
        lse_out[pl.ds(start, count)] = wide
    return dot(mixed_out[...], flat(wo))


def attend_steps(parts, source, gain, res_out, two_out, total, steps):
    step = pl.program_id(0)

    @pl.when(step < steps)
    def _():
        part = attend_step(*parts)

        @pl.when(step == 0)
        def _():
            total[...] = source[...].astype(jnp.float32) + part

        @pl.when(step > 0)
        def _():
            total[...] += part

        @pl.when(step == steps - 1)
        def _():
            residual = total[...]
            res_out[...] = residual
            two_out[...] = (
                residual * inverse_rms(residual) * gain[...].astype(jnp.float32)
            ).astype(jnp.bfloat16)


def attend_kernel(steps, idx, q, kv, low, high, bias, wo, source, gain, *rest):
    k_out, v_out, mixed_out, lse_out, res_out, two_out, total = rest[-7:]
    parts = (q, kv, low, high, bias, wo, k_out, v_out, mixed_out, lse_out)
    attend_steps(parts, source, gain, res_out, two_out, total, steps)


class Feed:
    def __init__(self, moment, weights, outs, held, sems):
        self.moment, self.weights, self.outs, self.held, self.sems = (
            moment,
            weights,
            outs,
            held,
            sems,
        )
        size = weights[0].shape[1]
        self.tiles = chunks(size, wide_tile(size))

    def fetch(self, number, part):
        start, size = self.tiles[number]
        place = (slice(None), pl.ds(start, size)) if part < 2 else (pl.ds(start, size),)
        return pltpu.make_async_copy(
            self.weights[part].at[place], self.held[part].at[place], self.sems.at[3 * number + part]
        )

    def start(self):
        for number in range(len(self.tiles)):
            for part in range(3):
                self.fetch(number, part).start()

    def run(self, normed, total, result):
        gate_w, up_w, down_w = self.held[:3]
        stores = []
        for number, (start, size) in enumerate(self.tiles):
            lanes = slice(start, start + size)
            self.fetch(number, 0).wait()
            gate = dot(normed, gate_w[:, lanes])
            self.fetch(number, 1).wait()
            up = dot(normed, up_w[:, lanes])
            half, _, _ = gelu_parts(gate)
            gated = (gate * half * up).astype(jnp.bfloat16)
            values = (gate.astype(jnp.bfloat16), up.astype(jnp.bfloat16), gated)
            for part, value in enumerate(values):
                held = self.held[3 + part]
                held[:, lanes] = value
                copy = pltpu.make_async_copy(
                    held.at[:, pl.ds(start, size)],
                    self.outs[part].at[self.moment, :, pl.ds(start, size)],
                    self.sems.at[3 * len(self.tiles) + 3 * number + part],
                )
                copy.start()
                stores.append(copy)
            self.fetch(number, 2).wait()
            total[...] += dot(gated, down_w[lanes])
        result[...] = total[...].astype(jnp.bfloat16)
        for copy in stores:
            copy.wait()


def feed_kernel(moment, idx, two, residual, wg, wu, wd, *rest):
    outs, result, total, held, sems = rest[-12:-9], rest[-9], rest[-8], rest[-7:-1], rest[-1]
    feed = Feed(moment, (wg, wu, wd), outs, held, sems)
    feed.start()
    total[...] = residual[...]
    feed.run(two[...], total, result)


def attend_feed_kernel(
    moment, steps, idx, q, kv, low, high, bias, wo, source, gain, wg, wu, wd, *rest
):
    k_out, v_out, mixed_out, lse_out, res_out, two_out = rest[-18:-12]
    outs, result, total, held, sems = rest[-12:-9], rest[-9], rest[-8], rest[-7:-1], rest[-1]
    feed = Feed(moment, (wg, wu, wd), outs, held, sems)
    pl.when(pl.program_id(0) == 0)(feed.start)
    parts = (q, kv, low, high, bias, wo, k_out, v_out, mixed_out, lse_out)
    attend_steps(parts, source, gain, res_out, two_out, total, steps)

    @pl.when(pl.program_id(0) == steps)
    def _():
        feed.run(two_out[...], total, result)


def attend_feed_back_kernel(
    moment, steps, extras, idx, q, kv, low, high, bias, wo, source, gain, wg, wu, wd, *rest
):
    arrived, own, packed = rest[:3]
    older = rest[3 : 3 + extras]
    k_out, v_out, mixed_out, lse_out, res_out, two_out = rest[3 + extras : 9 + extras]
    outs, g_out = rest[9 + extras : 12 + extras], rest[12 + extras]
    grad_outs = rest[13 + extras : 15 + extras]
    branch_out, gain_out, result, grad_out, grad_mixed = rest[15 + extras : 20 + extras]
    total, held, sems = rest[20 + extras], rest[21 + extras : 27 + extras], rest[27 + extras]
    gate_back, up_back, res_back, dg_all, du_all, g_arrived, g_own, wo_all, more = rest[28 + extras :]
    feed = Feed(moment, (wg, wu, wd), outs, held, sems)
    taken = idx[1]
    shard = wo_all.shape[1]
    fixed = [
        (arrived, g_arrived),
        (own, g_own),
        (packed.at[:, pl.ds(3 * shard, shard)], wo_all),
    ]
    kept = [
        (older[6].at[taken], gate_back),
        (older[7].at[taken], up_back),
        (older[4].at[taken], res_back),
    ]

    def copy(number):
        here, there = (fixed + kept)[number]
        return pltpu.make_async_copy(here, there, more.at[number])

    @pl.when(pl.program_id(0) == 0)
    def _():
        feed.start()
        for number in range(3):
            copy(number).start()

        @pl.when(taken != moment)
        def _():
            for number in range(3, 6):
                copy(number).start()

    parts = (q, kv, low, high, bias, wo, k_out, v_out, mixed_out, lse_out)
    attend_steps(parts, source, gain, res_out, two_out, total, steps)

    @pl.when(pl.program_id(0) == steps)
    def _():
        feed.run(two_out[...], total, result)

        @pl.when(taken != moment)
        def _():
            for number in range(3, 6):
                copy(number).wait()

        @pl.when(taken == moment)
        def _():
            gate_back[...] = held[3][...]
            up_back[...] = held[4][...]
            res_back[...] = res_out[...]

        for number in range(3):
            copy(number).wait()
        grads = jnp.where(
            idx[0] == 1, g_arrived[...].astype(jnp.float32), g_own[...].astype(jnp.float32)
        ).astype(jnp.bfloat16)
        g_out[...] = grads
        gate_w, up_w, down_w = held[:3]
        stores = []
        for number, (start, size) in enumerate(feed.tiles):
            lanes = slice(start, start + size)
            grad_gate, grad_up = feed_grads(
                nt_dot(grads, down_w[lanes]), gate_back[:, lanes], up_back[:, lanes]
            )
            for part, (value, all_of) in enumerate(((grad_gate, dg_all), (grad_up, du_all))):
                all_of[:, lanes] = value
                store = pltpu.make_async_copy(
                    all_of.at[:, pl.ds(start, size)],
                    grad_outs[part].at[moment - 1, :, pl.ds(start, size)],
                    more.at[6 + 2 * number + part],
                )
                store.start()
                stores.append(store)
            part = nt_dot(grad_gate, gate_w[:, lanes]) + nt_dot(grad_up, up_w[:, lanes])
            if number:
                total[...] += part
            else:
                total[...] = part
        pulled, grad_gain = norm_back(
            total[...], res_back[...], gain[...].astype(jnp.float32)
        )
        gain_out[...] = jnp.broadcast_to(grad_gain, gain_out.shape)
        grad_residual = grads.astype(jnp.float32) + pulled
        grad_out[...] = grad_residual
        branch = grad_residual.astype(jnp.bfloat16)
        branch_out[...] = branch
        grad_mixed[...] = nt_dot(branch, flat(wo_all)).astype(jnp.bfloat16)
        for store in stores:
            store.wait()


def attend(store, slots, moment, scalars, kv, low, high, bias, params, back=None):
    rows, width = kv.shape[1:]
    packed, gain_two = params[1:3]
    weights = params[3:]
    shard = (packed.shape[1] - 16) // 4
    ext = rows + 2 * HALO
    quads = width // WIDE
    last = lambda j: jnp.minimum(j, quads - 1)
    at_start = lambda j: (0, 0)
    at_tile = lambda j: (0, last(j))
    halo_spec = pl.BlockSpec((2, HALO, WIDE), lambda j, s: (0, 0, last(j)))
    fed = feed_parts(rows, width, weights) if weights else ([], [], [], 0)
    kernel = functools.partial(attend_feed_kernel, moment) if weights else attend_kernel
    kernel = functools.partial(kernel, quads)
    back_ins, kept, fresh, scratch = [], [], [], []
    if back is not None:
        back_ins = [*back, packed]
        hidden = weights[0].shape[1]
        kept = [
            ("grad_result", (rows, width), (rows, width), at_start, jnp.bfloat16, moment - 1),
            ("grad_gate", (rows, hidden), None, None, jnp.bfloat16),
            ("grad_up", (rows, hidden), None, None, jnp.bfloat16),
            ("grad_branch", (rows, width), (rows, width), at_start, jnp.bfloat16, moment - 1),
            ("gain_two", (8, width), (8, width), at_start, jnp.float32, moment - 1),
        ]
        fresh = [
            ((rows, width), jnp.float32, whole_spec((rows, width))),
            ((rows, width), jnp.bfloat16, whole_spec((rows, width))),
        ]
        scratch = (
            [pltpu.VMEM((rows, hidden), jnp.bfloat16)] * 2
            + [pltpu.VMEM((rows, width), jnp.float32)]
            + [pltpu.VMEM((rows, hidden), jnp.bfloat16)] * 2
            + [pltpu.VMEM((rows, width), jnp.bfloat16)] * 2
            + [pltpu.VMEM((packed.shape[0], shard, width), jnp.bfloat16)]
            + [pltpu.SemaphoreType.DMA((6 + 2 * len(chunks(hidden, wide_tile(hidden))),))]
        )
        extras = 9 + sum(entry[0] in store for entry in kept)
        kernel = functools.partial(attend_feed_back_kernel, moment, quads, extras)
    return slot_call(
        kernel,
        (quads + (1 if weights else 0),),
        scalars,
        [store["queries"], kv, low, high, bias, packed, store["source"], gain_two]
        + [*weights, *back_ins],
        [
            pl.BlockSpec((None, rows, WIDE), lambda j, s: (moment, 0, last(j))),
            pl.BlockSpec((2, rows, WIDE), lambda j, s: (0, 0, last(j))),
            halo_spec,
            halo_spec,
            pl.BlockSpec((None,) + bias.shape[1:], lambda j, s: (s[2], 0, 0)),
            pl.BlockSpec((WIDE // shard, shard, width), lambda j, s: (last(j), 3, 0)),
            pl.BlockSpec((None, rows, width), lambda j, s: (moment, 0, 0)),
            whole_spec((1, width)),
        ]
        + [pl.BlockSpec(memory_space=pl.ANY)] * (len(weights) + len(back_ins)),
        [
            ("keys", (ext, width), (ext, WIDE), at_tile, jnp.bfloat16),
            ("values", (ext, width), (ext, WIDE), at_tile, jnp.bfloat16),
            ("mixed", (rows, width), (rows, WIDE), at_tile, jnp.bfloat16),
            ("lse", (rows, quads * BLOCK), (rows, BLOCK), at_tile, jnp.float32),
            ("residual", (rows, width), (rows, width), at_start, jnp.float32),
            ("normed_two", (rows, width), (rows, width), at_start, jnp.bfloat16),
        ]
        + fed[0]
        + kept,
        fed[1] + fresh,
        store,
        slots,
        moment,
        [pltpu.VMEM((rows, width), jnp.float32)] + fed[2] + scratch,
        cost_of(
            width * rows * ((BLOCK + 2 * HALO) * 8 + width * 2) + fed[3],
            2 * width * width + 20 * rows * width + fed[3] // rows,
        ),
    )


def feed_parts(rows, width, weights):
    hidden = weights[0].shape[1]
    tiles = len(chunks(hidden, wide_tile(hidden)))
    return (
        [(name, (rows, hidden), None, None, jnp.bfloat16) for name in ("gate", "up", "gated")],
        [((rows, width), jnp.bfloat16, whole_spec((rows, width)))],
        [pltpu.VMEM(weight.shape, jnp.bfloat16) for weight in weights]
        + [pltpu.VMEM((rows, hidden), jnp.bfloat16)] * 3
        + [pltpu.SemaphoreType.DMA((6 * tiles,))],
        6 * rows * width * hidden,
    )


def feed(store, slots, moment, scalars, params):
    weights = params[3:]
    rows, width = store["residual"].shape[1:]
    fed = feed_parts(rows, width, weights)
    return slot_call(
        functools.partial(feed_kernel, moment),
        (1,),
        scalars,
        [store["normed_two"], store["residual"], *weights],
        [pl.BlockSpec((None, rows, width), lambda j, s: (moment, 0, 0))] * 2
        + [pl.BlockSpec(memory_space=pl.ANY)] * 3,
        fed[0],
        fed[1],
        store,
        slots,
        moment,
        [pltpu.VMEM((rows, width), jnp.float32)] + fed[2],
        cost_of(fed[3], fed[3] // rows + 10 * rows * width),
    )


def gelu_parts(gate):
    root = 0.7978845608028654
    bend = jnp.tanh(root * (gate + 0.044715 * gate * gate * gate))
    return 0.5 * (1.0 + bend), bend, root


def feed_grads(grad_gated, gate, up):
    gate, up = gate.astype(jnp.float32), up.astype(jnp.float32)
    half, bend, root = gelu_parts(gate)
    slope = half + 0.5 * gate * (1.0 - bend * bend) * root * (1.0 + 3.0 * 0.044715 * gate * gate)
    return (
        (grad_gated * up * slope).astype(jnp.bfloat16),
        (grad_gated * gate * half).astype(jnp.bfloat16),
    )


def feed_back_kernel(idx, arrived, own, gate, up, residual, gain, wd, wg, wu, wo, *rest):
    g_out, dg_out, du_out, branch_out, gain_out, res_out, mixed_out, total = rest[-8:]
    step = pl.program_id(0)

    @pl.when(step == 0)
    def _():
        g_out[...] = jnp.where(
            idx[0] == 1, arrived[...].astype(jnp.float32), own[...].astype(jnp.float32)
        ).astype(jnp.bfloat16)

    grad_gated = nt_dot(g_out[...], wd[...])
    grad_gate, grad_up = feed_grads(grad_gated, gate[...], up[...])
    dg_out[...] = grad_gate
    du_out[...] = grad_up
    part = nt_dot(grad_gate, wg[...]) + nt_dot(grad_up, wu[...])

    @pl.when(step == 0)
    def _():
        total[...] = part

    @pl.when(step > 0)
    def _():
        total[...] += part

    @pl.when(step == pl.num_programs(0) - 1)
    def _():
        grads, grad_gain = norm_back(total[...], residual[...], gain[...].astype(jnp.float32))
        gain_out[...] = jnp.broadcast_to(grad_gain, gain_out.shape)
        grad_residual = g_out[...].astype(jnp.float32) + grads
        res_out[...] = grad_residual
        branch = grad_residual.astype(jnp.bfloat16)
        branch_out[...] = branch
        mixed_out[...] = nt_dot(branch, flat(wo)).astype(jnp.bfloat16)


def norm_back(grads, values, gain):
    scale = inverse_rms(values)
    pulled = grads * gain
    mean = jnp.mean(pulled * values, axis=-1, keepdims=True)
    return (
        scale * pulled - values * (scale * scale * scale * mean),
        jnp.sum(grads * values * scale, axis=0, keepdims=True),
    )


def feed_back(store, slots, moment, scalars, arrived, own, params):
    packed, gain_two, gate_w, up_w, down_w = params[1:]
    rows, width = arrived.shape
    hidden = gate_w.shape[1]
    tile = wide_tile(hidden)
    at_tile = lambda j: (0, j)
    at_start = lambda j: (0, 0)
    taken_tile = pl.BlockSpec((None, rows, tile), lambda j, s: (s[1], 0, j))
    return slot_call(
        feed_back_kernel,
        (hidden // tile,),
        scalars,
        [arrived, own, store["gate"], store["up"], store["residual"], gain_two]
        + [down_w, gate_w, up_w, packed],
        [whole_spec((rows, width)), whole_spec((rows, width)), taken_tile, taken_tile]
        + [pl.BlockSpec((None, rows, width), lambda j, s: (s[1], 0, 0)), whole_spec((1, width))]
        + [pl.BlockSpec((tile, width), lambda j, s: (j, 0))]
        + [pl.BlockSpec((width, tile), lambda j, s: (0, j))] * 2
        + [
            pl.BlockSpec(
                (packed.shape[0], (packed.shape[1] - 16) // 4, width), lambda j, s: (0, 3, 0)
            )
        ],
        [
            ("grad_result", (rows, width), (rows, width), at_start, jnp.bfloat16),
            ("grad_gate", (rows, hidden), (rows, tile), at_tile, jnp.bfloat16),
            ("grad_up", (rows, hidden), (rows, tile), at_tile, jnp.bfloat16),
            ("grad_branch", (rows, width), (rows, width), at_start, jnp.bfloat16),
            ("gain_two", (8, width), (8, width), at_start, jnp.float32),
        ],
        [
            ((rows, width), jnp.float32, whole_spec((rows, width))),
            ((rows, width), jnp.bfloat16, whole_spec((rows, width))),
        ],
        store,
        slots,
        moment,
        [pltpu.VMEM((rows, width), jnp.float32)],
        cost_of(6 * rows * width * hidden + 2 * rows * width * width, 6 * width * hidden),
    )


def attend_back_kernel(idx, q, keys, values, mixed, lse, grad_mixed, bias, *rest):
    q_out, center, top, bottom, k_total, v_total = rest[-6:]
    rows = q.shape[0]
    scale = jnp.bfloat16(HEAD_DIM**-0.5)
    k_total[...] = jnp.zeros_like(k_total)
    v_total[...] = jnp.zeros_like(v_total)
    tiles = [
        (start, count, slice(pair * 2 * HEAD_DIM, (pair + 1) * 2 * HEAD_DIM), pair)
        for start, count in row_blocks(rows)
        for pair in range(WIDE // (2 * HEAD_DIM))
    ]
    held = {}
    for start, count, lanes, pair in tiles:
        span = count + 2 * HALO
        q_both = stacked_heads(q[pl.ds(start, count), lanes] * scale)
        g_both = stacked_heads(grad_mixed[pl.ds(start, count), lanes])
        scores = nt_dot(q_both, keys[pl.ds(start, span), lanes])
        grad_probs = nt_dot(g_both, values[pl.ds(start, span), lanes])
        held[start, pair] = (q_both, g_both, scores, grad_probs)
    for start, count, lanes, pair in tiles:
        span = count + 2 * HALO
        q_both, g_both, scores, grad_probs = held[start, pair]
        block_bias = bias[pl.ds(start, count), :span]
        both_bias = jnp.concatenate([block_bias, block_bias], 0)
        m_pair = mixed[pl.ds(start, count), lanes].astype(jnp.float32)
        log_sum = jnp.concatenate(
            [lse[pl.ds(start, count), 2 * pair + n : 2 * pair + n + 1] for n in range(2)], 0
        )
        probs = jnp.exp(scores + (both_bias - log_sum))
        mean = jnp.sum(
            g_both.astype(jnp.float32) * jnp.concatenate([m_pair, m_pair], 0),
            axis=-1,
            keepdims=True,
        )
        grad_scores = (probs * (grad_probs - mean)).astype(jnp.bfloat16)
        held[start, pair] = (q_both, g_both, probs.astype(jnp.bfloat16), grad_scores)
    for start, count, lanes, pair in tiles:
        span = count + 2 * HALO
        q_both, g_both, probs, grad_scores = held[start, pair]
        grad_q = dot(grad_scores, keys[pl.ds(start, span), lanes])
        q_out[pl.ds(start, count), lanes] = (
            unstacked_heads(grad_q) * (HEAD_DIM**-0.5)
        ).astype(jnp.bfloat16)
        k_total[pl.ds(start, span), lanes] += tn_dot(grad_scores, q_both)
        v_total[pl.ds(start, span), lanes] += tn_dot(probs, g_both)
    for place, total in ((0, k_total), (1, v_total)):
        top[place] = total[pl.ds(0, HALO)].astype(jnp.bfloat16)
        center[place] = total[pl.ds(HALO, rows)]
        bottom[place] = total[pl.ds(HALO + rows, HALO)].astype(jnp.bfloat16)


def attend_back(store, slots, moment, scalars, grad_mixed, bias):
    rows, width = grad_mixed.shape
    ext = rows + 2 * HALO
    taken = pl.BlockSpec((None, rows, WIDE), lambda j, s: (s[1], 0, j))
    taken_ext = pl.BlockSpec((None, ext, WIDE), lambda j, s: (s[1], 0, j))
    halo_spec = pl.BlockSpec((2, HALO, WIDE), lambda j, s: (0, 0, j))
    work = width * rows * (BLOCK + 2 * HALO) * 2
    return slot_call(
        attend_back_kernel,
        (width // WIDE,),
        scalars,
        [store["queries"], store["keys"], store["values"], store["mixed"], store["lse"]]
        + [grad_mixed, bias],
        [
            taken,
            taken_ext,
            taken_ext,
            taken,
            pl.BlockSpec((None, rows, BLOCK), lambda j, s: (s[1], 0, j)),
            pl.BlockSpec((rows, WIDE), lambda j, s: (0, j)),
            pl.BlockSpec((None,) + bias.shape[1:], lambda j, s: (s[2], 0, 0)),
        ],
        [("grad_queries", (rows, width), (rows, WIDE), lambda j: (0, j), jnp.bfloat16)],
        [
            (
                (2, rows, width),
                jnp.float32,
                pl.BlockSpec((2, rows, WIDE), lambda j, s: (0, 0, j)),
            ),
            ((2, HALO, width), jnp.bfloat16, halo_spec),
            ((2, HALO, width), jnp.bfloat16, halo_spec),
        ],
        store,
        slots,
        moment,
        [pltpu.VMEM((ext, WIDE), jnp.float32)] * 2,
        cost_of(work * 20, 24 * rows * width),
    )


def project_back_kernel(
    idx, grad_q, center, below, above, source, gain, grad_res, wq, wk, wv, *rest
):
    k_out, v_out, gain_out, in_out, total = rest[-5:]
    step = pl.program_id(0)
    rows = source.shape[0]
    for place, out in ((0, k_out), (1, v_out)):
        head = center[place, pl.ds(0, HALO)] + below[place].astype(jnp.float32)
        tail = center[place, pl.ds(rows - HALO, HALO)] + above[place].astype(jnp.float32)
        out[pl.ds(0, HALO)] = head.astype(jnp.bfloat16)
        out[pl.ds(HALO, rows - 2 * HALO)] = center[place, pl.ds(HALO, rows - 2 * HALO)].astype(
            jnp.bfloat16
        )
        out[pl.ds(rows - HALO, HALO)] = tail.astype(jnp.bfloat16)
    part = nt_dot(grad_q[...], flat(wq))
    part += nt_dot(k_out[...], flat(wk)) + nt_dot(v_out[...], flat(wv))

    @pl.when(step == 0)
    def _():
        total[...] = part

    @pl.when(step > 0)
    def _():
        total[...] += part

    @pl.when(step == pl.num_programs(0) - 1)
    def _():
        grads, grad_gain = norm_back(
            total[...], source[...].astype(jnp.float32), gain[...].astype(jnp.float32)
        )
        gain_out[...] = jnp.broadcast_to(grad_gain, gain_out.shape)
        in_out[...] = (grad_res[...] + grads).astype(jnp.bfloat16)


def project_back(store, slots, moment, scalars, center, below, above, grad_res, params):
    rows, width = grad_res.shape
    gain_one, packed = params[:2]
    at_tile = lambda j: (0, j)
    at_start = lambda j: (0, 0)
    halo_spec = pl.BlockSpec((2, HALO, BROAD), lambda j, s: (0, 0, j))
    return slot_call(
        project_back_kernel,
        (width // BROAD,),
        scalars,
        [store["grad_queries"], center, below, above, store["source"], gain_one, grad_res]
        + [packed] * 3,
        [
            pl.BlockSpec((None, rows, BROAD), lambda j, s: (moment, 0, j)),
            pl.BlockSpec((2, rows, BROAD), lambda j, s: (0, 0, j)),
            halo_spec,
            halo_spec,
            pl.BlockSpec((None, rows, width), lambda j, s: (s[1], 0, 0)),
            whole_spec((1, width)),
            whole_spec((rows, width)),
        ]
        + [packed_spec(packed, number, BROAD) for number in range(3)],
        [
            ("grad_keys", (rows, width), (rows, BROAD), at_tile, jnp.bfloat16),
            ("grad_values", (rows, width), (rows, BROAD), at_tile, jnp.bfloat16),
            ("gain_one", (8, width), (8, width), at_start, jnp.float32),
        ],
        [((rows, width), jnp.bfloat16, whole_spec((rows, width)))],
        store,
        slots,
        moment,
        [pltpu.VMEM((rows, width), jnp.float32)],
        cost_of(6 * rows * width * width, 6 * width * width + 20 * rows * width),
    )


def window_bias(lengths_row, shard_no, rows, seq_len):
    ends = jnp.cumsum(lengths_row)
    first = shard_no * rows
    row = jnp.arange(rows, dtype=jnp.int32)
    place = (row // BLOCK * BLOCK)[:, None] - HALO + jnp.arange(BLOCK + 2 * HALO, dtype=jnp.int32)

    def document(position):
        return jnp.sum((position[..., None] >= ends).astype(jnp.int32), axis=-1)

    key = first + place
    allowed = (
        (jnp.abs(row[:, None] - place) <= RADIUS)
        & (key >= 0)
        & (key < seq_len)
        & (document(first + row)[:, None] == document(key))
    )
    return jnp.where(allowed, 0.0, NEVER).astype(jnp.float32)


def after(cells, *others):
    return lax.optimization_barrier((cells,) + others)[0] if others else cells


class Link:
    def __init__(self, axis, pairs, depth):
        self.axis, self.pairs, self.depth, self.sent = axis, pairs, depth, []

    def __call__(self, cells, depth=None):
        depth = self.depth if depth is None else depth
        if depth and len(self.sent) >= depth:
            cells = after(cells, self.sent[-depth])
        self.sent.append(lax.ppermute(cells, self.axis, self.pairs))
        return self.sent[-1]


def links(depth=2):
    span = lax.axis_size("seq")
    high = span // 2
    across = [(h * 2 + c, ((h + 1) % high) * 2 + c) for h in range(high) for c in range(2)]
    pairs = [(i, i ^ 1) for i in range(span)]
    rings = lax.axis_size("wt")
    along = [(i, (i + 1) % rings) for i in range(rings)]
    return Link("seq", across, depth), Link("seq", pairs, 0), Link("wt", along, 0)


def places():
    high = lax.axis_size("seq") // 2
    shard_no = lax.axis_index("seq")
    return high, shard_no // 2, shard_no % 2


class Gather:
    def __init__(self, shard, lines):
        self.across, self.swap = lines[:2]
        self.level = lax.all_gather(shard, "wt", axis=0)

    def cross(self, *others):
        self.row = [after(self.level, *others)]
        for _ in range(1, lax.axis_size("seq") // 2):
            self.row.append(self.across(self.row[-1]))
        return self

    def pieces(self, *others):
        found = {}
        for j, part in enumerate(self.row):
            part = after(part, *others) if j else part
            found[(None, j, 0)] = part
            found[(None, j, 1)] = self.swap(part)
        return found


def ring_gather(shard, lines, between):
    across, swap, along = lines
    found, current = {}, shard
    for k in range(lax.axis_size("wt")):
        current = along(current) if k else current
        if k == lax.axis_size("wt") - 1:
            between()
        cells = current
        for j in range(lax.axis_size("seq") // 2):
            if j:
                cells = across(cells, 1) if k == lax.axis_size("wt") - 1 else across(cells)
            found[(k, j, 0)] = cells
            found[(k, j, 1)] = swap(cells)
    return found


def assemble_kernel(count, plan, seat_ref, *refs):
    parts, wholes, sems = refs[:count], refs[count:-1], refs[-1]
    copies = []
    for number, (source, start, rows, seat, ring, whole, to) in enumerate(plan):
        there = wholes[whole].at[seat_ref[seat]]
        if ring is None:
            here, there = parts[source].at[:, pl.ds(start, rows)], there.at[:, pl.ds(to, rows)]
        else:
            here = parts[source].at[pl.ds(start, rows)]
            there = there.at[seat_ref[ring], pl.ds(to, rows)]
        copies.append(pltpu.make_async_copy(here, there, sems.at[number]))
    for copy in copies:
        copy.start()
    for copy in copies:
        copy.wait()


def assemble(pieces, pack):
    high, h, c = places()
    rings, z = lax.axis_size("wt"), lax.axis_index("wt")
    seats = [
        lax.rem(h - j + high, high) * 2 + (c + p) % 2 for j in range(high) for p in range(2)
    ] + [lax.rem(z - k + rings, rings) for k in range(rings)]
    sources, plan = [], []
    for (k, j, p), part in pieces.items():
        start = 0
        for whole, rows in enumerate(pack):
            ring = None if k is None else 2 * high + k
            plan.append((len(sources), start, rows, j * 2 + p, ring, whole, 0))
            start += rows
        sources.append(part)
    width, kind = sources[0].shape[-1], sources[0].dtype
    shapes = [(2 * high, rings, rows, width) for rows in pack]
    if any(rows % 16 for rows in pack):
        wholes = [jnp.zeros(shape, kind) for shape in shapes]
        for source, start, rows, seat, ring, whole, to in plan:
            part = sources[source]
            part = part[None] if ring is None else part[None, None]
            part = part[:, :, start : start + rows]
            place = (seats[seat], 0 if ring is None else seats[ring], to, 0)
            wholes[whole] = lax.dynamic_update_slice(wholes[whole], part, place)
    else:
        wholes = pl.pallas_call(
            functools.partial(assemble_kernel, len(sources), plan),
            out_shape=[jax.ShapeDtypeStruct(shape, kind) for shape in shapes],
            grid_spec=pltpu.PrefetchScalarGridSpec(
                num_scalar_prefetch=1,
                grid=(),
                in_specs=[pl.BlockSpec(memory_space=pl.ANY)] * len(sources),
                out_specs=[pl.BlockSpec(memory_space=pltpu.VMEM)] * len(shapes),
                scratch_shapes=[pltpu.SemaphoreType.DMA((len(plan),))],
            ),
            compiler_params=pltpu.CompilerParams(vmem_limit_bytes=40 * 2**20),
            cost_estimate=cost_of(0, 2 * sum(source.size * 2 for source in sources)),
        )(jnp.stack(seats).astype(jnp.int32), *sources)
    return [whole.reshape(-1, width) for whole in wholes]


def plus(left, right, kind):
    return (left.astype(jnp.float32) + right.astype(jnp.float32)).astype(kind)


class Scatter:
    def __init__(self, partial, lines, kind=jnp.bfloat16, along_first=False):
        self.across, self.swap = lines[:2]
        self.kind, self.along_first = kind, along_first
        high, h, c = places()
        self.high, self.h = high, h
        cells = partial.reshape(high, 2, -1, partial.shape[-1])
        self.mine = lax.dynamic_index_in_dim(cells, c, 1, False)
        self.received = self.swap(lax.dynamic_index_in_dim(cells, 1 - c, 1, False))
        if along_first:
            rows = self.mine.shape[1]
            rings = lax.axis_size("wt")
            whole = plus(self.mine, self.received, kind)
            whole = whole.reshape(high, rings, rows // rings, -1).swapaxes(0, 1)
            self.summed = whole.reshape(high * rows, -1)
            summed = lax.psum_scatter(self.summed, "wt", scatter_dimension=0, tiled=True)
            self.mine = summed.reshape(high, rows // rings, -1)
            self.level = None
        else:
            self.level = self.block(1)

    def block(self, j):
        place = lax.rem(self.h - j + self.high, self.high)
        mine = lax.dynamic_index_in_dim(self.mine, place, 0, False)
        if self.along_first:
            return mine
        return plus(mine, lax.dynamic_index_in_dim(self.received, place, 0, False), self.kind)

    def cross(self, *others):
        self.level = self.block(1) if self.level is None else self.level
        self.sent = after(self.level, *others)
        self.arrived = self.across(self.sent)
        return self

    def add(self, *others):
        level = self.arrived
        for j in range(2, self.high + 1):
            level = plus(after(level, *others), self.block(j), self.kind)
            if j < self.high:
                level = self.across(level)
        self.level = level
        return self

    def finish(self):
        level = self.level
        if not self.along_first:
            level = lax.psum_scatter(level, "wt", scatter_dimension=0, tiled=True)
        return level.astype(jnp.float32)


def ring_scatter(partial, lines):
    across, swap, along = lines
    high, h, c = places()
    rings, z = lax.axis_size("wt"), lax.axis_index("wt")
    cells = partial.reshape(high, 2, rings, -1, partial.shape[-1])
    mine = lax.dynamic_index_in_dim(cells, c, 1, False)
    received = swap(lax.dynamic_index_in_dim(cells, 1 - c, 1, False))
    size = (1, 1) + cells.shape[3:]

    def block(j, k):
        place = (lax.rem(h - j + high, high), lax.rem(z - k + rings, rings), 0, 0)
        return plus(
            lax.dynamic_slice(mine, place, size)[0, 0],
            lax.dynamic_slice(received, place, size)[0, 0],
            jnp.bfloat16,
        )

    total = None
    for k in range(1, rings + 1):
        level = block(1, k)
        for j in range(2, high + 1):
            level = plus(across(level), block(j, k), jnp.bfloat16)
        if total is None:
            total = level
        else:
            total = plus(along(total), level, jnp.float32 if k == rings else jnp.bfloat16)
    return total.astype(jnp.float32)


def per_device(
    inputs,
    lengths,
    cotangent,
    gain_attn,
    w_query,
    w_key,
    w_value,
    w_out,
    gain_mlp,
    w_gate,
    w_up,
    w_down,
):
    section_no = lax.axis_index("section")
    shard_no = lax.axis_index("seq")
    micro_count, rows_local, model_width = inputs.shape
    seq_len = rows_local * lax.axis_size("seq")
    is_first = (section_no == 0).astype(jnp.int32)
    slots = micro_count + 1
    bias = jnp.stack(
        [
            window_bias(lengths[number], shard_no, rows_local, seq_len)
            for number in range(micro_count)
        ]
    )

    def choose(of_first, of_second):
        return is_first * of_first + (1 - is_first) * of_second

    rows = w_query.shape[1]
    gains = jnp.pad(
        jnp.concatenate([gain_attn, gain_mlp], 1), ((0, 15), (0, model_width - 2 * rows))
    )
    lines = links()
    narrow = jnp.concatenate([w_query[0], w_key[0], w_value[0], w_out[0], gains], 0)
    gate_gather = Gather(w_gate[0], lines)
    up_gather = Gather(w_up[0], lines)
    down_gather = Gather(w_down[0], lines)
    pieces = ring_gather(narrow, lines, gate_gather.cross)
    (packed,) = assemble(pieces, [narrow.shape[0]])
    packed = packed.reshape(-1, narrow.shape[0], model_width)
    gain_rows = packed[:, 4 * rows]
    gain_one = gain_rows[:, :rows].reshape(1, -1)
    gain_two = gain_rows[:, rows : 2 * rows].reshape(1, -1)
    params = (gain_one, packed, gain_two)

    store, results, grad_sources, sums = {}, [], [], {}
    arrived = [jnp.zeros((rows_local, model_width), jnp.bfloat16)]
    arrived_grad = [arrived[0]]

    def taken_slot(moment):
        return choose(max(moment - 1, 0), min(moment + 1, micro_count))

    def forward(moment, params):
        early, late = min(moment, micro_count - 1), max(moment - 1, 0)
        scalars = jnp.stack([is_first, taken_slot(moment - 1), choose(early, late)])
        started = None
        layer_in = after(arrived[moment], *grad_sources[-1:])
        kv, tail, head = project(store, slots, moment, scalars, inputs[early], layer_in, params)
        low = shifted(tail, "seq", 1)
        high = shifted(head, "seq", -1)
        if moment == 0:
            up_gather.cross()
            down_gather.cross(low, high)
            kv = after(kv, up_gather.row[-1])
            attend(store, slots, moment, scalars, kv, low, high, bias, params)
            two = store["normed_two"]
            (gate_w,) = assemble(gate_gather.pieces(kv), [rows])
            (up_w,) = assemble(up_gather.pieces(kv), [rows])
            (down_w,) = assemble(down_gather.pieces(two, gate_w, up_w), [w_down.shape[1]])
            params = params + (gate_w, up_w, down_w)
            (result,) = feed(store, slots, moment, scalars, params)
        else:
            back = (arrived_grad[moment - 1], cotangent[min(moment - 1, micro_count - 1)])
            result, *started = attend(
                store, slots, moment, scalars, kv, low, high, bias, params, back
            )
        results.append(result)
        if moment < micro_count:
            arrived.append(shifted(result, "section", 1))
        return params, started

    def both(name, start):
        chosen = lax.dynamic_slice_in_dim(store[name], start, micro_count, 0)
        return chosen.reshape(-1, chosen.shape[-1])

    def product(left, right, then=()):
        left = after(both(left, 1 - is_first), *then)
        return jnp.dot(
            left.T, both(right, is_first), preferred_element_type=jnp.float32
        ).astype(jnp.bfloat16)

    def backward(moment, started=None):
        early, late = min(moment, micro_count - 1), max(moment - 1, 0)
        scalars = jnp.stack(
            [is_first, taken_slot(moment), choose(late, early)]
        )
        grad_res, grad_mixed = started or feed_back(
            store, slots, moment, scalars, arrived_grad[moment], cotangent[early], params
        )
        if moment == micro_count:
            lines = links()
            gate_part = product("normed_two", "grad_gate")
            gate_sum = Scatter(gate_part, lines)
            out_part = product("mixed", "grad_branch", then=(gate_part,))
            out_sum = Scatter(out_part, lines, along_first=True)
            up_part = product("normed_two", "grad_up", then=(out_part,))
            up_sum = Scatter(up_part, lines)
            gate_sum.cross(up_part)
            down_part = product("gated", "grad_result", then=(gate_sum.sent, out_sum.summed))
            down_sum = Scatter(down_part, lines)
            grad_mixed = after(grad_mixed, down_part, up_sum.level)
        center, top, bottom = attend_back(store, slots, moment, scalars, grad_mixed, bias)
        above = shifted(top, "seq", -1)
        below = shifted(bottom, "seq", 1)
        if moment == micro_count:
            up_sum.cross(above, below)
            gate_sum.add(center)
            center = after(center, gate_sum.level, down_sum.level)
            down_sum.cross(above, below)
            sums.update(lines=lines, gate=gate_sum, up=up_sum, down=down_sum, out=out_sum)
        (grad_source,) = project_back(
            store, slots, moment, scalars, center, below, above, grad_res, params
        )
        grad_sources.append(grad_source)
        if moment < micro_count:
            arrived_grad.append(shifted(grad_source, "section", -1))

    params, _ = forward(0, params)
    for moment in range(1, slots):
        _, started = forward(moment, params)
        backward(moment - 1, started)
    backward(micro_count)

    activations = jnp.stack(
        [
            jnp.where(is_first == 1, results[number], results[number + 1])
            for number in range(micro_count)
        ]
    )[None]
    input_grads = jnp.stack(
        [
            jnp.where(is_first == 1, grad_sources[number + 1], grad_sources[number])
            for number in range(micro_count)
        ]
    )[None]
    lines, gate_sum, up_sum, down_sum, out_sum = (
        sums[name] for name in ("lines", "gate", "up", "down", "out")
    )
    up_sum.add(grad_sources[-1])
    gain_rows = jnp.concatenate(
        [
            jnp.sum(lax.dynamic_slice_in_dim(store[name], is_first, micro_count, 0), 0)
            for name in ("gain_one", "gain_two")
        ]
    ).astype(jnp.bfloat16)
    picked = jnp.arange(2 * 8)[:, None] == jnp.arange(BLOCK)[None] * 8
    right = jnp.concatenate(
        [both(name, is_first) for name in ("grad_queries", "grad_keys", "grad_values")], 1
    )
    right = jnp.concatenate(
        [
            jnp.pad(right, ((0, 0), (0, BLOCK))),
            jnp.pad(picked.astype(jnp.bfloat16), ((0, 0), (right.shape[1], 0))),
        ]
    )
    left = after(jnp.concatenate([both("normed", 1 - is_first), gain_rows]), up_sum.level)
    qkv_part = jnp.dot(left.T, right, preferred_element_type=jnp.float32).astype(jnp.bfloat16)
    grad_up_w = up_sum.finish()
    down_sum.add(qkv_part, grad_up_w)
    qkv_all = ring_scatter(qkv_part, lines)
    grad_out_w = out_sum.cross().add().finish()
    grad_gate_w, grad_down_w = gate_sum.finish(), down_sum.finish()
    grad_query_w, grad_key_w, grad_value_w, gain_sum = (
        qkv_all[:, number * model_width : (number + 1) * model_width] for number in range(4)
    )
    return (
        activations,
        input_grads,
        gain_sum[:, 0][None],
        grad_query_w[None],
        grad_key_w[None],
        grad_value_w[None],
        grad_out_w[None],
        gain_sum[:, 1][None],
        grad_gate_w[None],
        grad_up_w[None],
        grad_down_w[None],
    )


def solution(mesh):
    placed = (
        P("wt", "seq", None),
        P("wt", None),
        P("wt", "seq", None),
        P("section", ("seq", "wt")),
        P("section", ("seq", "wt"), None),
        P("section", ("seq", "wt"), None),
        P("section", ("seq", "wt"), None),
        P("section", ("seq", "wt"), None),
        P("section", ("seq", "wt")),
        P("section", ("seq", "wt"), None),
        P("section", ("seq", "wt"), None),
        P("section", ("seq", "wt"), None),
    )
    return jax.shard_map(
        per_device,
        mesh=mesh,
        in_specs=placed,
        out_specs=(
            P("section", "wt", "seq", None),
            P("section", "wt", "seq", None),
            P("section", ("seq", "wt")),
            P("section", ("seq", "wt"), None),
            P("section", ("seq", "wt"), None),
            P("section", ("seq", "wt"), None),
            P("section", ("seq", "wt"), None),
            P("section", ("seq", "wt")),
            P("section", ("seq", "wt"), None),
            P("section", ("seq", "wt"), None),
            P("section", ("seq", "wt"), None),
        ),
        check_vma=False,
    )
```

```python
import functools

import jax
import jax.numpy as jnp
from jax import lax
from jax.experimental import pallas as pl
from jax.experimental.pallas import tpu as pltpu
from jax.sharding import PartitionSpec as P

HEAD_DIM = 64
RADIUS = 127


EPSILON = 1e-06


def shifted(shard, axis, by):
    length = lax.axis_size(axis)
    pairs = [(i, i + by) for i in range(length) if 0 <= i + by < length]
    return lax.ppermute(shard, axis, pairs)


HALO = 128
BLOCK = 128
WIDE = 256
BROAD = 512
NEVER = -1e30


def call(kernel, grid, scalars, ins, in_specs, outs, out_specs, scratch=(), aliases=None, cost=None):
    return pl.pallas_call(
        kernel,
        out_shape=outs,
        grid_spec=pltpu.PrefetchScalarGridSpec(
            num_scalar_prefetch=1,
            grid=grid,
            in_specs=in_specs,
            out_specs=out_specs,
            scratch_shapes=list(scratch),
        ),
        input_output_aliases=aliases or {},
        compiler_params=pltpu.CompilerParams(
            vmem_limit_bytes=56 * 2**20, dimension_semantics=("arbitrary",) * len(grid)
        ),
        cost_estimate=cost,
    )(scalars, *ins)


def cost_of(flops, moved, transcendentals=0):
    return pl.CostEstimate(
        flops=int(flops), bytes_accessed=int(moved), transcendentals=int(transcendentals)
    )


def nt_dot(left, right):
    return lax.dot_general(
        left, right, (((1,), (1,)), ((), ())), preferred_element_type=jnp.float32
    )


def tn_dot(left, right):
    return lax.dot_general(
        left, right, (((0,), (0,)), ((), ())), preferred_element_type=jnp.float32
    )


def dot(left, right):
    return jnp.dot(left, right, preferred_element_type=jnp.float32)


def inverse_rms(values):
    return lax.rsqrt(jnp.mean(values * values, axis=-1, keepdims=True) + EPSILON)


def flat(ref):
    cells = ref[...]
    return cells.reshape(-1, cells.shape[-1])


def packed_spec(packed, number, tile):
    rows = (packed.shape[1] - 16) // 4
    return pl.BlockSpec((packed.shape[0], rows, tile), lambda j, s: (0, number, j))


def project_kernel(idx, own, arrived, gain, wq, wk, wv, *rest):
    x_out, n_out, q_out, kv_out, tail_out, head_out = rest[-6:]

    @pl.when(pl.program_id(0) == 0)
    def _():
        picked = jnp.where(
            idx[0] == 1, own[...].astype(jnp.float32), arrived[...].astype(jnp.float32)
        )
        x_out[...] = picked.astype(jnp.bfloat16)
        n_out[...] = (picked * inverse_rms(picked) * gain[...].astype(jnp.float32)).astype(
            jnp.bfloat16
        )

    normed = n_out[...]
    kv_out[0] = dot(normed, flat(wk)).astype(jnp.bfloat16)
    kv_out[1] = dot(normed, flat(wv)).astype(jnp.bfloat16)
    q_out[...] = dot(normed, flat(wq)).astype(jnp.bfloat16)
    tail_out[...] = kv_out[:, pl.ds(kv_out.shape[1] - HALO, HALO)]
    head_out[...] = kv_out[:, pl.ds(0, HALO)]


def slot_call(kernel, grid, scalars, ins, in_specs, kept, fresh, store, slots, moment, scratch=(), cost=None):
    aliases, extra = {}, []
    outs, out_specs = [], []
    for name, shape, block, index, kind, *own in kept:
        slot = own[0] if own else moment
        outs.append(jax.ShapeDtypeStruct((slots,) + shape, kind))
        if block is None:
            out_specs.append(pl.BlockSpec(memory_space=pl.ANY))
        else:
            out_specs.append(
                pl.BlockSpec(
                    (None,) + block, lambda j, s, index=index, slot=slot: (slot,) + index(j)
                )
            )
        if name in store:
            aliases[1 + len(ins) + len(extra)] = len(outs) - 1
            extra.append(store[name])
    for shape, kind, spec in fresh:
        outs.append(jax.ShapeDtypeStruct(shape, kind))
        out_specs.append(spec)
    results = call(
        kernel,
        grid,
        scalars,
        list(ins) + extra,
        list(in_specs) + [pl.BlockSpec(memory_space=pl.ANY)] * len(extra),
        outs,
        out_specs,
        scratch,
        aliases,
        cost,
    )
    for (name, *_), value in zip(kept, results):
        store[name] = value
    return results[len(kept) :]


def whole_spec(shape):
    return pl.BlockSpec(shape, lambda j, s: (0,) * len(shape))


def project(store, slots, moment, scalars, own, arrived, params):
    rows, width = arrived.shape
    gain_one, packed = params[:2]
    tile = BROAD
    at_start = lambda j: (0, 0)
    halo_spec = pl.BlockSpec((2, HALO, tile), lambda j, s: (0, 0, j))
    return slot_call(
        project_kernel,
        (width // tile,),
        scalars,
        [own, arrived, gain_one, packed, packed, packed],
        [whole_spec((rows, width)), whole_spec((rows, width)), whole_spec((1, width))]
        + [packed_spec(packed, number, tile) for number in range(3)],
        [
            ("source", (rows, width), (rows, width), at_start, jnp.bfloat16),
            ("normed", (rows, width), (rows, width), at_start, jnp.bfloat16),
            ("queries", (rows, width), (rows, tile), lambda j: (0, j), jnp.bfloat16),
        ],
        [
            (
                (2, rows, width),
                jnp.bfloat16,
                pl.BlockSpec((2, rows, tile), lambda j, s: (0, 0, j)),
            ),
            ((2, HALO, width), jnp.bfloat16, halo_spec),
            ((2, HALO, width), jnp.bfloat16, halo_spec),
        ],
        store,
        slots,
        moment,
        cost=cost_of(6 * rows * width * width, 6 * width * width + 14 * rows * width),
    )


def row_blocks(rows):
    return [(start, min(BLOCK, rows - start)) for start in range(0, rows, BLOCK)]


def head_masks(kind):
    lane = lax.broadcasted_iota(jnp.int32, (1, 2 * HEAD_DIM), 1)
    low = (lane < HEAD_DIM).astype(kind)
    return (low, (1 - low).astype(kind))


def wide_tile(size):
    return max(tile for tile in range(128, 1409, 128) if size % tile == 0)


def chunks(size, tile):
    return [(start, min(tile, size - start)) for start in range(0, size, tile)]


def stacked_heads(pair):
    return jnp.concatenate([pair * mask for mask in head_masks(pair.dtype)], 0)


def unstacked_heads(stacked):
    rows = stacked.shape[0] // 2
    low = lax.broadcasted_iota(jnp.int32, (1, 2 * HEAD_DIM), 1) < HEAD_DIM
    return jnp.where(low, stacked[:rows], stacked[rows:])


def attend_step(q, kv, low, high, bias, wo, k_out, v_out, mixed_out, lse_out):
    rows = q.shape[0]
    for place, out in ((0, k_out), (1, v_out)):
        out[pl.ds(0, HALO)] = low[place]
        out[pl.ds(HALO, rows)] = kv[place]
        out[pl.ds(HALO + rows, HALO)] = high[place]
    scale = jnp.bfloat16(HEAD_DIM**-0.5)
    tiles = [
        (start, count, pair)
        for start, count in row_blocks(rows)
        for pair in range(WIDE // (2 * HEAD_DIM))
    ]
    sums = {}
    scores, powers, totals = {}, {}, {}
    for start, count, pair in tiles:
        span = count + 2 * HALO
        lanes = slice(pair * 2 * HEAD_DIM, (pair + 1) * 2 * HEAD_DIM)
        q_both = stacked_heads(q[pl.ds(start, count), lanes] * scale)
        block_bias = bias[pl.ds(start, count), :span]
        scores[start, pair] = nt_dot(
            q_both, k_out[pl.ds(start, span), lanes]
        ) + jnp.concatenate([block_bias, block_bias], 0)
    for start, count, pair in tiles:
        value = scores[start, pair]
        most = jnp.max(value, axis=-1, keepdims=True)
        power = jnp.exp(value - most)
        powers[start, pair] = power.astype(jnp.bfloat16)
        totals[start, pair] = jnp.sum(power, axis=-1, keepdims=True)
        log_sum = most + jnp.log(totals[start, pair])
        sums[start, pair] = (log_sum[:count], log_sum[count:])
    for start, count, pair in tiles:
        span = count + 2 * HALO
        lanes = slice(pair * 2 * HEAD_DIM, (pair + 1) * 2 * HEAD_DIM)
        mixed = dot(powers[start, pair], v_out[pl.ds(start, span), lanes])
        mixed = mixed * (1.0 / totals[start, pair])
        mixed_out[pl.ds(start, count), lanes] = unstacked_heads(mixed).astype(jnp.bfloat16)
    for start, count in row_blocks(rows):
        lane = lax.broadcasted_iota(jnp.int32, (count, 2 * HEAD_DIM), 1)
        wide = jnp.zeros((count, 2 * HEAD_DIM), jnp.float32)
        for pair in range(WIDE // (2 * HEAD_DIM)):
            for number, value in enumerate(sums[start, pair]):
                wide = jnp.where(lane == 2 * pair + number, value, wide)
        lse_out[pl.ds(start, count)] = wide
    return dot(mixed_out[...], flat(wo))


def attend_steps(parts, source, gain, res_out, two_out, total, steps):
    step = pl.program_id(0)

    @pl.when(step < steps)
    def _():
        part = attend_step(*parts)

        @pl.when(step == 0)
        def _():
            total[...] = source[...].astype(jnp.float32) + part

        @pl.when(step > 0)
        def _():
            total[...] += part

        @pl.when(step == steps - 1)
        def _():
            residual = total[...]
            res_out[...] = residual
            two_out[...] = (
                residual * inverse_rms(residual) * gain[...].astype(jnp.float32)
            ).astype(jnp.bfloat16)


def attend_kernel(steps, idx, q, kv, low, high, bias, wo, source, gain, *rest):
    k_out, v_out, mixed_out, lse_out, res_out, two_out, total = rest[-7:]
    parts = (q, kv, low, high, bias, wo, k_out, v_out, mixed_out, lse_out)
    attend_steps(parts, source, gain, res_out, two_out, total, steps)


class Feed:
    def __init__(self, moment, weights, outs, held, sems):
        self.moment, self.weights, self.outs, self.held, self.sems = (
            moment,
            weights,
            outs,
            held,
            sems,
        )
        size = weights[0].shape[1]
        self.tiles = chunks(size, wide_tile(size))

    def fetch(self, number, part):
        start, size = self.tiles[number]
        place = (slice(None), pl.ds(start, size)) if part < 2 else (pl.ds(start, size),)
        return pltpu.make_async_copy(
            self.weights[part].at[place], self.held[part].at[place], self.sems.at[3 * number + part]
        )

    def start(self):
        for number in range(len(self.tiles)):
            for part in range(3):
                self.fetch(number, part).start()

    def run(self, normed, total, result):
        gate_w, up_w, down_w = self.held[:3]
        stores = []
        for number, (start, size) in enumerate(self.tiles):
            lanes = slice(start, start + size)
            self.fetch(number, 0).wait()
            gate = dot(normed, gate_w[:, lanes])
            self.fetch(number, 1).wait()
            up = dot(normed, up_w[:, lanes])
            half, _, _ = gelu_parts(gate)
            gated = (gate * half * up).astype(jnp.bfloat16)
            values = (gate.astype(jnp.bfloat16), up.astype(jnp.bfloat16), gated)
            for part, value in enumerate(values):
                held = self.held[3 + part]
                held[:, lanes] = value
                copy = pltpu.make_async_copy(
                    held.at[:, pl.ds(start, size)],
                    self.outs[part].at[self.moment, :, pl.ds(start, size)],
                    self.sems.at[3 * len(self.tiles) + 3 * number + part],
                )
                copy.start()
                stores.append(copy)
            self.fetch(number, 2).wait()
            total[...] += dot(gated, down_w[lanes])
        result[...] = total[...].astype(jnp.bfloat16)
        for copy in stores:
            copy.wait()


def feed_kernel(moment, idx, two, residual, wg, wu, wd, *rest):
    outs, result, total, held, sems = rest[-12:-9], rest[-9], rest[-8], rest[-7:-1], rest[-1]
    feed = Feed(moment, (wg, wu, wd), outs, held, sems)
    feed.start()
    total[...] = residual[...]
    feed.run(two[...], total, result)


def attend_feed_kernel(
    moment, steps, idx, q, kv, low, high, bias, wo, source, gain, wg, wu, wd, *rest
):
    k_out, v_out, mixed_out, lse_out, res_out, two_out = rest[-18:-12]
    outs, result, total, held, sems = rest[-12:-9], rest[-9], rest[-8], rest[-7:-1], rest[-1]
    feed = Feed(moment, (wg, wu, wd), outs, held, sems)
    pl.when(pl.program_id(0) == 0)(feed.start)
    parts = (q, kv, low, high, bias, wo, k_out, v_out, mixed_out, lse_out)
    attend_steps(parts, source, gain, res_out, two_out, total, steps)

    @pl.when(pl.program_id(0) == steps)
    def _():
        feed.run(two_out[...], total, result)


def attend_feed_back_kernel(
    moment, steps, extras, idx, q, kv, low, high, bias, wo, source, gain, wg, wu, wd, *rest
):
    arrived, own, packed = rest[:3]
    older = rest[3 : 3 + extras]
    k_out, v_out, mixed_out, lse_out, res_out, two_out = rest[3 + extras : 9 + extras]
    outs, g_out = rest[9 + extras : 12 + extras], rest[12 + extras]
    grad_outs = rest[13 + extras : 15 + extras]
    branch_out, gain_out, result, grad_out, grad_mixed = rest[15 + extras : 20 + extras]
    total, held, sems = rest[20 + extras], rest[21 + extras : 27 + extras], rest[27 + extras]
    gate_back, up_back, res_back, dg_all, du_all, g_arrived, g_own, wo_all, more = rest[28 + extras :]
    feed = Feed(moment, (wg, wu, wd), outs, held, sems)
    taken = idx[1]
    shard = wo_all.shape[1]
    fixed = [
        (arrived, g_arrived),
        (own, g_own),
        (packed.at[:, pl.ds(3 * shard, shard)], wo_all),
    ]
    kept = [
        (older[6].at[taken], gate_back),
        (older[7].at[taken], up_back),
        (older[4].at[taken], res_back),
    ]

    def copy(number):
        here, there = (fixed + kept)[number]
        return pltpu.make_async_copy(here, there, more.at[number])

    @pl.when(pl.program_id(0) == 0)
    def _():
        feed.start()
        for number in range(3):
            copy(number).start()

        @pl.when(taken != moment)
        def _():
            for number in range(3, 6):
                copy(number).start()

    parts = (q, kv, low, high, bias, wo, k_out, v_out, mixed_out, lse_out)
    attend_steps(parts, source, gain, res_out, two_out, total, steps)

    @pl.when(pl.program_id(0) == steps)
    def _():
        feed.run(two_out[...], total, result)

        @pl.when(taken != moment)
        def _():
            for number in range(3, 6):
                copy(number).wait()

        @pl.when(taken == moment)
        def _():
            gate_back[...] = held[3][...]
            up_back[...] = held[4][...]
            res_back[...] = res_out[...]

        for number in range(3):
            copy(number).wait()
        grads = jnp.where(
            idx[0] == 1, g_arrived[...].astype(jnp.float32), g_own[...].astype(jnp.float32)
        ).astype(jnp.bfloat16)
        g_out[...] = grads
        gate_w, up_w, down_w = held[:3]
        stores = []
        for number, (start, size) in enumerate(feed.tiles):
            lanes = slice(start, start + size)
            grad_gate, grad_up = feed_grads(
                nt_dot(grads, down_w[lanes]), gate_back[:, lanes], up_back[:, lanes]
            )
            for part, (value, all_of) in enumerate(((grad_gate, dg_all), (grad_up, du_all))):
                all_of[:, lanes] = value
                store = pltpu.make_async_copy(
                    all_of.at[:, pl.ds(start, size)],
                    grad_outs[part].at[moment - 1, :, pl.ds(start, size)],
                    more.at[6 + 2 * number + part],
                )
                store.start()
                stores.append(store)
            part = nt_dot(grad_gate, gate_w[:, lanes]) + nt_dot(grad_up, up_w[:, lanes])
            if number:
                total[...] += part
            else:
                total[...] = part
        pulled, grad_gain = norm_back(
            total[...], res_back[...], gain[...].astype(jnp.float32)
        )
        gain_out[...] = jnp.broadcast_to(grad_gain, gain_out.shape)
        grad_residual = grads.astype(jnp.float32) + pulled
        grad_out[...] = grad_residual
        branch = grad_residual.astype(jnp.bfloat16)
        branch_out[...] = branch
        grad_mixed[...] = nt_dot(branch, flat(wo_all)).astype(jnp.bfloat16)
        for store in stores:
            store.wait()


def attend(store, slots, moment, scalars, kv, low, high, bias, params, back=None):
    rows, width = kv.shape[1:]
    packed, gain_two = params[1:3]
    weights = params[3:]
    shard = (packed.shape[1] - 16) // 4
    ext = rows + 2 * HALO
    quads = width // WIDE
    last = lambda j: jnp.minimum(j, quads - 1)
    at_start = lambda j: (0, 0)
    at_tile = lambda j: (0, last(j))
    halo_spec = pl.BlockSpec((2, HALO, WIDE), lambda j, s: (0, 0, last(j)))
    fed = feed_parts(rows, width, weights) if weights else ([], [], [], 0)
    kernel = functools.partial(attend_feed_kernel, moment) if weights else attend_kernel
    kernel = functools.partial(kernel, quads)
    back_ins, kept, fresh, scratch = [], [], [], []
    if back is not None:
        back_ins = [*back, packed]
        hidden = weights[0].shape[1]
        kept = [
            ("grad_result", (rows, width), (rows, width), at_start, jnp.bfloat16, moment - 1),
            ("grad_gate", (rows, hidden), None, None, jnp.bfloat16),
            ("grad_up", (rows, hidden), None, None, jnp.bfloat16),
            ("grad_branch", (rows, width), (rows, width), at_start, jnp.bfloat16, moment - 1),
            ("gain_two", (8, width), (8, width), at_start, jnp.float32, moment - 1),
        ]
        fresh = [
            ((rows, width), jnp.float32, whole_spec((rows, width))),
            ((rows, width), jnp.bfloat16, whole_spec((rows, width))),
        ]
        scratch = (
            [pltpu.VMEM((rows, hidden), jnp.bfloat16)] * 2
            + [pltpu.VMEM((rows, width), jnp.float32)]
            + [pltpu.VMEM((rows, hidden), jnp.bfloat16)] * 2
            + [pltpu.VMEM((rows, width), jnp.bfloat16)] * 2
            + [pltpu.VMEM((packed.shape[0], shard, width), jnp.bfloat16)]
            + [pltpu.SemaphoreType.DMA((6 + 2 * len(chunks(hidden, wide_tile(hidden))),))]
        )
        extras = 9 + sum(entry[0] in store for entry in kept)
        kernel = functools.partial(attend_feed_back_kernel, moment, quads, extras)
    return slot_call(
        kernel,
        (quads + (1 if weights else 0),),
        scalars,
        [store["queries"], kv, low, high, bias, packed, store["source"], gain_two]
        + [*weights, *back_ins],
        [
            pl.BlockSpec((None, rows, WIDE), lambda j, s: (moment, 0, last(j))),
            pl.BlockSpec((2, rows, WIDE), lambda j, s: (0, 0, last(j))),
            halo_spec,
            halo_spec,
            pl.BlockSpec((None,) + bias.shape[1:], lambda j, s: (s[2], 0, 0)),
            pl.BlockSpec((WIDE // shard, shard, width), lambda j, s: (last(j), 3, 0)),
            pl.BlockSpec((None, rows, width), lambda j, s: (moment, 0, 0)),
            whole_spec((1, width)),
        ]
        + [pl.BlockSpec(memory_space=pl.ANY)] * (len(weights) + len(back_ins)),
        [
            ("keys", (ext, width), (ext, WIDE), at_tile, jnp.bfloat16),
            ("values", (ext, width), (ext, WIDE), at_tile, jnp.bfloat16),
            ("mixed", (rows, width), (rows, WIDE), at_tile, jnp.bfloat16),
            ("lse", (rows, quads * BLOCK), (rows, BLOCK), at_tile, jnp.float32),
            ("residual", (rows, width), (rows, width), at_start, jnp.float32),
            ("normed_two", (rows, width), (rows, width), at_start, jnp.bfloat16),
        ]
        + fed[0]
        + kept,
        fed[1] + fresh,
        store,
        slots,
        moment,
        [pltpu.VMEM((rows, width), jnp.float32)] + fed[2] + scratch,
        cost_of(
            width * rows * ((BLOCK + 2 * HALO) * 8 + width * 2) + fed[3],
            2 * width * width + 20 * rows * width + fed[3] // rows,
        ),
    )


def feed_parts(rows, width, weights):
    hidden = weights[0].shape[1]
    tiles = len(chunks(hidden, wide_tile(hidden)))
    return (
        [(name, (rows, hidden), None, None, jnp.bfloat16) for name in ("gate", "up", "gated")],
        [((rows, width), jnp.bfloat16, whole_spec((rows, width)))],
        [pltpu.VMEM(weight.shape, jnp.bfloat16) for weight in weights]
        + [pltpu.VMEM((rows, hidden), jnp.bfloat16)] * 3
        + [pltpu.SemaphoreType.DMA((6 * tiles,))],
        6 * rows * width * hidden,
    )


def feed(store, slots, moment, scalars, params):
    weights = params[3:]
    rows, width = store["residual"].shape[1:]
    fed = feed_parts(rows, width, weights)
    return slot_call(
        functools.partial(feed_kernel, moment),
        (1,),
        scalars,
        [store["normed_two"], store["residual"], *weights],
        [pl.BlockSpec((None, rows, width), lambda j, s: (moment, 0, 0))] * 2
        + [pl.BlockSpec(memory_space=pl.ANY)] * 3,
        fed[0],
        fed[1],
        store,
        slots,
        moment,
        [pltpu.VMEM((rows, width), jnp.float32)] + fed[2],
        cost_of(fed[3], fed[3] // rows + 10 * rows * width),
    )


def gelu_parts(gate):
    root = 0.7978845608028654
    bend = jnp.tanh(root * (gate + 0.044715 * gate * gate * gate))
    return 0.5 * (1.0 + bend), bend, root


def feed_grads(grad_gated, gate, up):
    gate, up = gate.astype(jnp.float32), up.astype(jnp.float32)
    half, bend, root = gelu_parts(gate)
    slope = half + 0.5 * gate * (1.0 - bend * bend) * root * (1.0 + 3.0 * 0.044715 * gate * gate)
    return (
        (grad_gated * up * slope).astype(jnp.bfloat16),
        (grad_gated * gate * half).astype(jnp.bfloat16),
    )


def feed_back_kernel(idx, arrived, own, gate, up, residual, gain, wd, wg, wu, wo, *rest):
    g_out, dg_out, du_out, branch_out, gain_out, res_out, mixed_out, total = rest[-8:]
    step = pl.program_id(0)

    @pl.when(step == 0)
    def _():
        g_out[...] = jnp.where(
            idx[0] == 1, arrived[...].astype(jnp.float32), own[...].astype(jnp.float32)
        ).astype(jnp.bfloat16)

    grad_gated = nt_dot(g_out[...], wd[...])
    grad_gate, grad_up = feed_grads(grad_gated, gate[...], up[...])
    dg_out[...] = grad_gate
    du_out[...] = grad_up
    part = nt_dot(grad_gate, wg[...]) + nt_dot(grad_up, wu[...])

    @pl.when(step == 0)
    def _():
        total[...] = part

    @pl.when(step > 0)
    def _():
        total[...] += part

    @pl.when(step == pl.num_programs(0) - 1)
    def _():
        grads, grad_gain = norm_back(total[...], residual[...], gain[...].astype(jnp.float32))
        gain_out[...] = jnp.broadcast_to(grad_gain, gain_out.shape)
        grad_residual = g_out[...].astype(jnp.float32) + grads
        res_out[...] = grad_residual
        branch = grad_residual.astype(jnp.bfloat16)
        branch_out[...] = branch
        mixed_out[...] = nt_dot(branch, flat(wo)).astype(jnp.bfloat16)


def norm_back(grads, values, gain):
    scale = inverse_rms(values)
    pulled = grads * gain
    mean = jnp.mean(pulled * values, axis=-1, keepdims=True)
    return (
        scale * pulled - values * (scale * scale * scale * mean),
        jnp.sum(grads * values * scale, axis=0, keepdims=True),
    )


def feed_back(store, slots, moment, scalars, arrived, own, params):
    packed, gain_two, gate_w, up_w, down_w = params[1:]
    rows, width = arrived.shape
    hidden = gate_w.shape[1]
    tile = wide_tile(hidden)
    at_tile = lambda j: (0, j)
    at_start = lambda j: (0, 0)
    taken_tile = pl.BlockSpec((None, rows, tile), lambda j, s: (s[1], 0, j))
    return slot_call(
        feed_back_kernel,
        (hidden // tile,),
        scalars,
        [arrived, own, store["gate"], store["up"], store["residual"], gain_two]
        + [down_w, gate_w, up_w, packed],
        [whole_spec((rows, width)), whole_spec((rows, width)), taken_tile, taken_tile]
        + [pl.BlockSpec((None, rows, width), lambda j, s: (s[1], 0, 0)), whole_spec((1, width))]
        + [pl.BlockSpec((tile, width), lambda j, s: (j, 0))]
        + [pl.BlockSpec((width, tile), lambda j, s: (0, j))] * 2
        + [
            pl.BlockSpec(
                (packed.shape[0], (packed.shape[1] - 16) // 4, width), lambda j, s: (0, 3, 0)
            )
        ],
        [
            ("grad_result", (rows, width), (rows, width), at_start, jnp.bfloat16),
            ("grad_gate", (rows, hidden), (rows, tile), at_tile, jnp.bfloat16),
            ("grad_up", (rows, hidden), (rows, tile), at_tile, jnp.bfloat16),
            ("grad_branch", (rows, width), (rows, width), at_start, jnp.bfloat16),
            ("gain_two", (8, width), (8, width), at_start, jnp.float32),
        ],
        [
            ((rows, width), jnp.float32, whole_spec((rows, width))),
            ((rows, width), jnp.bfloat16, whole_spec((rows, width))),
        ],
        store,
        slots,
        moment,
        [pltpu.VMEM((rows, width), jnp.float32)],
        cost_of(6 * rows * width * hidden + 2 * rows * width * width, 6 * width * hidden),
    )


def attend_back_kernel(idx, q, keys, values, mixed, lse, grad_mixed, bias, *rest):
    q_out, center, top, bottom, k_total, v_total = rest[-6:]
    rows = q.shape[0]
    scale = jnp.bfloat16(HEAD_DIM**-0.5)
    k_total[...] = jnp.zeros_like(k_total)
    v_total[...] = jnp.zeros_like(v_total)
    tiles = [
        (start, count, slice(pair * 2 * HEAD_DIM, (pair + 1) * 2 * HEAD_DIM), pair)
        for start, count in row_blocks(rows)
        for pair in range(WIDE // (2 * HEAD_DIM))
    ]
    held = {}
    for start, count, lanes, pair in tiles:
        span = count + 2 * HALO
        q_both = stacked_heads(q[pl.ds(start, count), lanes] * scale)
        g_both = stacked_heads(grad_mixed[pl.ds(start, count), lanes])
        scores = nt_dot(q_both, keys[pl.ds(start, span), lanes])
        grad_probs = nt_dot(g_both, values[pl.ds(start, span), lanes])
        held[start, pair] = (q_both, g_both, scores, grad_probs)
    for start, count, lanes, pair in tiles:
        span = count + 2 * HALO
        q_both, g_both, scores, grad_probs = held[start, pair]
        block_bias = bias[pl.ds(start, count), :span]
        both_bias = jnp.concatenate([block_bias, block_bias], 0)
        m_pair = mixed[pl.ds(start, count), lanes].astype(jnp.float32)
        log_sum = jnp.concatenate(
            [lse[pl.ds(start, count), 2 * pair + n : 2 * pair + n + 1] for n in range(2)], 0
        )
        probs = jnp.exp(scores + (both_bias - log_sum))
        mean = jnp.sum(
            g_both.astype(jnp.float32) * jnp.concatenate([m_pair, m_pair], 0),
            axis=-1,
            keepdims=True,
        )
        grad_scores = (probs * (grad_probs - mean)).astype(jnp.bfloat16)
        held[start, pair] = (q_both, g_both, probs.astype(jnp.bfloat16), grad_scores)
    for start, count, lanes, pair in tiles:
        span = count + 2 * HALO
        q_both, g_both, probs, grad_scores = held[start, pair]
        grad_q = dot(grad_scores, keys[pl.ds(start, span), lanes])
        q_out[pl.ds(start, count), lanes] = (
            unstacked_heads(grad_q) * (HEAD_DIM**-0.5)
        ).astype(jnp.bfloat16)
        k_total[pl.ds(start, span), lanes] += tn_dot(grad_scores, q_both)
        v_total[pl.ds(start, span), lanes] += tn_dot(probs, g_both)
    for place, total in ((0, k_total), (1, v_total)):
        top[place] = total[pl.ds(0, HALO)].astype(jnp.bfloat16)
        center[place] = total[pl.ds(HALO, rows)]
        bottom[place] = total[pl.ds(HALO + rows, HALO)].astype(jnp.bfloat16)


def attend_back(store, slots, moment, scalars, grad_mixed, bias):
    rows, width = grad_mixed.shape
    ext = rows + 2 * HALO
    taken = pl.BlockSpec((None, rows, WIDE), lambda j, s: (s[1], 0, j))
    taken_ext = pl.BlockSpec((None, ext, WIDE), lambda j, s: (s[1], 0, j))
    halo_spec = pl.BlockSpec((2, HALO, WIDE), lambda j, s: (0, 0, j))
    work = width * rows * (BLOCK + 2 * HALO) * 2
    return slot_call(
        attend_back_kernel,
        (width // WIDE,),
        scalars,
        [store["queries"], store["keys"], store["values"], store["mixed"], store["lse"]]
        + [grad_mixed, bias],
        [
            taken,
            taken_ext,
            taken_ext,
            taken,
            pl.BlockSpec((None, rows, BLOCK), lambda j, s: (s[1], 0, j)),
            pl.BlockSpec((rows, WIDE), lambda j, s: (0, j)),
            pl.BlockSpec((None,) + bias.shape[1:], lambda j, s: (s[2], 0, 0)),
        ],
        [("grad_queries", (rows, width), (rows, WIDE), lambda j: (0, j), jnp.bfloat16)],
        [
            (
                (2, rows, width),
                jnp.float32,
                pl.BlockSpec((2, rows, WIDE), lambda j, s: (0, 0, j)),
            ),
            ((2, HALO, width), jnp.bfloat16, halo_spec),
            ((2, HALO, width), jnp.bfloat16, halo_spec),
        ],
        store,
        slots,
        moment,
        [pltpu.VMEM((ext, WIDE), jnp.float32)] * 2,
        cost_of(work * 20, 24 * rows * width),
    )


def project_back_kernel(
    idx, grad_q, center, below, above, source, gain, grad_res, wq, wk, wv, *rest
):
    k_out, v_out, gain_out, in_out, total = rest[-5:]
    step = pl.program_id(0)
    rows = source.shape[0]
    for place, out in ((0, k_out), (1, v_out)):
        head = center[place, pl.ds(0, HALO)] + below[place].astype(jnp.float32)
        tail = center[place, pl.ds(rows - HALO, HALO)] + above[place].astype(jnp.float32)
        out[pl.ds(0, HALO)] = head.astype(jnp.bfloat16)
        out[pl.ds(HALO, rows - 2 * HALO)] = center[place, pl.ds(HALO, rows - 2 * HALO)].astype(
            jnp.bfloat16
        )
        out[pl.ds(rows - HALO, HALO)] = tail.astype(jnp.bfloat16)
    part = nt_dot(grad_q[...], flat(wq))
    part += nt_dot(k_out[...], flat(wk)) + nt_dot(v_out[...], flat(wv))

    @pl.when(step == 0)
    def _():
        total[...] = part

    @pl.when(step > 0)
    def _():
        total[...] += part

    @pl.when(step == pl.num_programs(0) - 1)
    def _():
        grads, grad_gain = norm_back(
            total[...], source[...].astype(jnp.float32), gain[...].astype(jnp.float32)
        )
        gain_out[...] = jnp.broadcast_to(grad_gain, gain_out.shape)
        in_out[...] = (grad_res[...] + grads).astype(jnp.bfloat16)


def project_back(store, slots, moment, scalars, center, below, above, grad_res, params):
    rows, width = grad_res.shape
    gain_one, packed = params[:2]
    at_tile = lambda j: (0, j)
    at_start = lambda j: (0, 0)
    halo_spec = pl.BlockSpec((2, HALO, BROAD), lambda j, s: (0, 0, j))
    return slot_call(
        project_back_kernel,
        (width // BROAD,),
        scalars,
        [store["grad_queries"], center, below, above, store["source"], gain_one, grad_res]
        + [packed] * 3,
        [
            pl.BlockSpec((None, rows, BROAD), lambda j, s: (moment, 0, j)),
            pl.BlockSpec((2, rows, BROAD), lambda j, s: (0, 0, j)),
            halo_spec,
            halo_spec,
            pl.BlockSpec((None, rows, width), lambda j, s: (s[1], 0, 0)),
            whole_spec((1, width)),
            whole_spec((rows, width)),
        ]
        + [packed_spec(packed, number, BROAD) for number in range(3)],
        [
            ("grad_keys", (rows, width), (rows, BROAD), at_tile, jnp.bfloat16),
            ("grad_values", (rows, width), (rows, BROAD), at_tile, jnp.bfloat16),
            ("gain_one", (8, width), (8, width), at_start, jnp.float32),
        ],
        [((rows, width), jnp.bfloat16, whole_spec((rows, width)))],
        store,
        slots,
        moment,
        [pltpu.VMEM((rows, width), jnp.float32)],
        cost_of(6 * rows * width * width, 6 * width * width + 20 * rows * width),
    )


def window_bias(lengths_row, shard_no, rows, seq_len):
    ends = jnp.cumsum(lengths_row)
    first = shard_no * rows
    row = jnp.arange(rows, dtype=jnp.int32)
    place = (row // BLOCK * BLOCK)[:, None] - HALO + jnp.arange(BLOCK + 2 * HALO, dtype=jnp.int32)

    def document(position):
        return jnp.sum((position[..., None] >= ends).astype(jnp.int32), axis=-1)

    key = first + place
    allowed = (
        (jnp.abs(row[:, None] - place) <= RADIUS)
        & (key >= 0)
        & (key < seq_len)
        & (document(first + row)[:, None] == document(key))
    )
    return jnp.where(allowed, 0.0, NEVER).astype(jnp.float32)


def after(cells, *others):
    return lax.optimization_barrier((cells,) + others)[0] if others else cells


class Link:
    def __init__(self, axis, pairs, depth):
        self.axis, self.pairs, self.depth, self.sent = axis, pairs, depth, []

    def __call__(self, cells, depth=None):
        depth = self.depth if depth is None else depth
        if depth and len(self.sent) >= depth:
            cells = after(cells, self.sent[-depth])
        self.sent.append(lax.ppermute(cells, self.axis, self.pairs))
        return self.sent[-1]


def links(depth=2):
    span = lax.axis_size("seq")
    high = span // 2
    across = [(h * 2 + c, ((h + 1) % high) * 2 + c) for h in range(high) for c in range(2)]
    pairs = [(i, i ^ 1) for i in range(span)]
    rings = lax.axis_size("wt")
    along = [(i, (i + 1) % rings) for i in range(rings)]
    return Link("seq", across, depth), Link("seq", pairs, 0), Link("wt", along, 0)


def places():
    high = lax.axis_size("seq") // 2
    shard_no = lax.axis_index("seq")
    return high, shard_no // 2, shard_no % 2


class Gather:
    def __init__(self, shard, lines):
        self.across, self.swap = lines[:2]
        self.level = lax.all_gather(shard, "wt", axis=0)

    def cross(self, *others):
        self.row = [after(self.level, *others)]
        for _ in range(1, lax.axis_size("seq") // 2):
            self.row.append(self.across(self.row[-1]))
        return self

    def pieces(self, *others):
        found = {}
        for j, part in enumerate(self.row):
            part = after(part, *others) if j else part
            found[(None, j, 0)] = part
            found[(None, j, 1)] = self.swap(part)
        return found


def ring_gather(shard, lines, between):
    across, swap, along = lines
    found, current = {}, shard
    for k in range(lax.axis_size("wt")):
        current = along(current) if k else current
        if k == lax.axis_size("wt") - 1:
            between()
        cells = current
        for j in range(lax.axis_size("seq") // 2):
            if j:
                cells = across(cells, 1) if k == lax.axis_size("wt") - 1 else across(cells)
            found[(k, j, 0)] = cells
            found[(k, j, 1)] = swap(cells)
    return found


def assemble_kernel(count, plan, seat_ref, *refs):
    parts, wholes, sems = refs[:count], refs[count:-1], refs[-1]
    copies = []
    for number, (source, start, rows, seat, ring, whole, to) in enumerate(plan):
        there = wholes[whole].at[seat_ref[seat]]
        if ring is None:
            here, there = parts[source].at[:, pl.ds(start, rows)], there.at[:, pl.ds(to, rows)]
        else:
            here = parts[source].at[pl.ds(start, rows)]
            there = there.at[seat_ref[ring], pl.ds(to, rows)]
        copies.append(pltpu.make_async_copy(here, there, sems.at[number]))
    for copy in copies:
        copy.start()
    for copy in copies:
        copy.wait()


def assemble(pieces, pack):
    high, h, c = places()
    rings, z = lax.axis_size("wt"), lax.axis_index("wt")
    seats = [
        lax.rem(h - j + high, high) * 2 + (c + p) % 2 for j in range(high) for p in range(2)
    ] + [lax.rem(z - k + rings, rings) for k in range(rings)]
    sources, plan = [], []
    for (k, j, p), part in pieces.items():
        start = 0
        for whole, rows in enumerate(pack):
            ring = None if k is None else 2 * high + k
            plan.append((len(sources), start, rows, j * 2 + p, ring, whole, 0))
            start += rows
        sources.append(part)
    width, kind = sources[0].shape[-1], sources[0].dtype
    shapes = [(2 * high, rings, rows, width) for rows in pack]
    if any(rows % 16 for rows in pack):
        wholes = [jnp.zeros(shape, kind) for shape in shapes]
        for source, start, rows, seat, ring, whole, to in plan:
            part = sources[source]
            part = part[None] if ring is None else part[None, None]
            part = part[:, :, start : start + rows]
            place = (seats[seat], 0 if ring is None else seats[ring], to, 0)
            wholes[whole] = lax.dynamic_update_slice(wholes[whole], part, place)
    else:
        wholes = pl.pallas_call(
            functools.partial(assemble_kernel, len(sources), plan),
            out_shape=[jax.ShapeDtypeStruct(shape, kind) for shape in shapes],
            grid_spec=pltpu.PrefetchScalarGridSpec(
                num_scalar_prefetch=1,
                grid=(),
                in_specs=[pl.BlockSpec(memory_space=pl.ANY)] * len(sources),
                out_specs=[pl.BlockSpec(memory_space=pltpu.VMEM)] * len(shapes),
                scratch_shapes=[pltpu.SemaphoreType.DMA((len(plan),))],
            ),
            compiler_params=pltpu.CompilerParams(vmem_limit_bytes=40 * 2**20),
            cost_estimate=cost_of(0, 2 * sum(source.size * 2 for source in sources)),
        )(jnp.stack(seats).astype(jnp.int32), *sources)
    return [whole.reshape(-1, width) for whole in wholes]


def plus(left, right, kind):
    return (left.astype(jnp.float32) + right.astype(jnp.float32)).astype(kind)


class Scatter:
    def __init__(self, partial, lines, kind=jnp.bfloat16, along_first=False):
        self.across, self.swap = lines[:2]
        self.kind, self.along_first = kind, along_first
        high, h, c = places()
        self.high, self.h = high, h
        cells = partial.reshape(high, 2, -1, partial.shape[-1])
        self.mine = lax.dynamic_index_in_dim(cells, c, 1, False)
        self.received = self.swap(lax.dynamic_index_in_dim(cells, 1 - c, 1, False))
        if along_first:
            rows = self.mine.shape[1]
            rings = lax.axis_size("wt")
            whole = plus(self.mine, self.received, kind)
            whole = whole.reshape(high, rings, rows // rings, -1).swapaxes(0, 1)
            self.summed = whole.reshape(high * rows, -1)
            summed = lax.psum_scatter(self.summed, "wt", scatter_dimension=0, tiled=True)
            self.mine = summed.reshape(high, rows // rings, -1)
            self.level = None
        else:
            self.level = self.block(1)

    def block(self, j):
        place = lax.rem(self.h - j + self.high, self.high)
        mine = lax.dynamic_index_in_dim(self.mine, place, 0, False)
        if self.along_first:
            return mine
        return plus(mine, lax.dynamic_index_in_dim(self.received, place, 0, False), self.kind)

    def cross(self, *others):
        self.level = self.block(1) if self.level is None else self.level
        self.sent = after(self.level, *others)
        self.arrived = self.across(self.sent)
        return self

    def add(self, *others):
        level = self.arrived
        for j in range(2, self.high + 1):
            level = plus(after(level, *others), self.block(j), self.kind)
            if j < self.high:
                level = self.across(level)
        self.level = level
        return self

    def finish(self):
        level = self.level
        if not self.along_first:
            level = lax.psum_scatter(level, "wt", scatter_dimension=0, tiled=True)
        return level.astype(jnp.float32)


def ring_scatter(partial, lines):
    across, swap, along = lines
    high, h, c = places()
    rings, z = lax.axis_size("wt"), lax.axis_index("wt")
    cells = partial.reshape(high, 2, rings, -1, partial.shape[-1])
    mine = lax.dynamic_index_in_dim(cells, c, 1, False)
    received = swap(lax.dynamic_index_in_dim(cells, 1 - c, 1, False))
    size = (1, 1) + cells.shape[3:]

    def block(j, k):
        place = (lax.rem(h - j + high, high), lax.rem(z - k + rings, rings), 0, 0)
        return plus(
            lax.dynamic_slice(mine, place, size)[0, 0],
            lax.dynamic_slice(received, place, size)[0, 0],
            jnp.bfloat16,
        )

    total = None
    for k in range(1, rings + 1):
        level = block(1, k)
        for j in range(2, high + 1):
            level = plus(across(level), block(j, k), jnp.bfloat16)
        if total is None:
            total = level
        else:
            total = plus(along(total), level, jnp.float32 if k == rings else jnp.bfloat16)
    return total.astype(jnp.float32)


def per_device(
    inputs,
    lengths,
    cotangent,
    gain_attn,
    w_query,
    w_key,
    w_value,
    w_out,
    gain_mlp,
    w_gate,
    w_up,
    w_down,
):
    section_no = lax.axis_index("section")
    shard_no = lax.axis_index("seq")
    micro_count, rows_local, model_width = inputs.shape
    seq_len = rows_local * lax.axis_size("seq")
    is_first = (section_no == 0).astype(jnp.int32)
    slots = micro_count + 1
    bias = jnp.stack(
        [
            window_bias(lengths[number], shard_no, rows_local, seq_len)
            for number in range(micro_count)
        ]
    )

    def choose(of_first, of_second):
        return is_first * of_first + (1 - is_first) * of_second

    rows = w_query.shape[1]
    gains = jnp.pad(
        jnp.concatenate([gain_attn, gain_mlp], 1), ((0, 15), (0, model_width - 2 * rows))
    )
    lines = links()
    narrow = jnp.concatenate([w_query[0], w_key[0], w_value[0], w_out[0], gains], 0)
    gate_gather = Gather(w_gate[0], lines)
    up_gather = Gather(w_up[0], lines)
    down_gather = Gather(w_down[0], lines)
    pieces = ring_gather(narrow, lines, gate_gather.cross)
    (packed,) = assemble(pieces, [narrow.shape[0]])
    packed = packed.reshape(-1, narrow.shape[0], model_width)
    gain_rows = packed[:, 4 * rows]
    gain_one = gain_rows[:, :rows].reshape(1, -1)
    gain_two = gain_rows[:, rows : 2 * rows].reshape(1, -1)
    params = (gain_one, packed, gain_two)

    store, results, grad_sources, sums = {}, [], [], {}
    arrived = [jnp.zeros((rows_local, model_width), jnp.bfloat16)]
    arrived_grad = [arrived[0]]

    def taken_slot(moment):
        return choose(max(moment - 1, 0), min(moment + 1, micro_count))

    def forward(moment, params):
        early, late = min(moment, micro_count - 1), max(moment - 1, 0)
        scalars = jnp.stack([is_first, taken_slot(moment - 1), choose(early, late)])
        started = None
        layer_in = after(arrived[moment], *grad_sources[-1:])
        kv, tail, head = project(store, slots, moment, scalars, inputs[early], layer_in, params)
        low = shifted(tail, "seq", 1)
        high = shifted(head, "seq", -1)
        if moment == 0:
            up_gather.cross()
            down_gather.cross(low, high)
            kv = after(kv, up_gather.row[-1])
            attend(store, slots, moment, scalars, kv, low, high, bias, params)
            two = store["normed_two"]
            (gate_w,) = assemble(gate_gather.pieces(kv), [rows])
            (up_w,) = assemble(up_gather.pieces(kv), [rows])
            (down_w,) = assemble(down_gather.pieces(two, gate_w, up_w), [w_down.shape[1]])
            params = params + (gate_w, up_w, down_w)
            (result,) = feed(store, slots, moment, scalars, params)
        else:
            back = (arrived_grad[moment - 1], cotangent[min(moment - 1, micro_count - 1)])
            result, *started = attend(
                store, slots, moment, scalars, kv, low, high, bias, params, back
            )
        results.append(result)
        if moment < micro_count:
            arrived.append(shifted(result, "section", 1))
        return params, started

    def both(name, start):
        chosen = lax.dynamic_slice_in_dim(store[name], start, micro_count, 0)
        return chosen.reshape(-1, chosen.shape[-1])

    def product(left, right, then=()):
        left = after(both(left, 1 - is_first), *then)
        return jnp.dot(
            left.T, both(right, is_first), preferred_element_type=jnp.float32
        ).astype(jnp.bfloat16)

    def backward(moment, started=None):
        early, late = min(moment, micro_count - 1), max(moment - 1, 0)
        scalars = jnp.stack(
            [is_first, taken_slot(moment), choose(late, early)]
        )
        grad_res, grad_mixed = started or feed_back(
            store, slots, moment, scalars, arrived_grad[moment], cotangent[early], params
        )
        if moment == micro_count:
            lines = links()
            gate_part = product("normed_two", "grad_gate")
            gate_sum = Scatter(gate_part, lines)
            out_part = product("mixed", "grad_branch", then=(gate_part,))
            out_sum = Scatter(out_part, lines, along_first=True)
            up_part = product("normed_two", "grad_up", then=(out_part,))
            up_sum = Scatter(up_part, lines)
            gate_sum.cross(up_part)
            down_part = product("gated", "grad_result", then=(gate_sum.sent, out_sum.summed))
            down_sum = Scatter(down_part, lines)
            grad_mixed = after(grad_mixed, down_part, up_sum.level)
        center, top, bottom = attend_back(store, slots, moment, scalars, grad_mixed, bias)
        above = shifted(top, "seq", -1)
        below = shifted(bottom, "seq", 1)
        if moment == micro_count:
            up_sum.cross(above, below)
            gate_sum.add(center)
            center = after(center, gate_sum.level, down_sum.level)
            down_sum.cross(above, below)
            sums.update(lines=lines, gate=gate_sum, up=up_sum, down=down_sum, out=out_sum)
        (grad_source,) = project_back(
            store, slots, moment, scalars, center, below, above, grad_res, params
        )
        grad_sources.append(grad_source)
        if moment < micro_count:
            arrived_grad.append(shifted(grad_source, "section", -1))

    params, _ = forward(0, params)
    for moment in range(1, slots):
        _, started = forward(moment, params)
        backward(moment - 1, started)
    backward(micro_count)

    activations = jnp.stack(
        [
            jnp.where(is_first == 1, results[number], results[number + 1])
            for number in range(micro_count)
        ]
    )[None]
    input_grads = jnp.stack(
        [
            jnp.where(is_first == 1, grad_sources[number + 1], grad_sources[number])
            for number in range(micro_count)
        ]
    )[None]
    lines, gate_sum, up_sum, down_sum, out_sum = (
        sums[name] for name in ("lines", "gate", "up", "down", "out")
    )
    gain_rows = jnp.concatenate(
        [
            jnp.sum(lax.dynamic_slice_in_dim(store[name], is_first, micro_count, 0), 0)
            for name in ("gain_one", "gain_two")
        ]
    ).astype(jnp.bfloat16)
    picked = jnp.arange(2 * 8)[:, None] == jnp.arange(BLOCK)[None] * 8
    right = jnp.concatenate(
        [both(name, is_first) for name in ("grad_queries", "grad_keys", "grad_values")], 1
    )
    right = jnp.concatenate(
        [
            jnp.pad(right, ((0, 0), (0, BLOCK))),
            jnp.pad(picked.astype(jnp.bfloat16), ((0, 0), (right.shape[1], 0))),
        ]
    )
    left = jnp.concatenate([both("normed", 1 - is_first), gain_rows])
    qkv_part = jnp.dot(left.T, right, preferred_element_type=jnp.float32).astype(jnp.bfloat16)
    up_sum.add(qkv_part)
    grad_up_w = up_sum.finish()
    down_sum.add(up_sum.level)
    qkv_all = ring_scatter(qkv_part, lines)
    grad_out_w = out_sum.cross().add().finish()
    grad_gate_w, grad_down_w = gate_sum.finish(), down_sum.finish()
    grad_query_w, grad_key_w, grad_value_w, gain_sum = (
        qkv_all[:, number * model_width : (number + 1) * model_width] for number in range(4)
    )
    return (
        activations,
        input_grads,
        gain_sum[:, 0][None],
        grad_query_w[None],
        grad_key_w[None],
        grad_value_w[None],
        grad_out_w[None],
        gain_sum[:, 1][None],
        grad_gate_w[None],
        grad_up_w[None],
        grad_down_w[None],
    )


def solution(mesh):
    placed = (
        P("wt", "seq", None),
        P("wt", None),
        P("wt", "seq", None),
        P("section", ("seq", "wt")),
        P("section", ("seq", "wt"), None),
        P("section", ("seq", "wt"), None),
        P("section", ("seq", "wt"), None),
        P("section", ("seq", "wt"), None),
        P("section", ("seq", "wt")),
        P("section", ("seq", "wt"), None),
        P("section", ("seq", "wt"), None),
        P("section", ("seq", "wt"), None),
    )
    return jax.shard_map(
        per_device,
        mesh=mesh,
        in_specs=placed,
        out_specs=(
            P("section", "wt", "seq", None),
            P("section", "wt", "seq", None),
            P("section", ("seq", "wt")),
            P("section", ("seq", "wt"), None),
            P("section", ("seq", "wt"), None),
            P("section", ("seq", "wt"), None),
            P("section", ("seq", "wt"), None),
            P("section", ("seq", "wt")),
            P("section", ("seq", "wt"), None),
            P("section", ("seq", "wt"), None),
            P("section", ("seq", "wt"), None),
        ),
        check_vma=False,
    )
```
